32 devices in a mesh: tm: 4 (over y, core), space: 8 (over z, x).
Axes of the slice: x: 2, y: 2, z: 4, core: 2. Of those that a mesh axis runs over, the one named last changes fastest.
Arguments:
- snapshots: float32 [512, 128, 512], P('space', None, 'tm'), may hold values from -6 to 6
- land_mask: int32 [512, 128], P('space'), may hold values 0 or 1
- taps_rows: float32 [6], replicated, may hold values from -2.5 to 2.5
- taps_cols: float32 [6], replicated, may hold values from -2.5 to 2.5
- probes: float32 [256, 64, 128], P('space'), may hold values from -6 to 6
Outputs:
- basis: float32 [256, 64, 128], P('space', None, 'tm')
- coefficients: float32 [128, 128], P('tm')
The draws below stay inside these ranges and needn't reach their ends.
All inputs are finite; a program needn't handle non-finite values. No bound on the sum of `land_mask` on one device may be relied on, other than what follows from the above.
Results may differ from the reference program's by a relative error of at most 0.00028.
Values sent between devices are 32-bit elements; how exact they have to be, the bound alone decides.
No kernel may reach another device: no remote copies, remote signals or barrier semaphores. Data moves between devices by JAX's collectives and lax.ppermute only.
A program may use at most 64 MiB of HBM per device.

```python
import jax
import jax.numpy as jnp
from jax import lax

CY = 128
COLS = 128
NPROBE = 128
SIGN_STEPS = 8
NX = 512
SNAP = 512
N_TM = 4


def with_ends(values, stream_key, smallest, top_value):
    index_at = [jax.random.randint(jax.random.fold_in(stream_key, axis), (), 0, length) for axis, length in enumerate(values.shape)]
    main_axis = values.shape.index(max(values.shape))
    next_to = index_at[:main_axis] + [(index_at[main_axis] + 1) % values.shape[main_axis]] + index_at[main_axis + 1:]
    return values.at[tuple(index_at)].set(smallest).at[tuple(next_to)].set(top_value)


def level_of(rng, extent, split, smallest, top_value):
    gain = 1.0
    for dim, shards_of in split:
        steps = jax.random.uniform(jax.random.fold_in(jax.random.fold_in(rng, 6), dim), (shards_of,), jnp.float32, smallest / len(split), top_value / len(split))
        gain = gain * jnp.repeat(jnp.exp(steps), extent[dim] // shards_of).reshape((-1,) + (1,) * (len(extent) - 1 - dim))
    return gain


def noise(stream_key, extent, spread, limit, split=(), held_as=jnp.bfloat16):
    drawn = spread * jax.random.normal(stream_key, extent, jnp.float32)
    if split:
        drawn = drawn * level_of(stream_key, extent, split, -0.22, 0.18)
    return jnp.clip(drawn, -limit, limit).astype(held_as)


def setup_inputs(seed: int = 0) -> dict:
    splits = jax.random.split(jax.random.key(seed), 6)
    return {
        "snapshots": noise(splits[0], (NX, CY, SNAP), 1.0, 6.0, ((0, 8), (2, 4)), jnp.float32),
        "land_mask": with_ends((jax.random.randint(splits[1], (NX, CY), 0, 4) < 3).astype(jnp.int32), jax.random.fold_in(splits[1], 1), 0, 1),
        "taps_rows": noise(splits[2], (6,), 0.5, 2.5, (), jnp.float32),
        "taps_cols": noise(splits[3], (6,), 0.5, 2.5, (), jnp.float32),
        "probes": noise(splits[4], (NX // 2, CY // 2, NPROBE), 1.0, 6.0, ((0, 8),), jnp.float32),
    }


exact_dot = lax.Precision.HIGHEST

def filter_block(block, land_mask, taps_rows, taps_cols):
    ocean_field = block * land_mask.astype(jnp.float32)[:, :, None]
    padded = jnp.pad(ocean_field, ((0, 0), (2, 4), (0, 0)))
    narrowed = taps_cols[0] * padded[:, 0:CY:2, :]
    for tap_index in range(1, 6):
        narrowed = narrowed + taps_cols[tap_index] * padded[:, tap_index:tap_index + CY:2, :]
    padded_rows = jnp.pad(narrowed, ((2, 4), (0, 0), (0, 0)))
    filtered = taps_rows[0] * padded_rows[0:NX:2]
    for tap_index in range(1, 6):
        filtered = filtered + taps_rows[tap_index] * padded_rows[tap_index:tap_index + NX:2]
    return filtered.reshape(NX // 2 * (CY // 2), COLS)

def merge_level(paired):
    gram_total = jnp.einsum('gra,grb->gab', paired, paired, precision=exact_dot)
    order_size = gram_total.shape[-1]
    identity = jnp.eye(order_size, dtype=jnp.float32)
    mean_eig = lax.optimization_barrier(jnp.sum(gram_total * identity, axis=(1, 2))) / order_size
    shifted = gram_total - mean_eig[:, None, None] * identity
    norm_scale = jnp.sqrt(lax.optimization_barrier(jnp.sum(shifted * shifted, axis=(1, 2))) + 1e-06)
    sign_iter = shifted / norm_scale[:, None, None]
    for sweep_index in range(SIGN_STEPS):
        square = jnp.einsum('gab,gbc->gac', sign_iter, sign_iter, precision=exact_dot)
        sign_iter = 1.5 * sign_iter - 0.5 * jnp.einsum('gab,gbc->gac', sign_iter, square, precision=exact_dot)
    projector = 0.5 * (identity + sign_iter)
    half_order = order_size // 2
    combine = projector[:, :, :half_order] + projector[:, :, half_order:]
    return jnp.einsum('gra,gab->grb', paired, combine, precision=exact_dot)

def reference(snapshots, land_mask, taps_rows, taps_cols, probes):
    stacked = snapshots.reshape(NX, CY, N_TM, COLS).transpose(2, 0, 1, 3)

    def filter_one(block):
        return filter_block(block, land_mask, taps_rows, taps_cols)
    blocks = lax.map(filter_one, stacked)
    for level_index in range(N_TM.bit_length() - 1):
        blocks = merge_level(jnp.concatenate([blocks[0::2], blocks[1::2]], axis=2))
    merged = blocks[0]
    flat_probes = probes.reshape(NX // 2 * (CY // 2), NPROBE)
    coefficients = jnp.einsum('rs,rp->sp', merged, flat_probes, precision=exact_dot)
    return (merged.reshape(NX // 2, CY // 2, COLS), coefficients)
```

```python
import functools

import jax
import jax.numpy as jnp
from jax import lax
from jax.experimental import pallas as pl
from jax.experimental.pallas import tpu as pltpu
from jax.sharding import PartitionSpec as P

SIGN_STEPS = 8
TAPS = 6
ROW_BLOCK = 16
exact = lax.Precision.HIGHEST
F32 = jnp.float32
VMEM_LIMIT = 48 * 1024 * 1024


def params():
    return pltpu.CompilerParams(vmem_limit_bytes=VMEM_LIMIT)


def whole():
    return pl.BlockSpec(memory_space=pltpu.VMEM)


def scalars():
    return pl.BlockSpec(memory_space=pltpu.SMEM)


def swap(x, axis, mask):
    count = lax.axis_size(axis)
    return lax.ppermute(x, axis, [(i, i ^ mask) for i in range(count)])


def shift_rows(x, by):
    edge = jnp.zeros((1, x.shape[1]), x.dtype)
    if by > 0:
        return jnp.concatenate([edge, x[:-1]], axis=0)
    return jnp.concatenate([x[1:], edge], axis=0)


def narrow_row(snap_ref, x, mask_even, mask_odd, taps):
    half = snap_ref.shape[1] // 2
    even = snap_ref[x, pl.ds(0, half, stride=2), :] * mask_even
    odd = snap_ref[x, pl.ds(1, half, stride=2), :] * mask_odd
    before = taps[0] * even + taps[1] * odd
    here = taps[2] * even + taps[3] * odd
    after = taps[4] * even + taps[5] * odd
    return shift_rows(before, 1) + here + shift_rows(after, -1)


def masks_of(mask_ref, mask_t):
    half = mask_ref.shape[1] // 2
    mask_t[...] = mask_ref[...].astype(F32).T
    return mask_t[pl.ds(0, half, stride=2), :], mask_t[pl.ds(1, half, stride=2), :]


def edge_kernel(taps_ref, first_ref, last_ref, mask_ref, top_ref, end_ref, mask_t):
    taps = [taps_ref[k] for k in range(TAPS)]
    even, odd = masks_of(mask_ref, mask_t)
    rows = mask_ref.shape[0]
    for x in range(2):
        top_ref[x] = narrow_row(first_ref, x, even[:, x:x + 1], odd[:, x:x + 1], taps)
        y = rows - 2 + x
        end_ref[x] = narrow_row(last_ref, x, even[:, y:y + 1], odd[:, y:y + 1], taps)


def filter_kernel(parts, me_ref, rtaps_ref, ctaps_ref, snap_ref, mask_ref, above_ref, below_ref, *rest):
    outs, (mask_t, narrowed, filtered) = rest[:parts], rest[parts:]
    step = pl.program_id(0)
    taps = [ctaps_ref[k] for k in range(TAPS)]
    even, odd = masks_of(mask_ref, mask_t)
    block = snap_ref.shape[0]
    for x in range(block):
        narrowed[2 + step * block + x] = narrow_row(snap_ref, x, even[:, x:x + 1], odd[:, x:x + 1], taps)

    @pl.when(step == pl.num_programs(0) - 1)
    def _():
        size = narrowed.shape[0]
        narrowed[0:2] = above_ref[...]
        narrowed[size - 2:size] = below_ref[...]
        rtaps = [rtaps_ref[k] for k in range(TAPS)]
        cells = narrowed.shape[1]
        for i in range((size - 4) // 2):
            total = rtaps[0] * narrowed[2 * i]
            for k in range(1, TAPS):
                total = total + rtaps[k] * narrowed[2 * i + k]
            filtered[i * cells:(i + 1) * cells, :] = total
        me = me_ref[0]
        piece = filtered.shape[0] // parts
        for k in range(parts):
            outs[k][...] = filtered[pl.ds(pl.multiple_of((me ^ k) * piece, 8), piece), :]


def probe_kernel(parts, me_ref, *refs):
    pieces, probes_ref, out_ref = refs[:parts], refs[parts], refs[parts + 1]
    me = me_ref[0]
    size = pieces[0].shape[0]
    total = None
    for k in range(parts):
        there = probes_ref[pl.ds(pl.multiple_of((me ^ k) * size, 8), size), :]
        term = lax.dot_general(pieces[k][...], there, (((0,), (0,)), ((), ())), precision=exact, preferred_element_type=F32)
        total = term if total is None else total + term
    out_ref[...] = total


def block_order(parts):
    return [(a, b) for a in range(parts) for b in range(a, parts)]


def send_groups(parts):
    groups, bit = [], 1
    while bit < parts:
        groups.append([k for k in range(parts) if k & (2 * bit - 1) == bit])
        bit *= 2
    return groups + [[0]]


def gram_kernel(parts, me_ref, *refs):
    pieces = refs[:parts]
    groups = send_groups(parts)
    outs = refs[parts:parts + len(groups)]
    wide, flat = refs[parts + len(groups):]
    me = me_ref[0]
    cols = pieces[0].shape[1]
    for k in range(parts):
        wide[:, pl.ds(pl.multiple_of((me ^ k) * cols, cols), cols)] = pieces[k][...]
    where = {ab: j for j, ab in enumerate(block_order(parts))}
    for a in range(0, parts, 2):
        left = wide[:, a * cols:(a + 2) * cols]
        for b in range(a, parts, 2):
            right = wide[:, b * cols:(b + 2) * cols]
            prod = lax.dot_general(left, right, (((0,), (0,)), ((), ())), precision=exact, preferred_element_type=F32)
            for i in range(2):
                for j in range(2):
                    if (a + i, b + j) in where:
                        at = where[a + i, b + j] * cols
                        flat[at:at + cols, :] = prod[i * cols:(i + 1) * cols, j * cols:(j + 1) * cols]
    size = flat.shape[0] // parts
    for group, out in zip(groups, outs):
        for at, k in enumerate(group):
            out[at] = flat[pl.ds(pl.multiple_of((me ^ k) * size, 8), size), :]


def split(x):
    high = x.astype(jnp.bfloat16)
    return high, (x - high.astype(F32)).astype(jnp.bfloat16)


def dot(a, b, dims):
    return lax.dot_general(a, b, (dims, ((), ())), preferred_element_type=F32)


def dot_parts(a, b, dims=((1,), (0,))):
    (ah, al), (bh, bl) = a, b
    return dot(ah, bh, dims) + (dot(ah, bl, dims) + dot(al, bh, dims))


def exact_dot(a, b, dims=((1,), (0,))):
    return lax.dot_general(a, b, (dims, ((), ())), precision=exact, preferred_element_type=F32)


def combine_of(grams):
    order = grams[0].shape[0]
    diagonal = lax.broadcasted_iota(jnp.int32, (order, order), 0) == lax.broadcasted_iota(jnp.int32, (order, order), 1)
    signs = []
    for gram in grams:
        mean = jnp.sum(jnp.where(diagonal, gram, 0.0)) / order
        shifted = jnp.where(diagonal, gram - mean, gram)
        signs.append(shifted / jnp.sqrt(jnp.sum(shifted * shifted, keepdims=True) + 1e-6))
    for _ in range(SIGN_STEPS):
        halves = [split(y) for y in signs]
        squares = [split(dot_parts(y, y)) for y in halves]
        cubes = [dot_parts(y, s) for y, s in zip(halves, squares)]
        signs = [1.5 * y - 0.5 * c for y, c in zip(signs, cubes)]
    half = order // 2
    combines = []
    for y in signs:
        projector = 0.5 * (jnp.where(diagonal, 1.0, 0.0) + y)
        combines.append(projector[:, :half] + projector[:, half:])
    return combines


def merge_kernel(parts, me_ref, *refs):
    gram_in, factors = refs[:parts], refs[parts:2 * parts]
    probe_ref = refs[2 * parts]
    outs = refs[2 * parts + 1:3 * parts + 1]
    flat, weight, turned = refs[3 * parts + 1:]
    me = me_ref[0]
    size, cols = gram_in[0].shape
    for k in range(parts):
        flat[pl.ds(pl.multiple_of((me ^ k) * size, 8), size), :] = gram_in[k][...]
    blocks = {ab: flat[j * cols:(j + 1) * cols, :] for j, ab in enumerate(block_order(parts))}
    weights, count = None, parts
    while count > 1:
        grams = []
        for p in range(0, count, 2):
            low = jnp.concatenate([blocks[p, p], blocks[p, p + 1]], axis=1)
            high = jnp.concatenate([blocks[p, p + 1].T, blocks[p + 1, p + 1]], axis=1)
            grams.append(jnp.concatenate([low, high], axis=0))
        combines = combine_of(grams)
        if weights is None:
            weights = combines
        else:
            per = len(weights) // len(combines)
            weights = [
                exact_dot(w, combines[i // per][(i % per) * cols:(i % per + 1) * cols, :])
                for i, w in enumerate(weights)
            ]
            weights = [jnp.concatenate(weights[i:i + per], axis=0) for i in range(0, len(weights), per)]
        merged = {}
        if count > 2:
            for p in range(count // 2):
                for q in range(p, count // 2):
                    if p == q:
                        cross = grams[p]
                    else:
                        cross = jnp.concatenate([
                            jnp.concatenate([blocks[2 * p + i, 2 * q], blocks[2 * p + i, 2 * q + 1]], axis=1)
                            for i in range(2)
                        ], axis=0)
                    right = exact_dot(cross, combines[q])
                    merged[p, q] = exact_dot(combines[p], right, ((0,), (0,)))
        blocks, count = merged, count // 2
    weight[...] = weights[0]
    total = None
    for k in range(parts):
        there = weight[pl.ds(pl.multiple_of((me ^ k) * cols, cols), cols), :]
        term = dot_parts(split(factors[k][...]), split(there))
        total = term if total is None else total + term
    rows = total.shape[0]
    turned[:, :rows] = total.T
    mine = weight[pl.ds(pl.multiple_of(me * cols, cols), cols), :]
    turned[:, rows:] = exact_dot(mine, probe_ref[...], ((0,), (0,)))
    width = cols // parts
    for k in range(parts):
        outs[k][...] = turned[pl.ds(pl.multiple_of((me ^ k) * width, 8), width), :]


def final_kernel(parts, me_ref, *refs):
    pieces, (basis_ref, coef_ref) = refs[:parts], refs[parts:]
    me = me_ref[0]
    rows = basis_ref.shape[0] // parts
    total = None
    for k in range(parts):
        basis_ref[pl.ds(pl.multiple_of((me ^ k) * rows, 8), rows), :] = pieces[k][:, :rows].T
        tail = pieces[k][:, rows:]
        total = tail if total is None else total + tail
    coef_ref[...] = total


def shape(*dims):
    return jax.ShapeDtypeStruct(dims, F32)


def local(snapshots, land_mask, taps_rows, taps_cols, probes):
    rows, grid_cols, cols = snapshots.shape
    half_rows, half_cols = rows // 2, grid_cols // 2
    parts, patches = lax.axis_size("tm"), lax.axis_size("space")
    cells = half_rows * half_cols
    piece = cells // parts
    me = lax.axis_index("tm").astype(jnp.int32).reshape(1)

    top, end = pl.pallas_call(
        edge_kernel,
        out_shape=(shape(2, half_cols, cols), shape(2, half_cols, cols)),
        grid=(1,),
        in_specs=[
            scalars(),
            pl.BlockSpec((2, grid_cols, cols), lambda i: (0, 0, 0)),
            pl.BlockSpec((2, grid_cols, cols), lambda i: (rows // 2 - 1, 0, 0)),
            pl.BlockSpec((rows, grid_cols), lambda i: (0, 0)),
        ],
        out_specs=(
            pl.BlockSpec((2, half_cols, cols), lambda i: (0, 0, 0)),
            pl.BlockSpec((2, half_cols, cols), lambda i: (0, 0, 0)),
        ),
        scratch_shapes=[pltpu.VMEM((grid_cols, rows), F32)],
        compiler_params=params(),
        name="edge",
    )(taps_cols, snapshots, snapshots, land_mask)
    up = [(i, i + 1) for i in range(patches - 1)]
    above = lax.ppermute(end, "space", up)
    below = lax.ppermute(top, "space", [(j, i) for i, j in up])

    same = pl.BlockSpec((2, half_cols, cols), lambda i: (0, 0, 0))
    pieces = pl.pallas_call(
        functools.partial(filter_kernel, parts),
        out_shape=[shape(piece, cols)] * parts,
        grid=(rows // ROW_BLOCK,),
        in_specs=[
            scalars(), scalars(), scalars(),
            pl.BlockSpec((ROW_BLOCK, grid_cols, cols), lambda i: (i, 0, 0)),
            pl.BlockSpec((ROW_BLOCK, grid_cols), lambda i: (i, 0)),
            same, same,
        ],
        out_specs=[pl.BlockSpec((piece, cols), lambda i: (0, 0))] * parts,
        scratch_shapes=[
            pltpu.VMEM((grid_cols, ROW_BLOCK), F32),
            pltpu.VMEM((rows + 4, half_cols, cols), F32),
            pltpu.VMEM((cells, cols), F32),
        ],
        compiler_params=params(),
        name="filter",
    )(me, taps_rows, taps_cols, snapshots, land_mask, above, below)

    factors = [pieces[0]] + [swap(pieces[k], "tm", k) for k in range(1, parts)]

    probe_sum = pl.pallas_call(
        functools.partial(probe_kernel, parts),
        out_shape=shape(cols, cols),
        in_specs=[scalars()] + [whole()] * (parts + 1),
        out_specs=whole(),
        compiler_params=params(),
        cost_estimate=pl.CostEstimate(flops=12 * cells * cols * cols, bytes_accessed=8 * cells * cols, transcendentals=0),
        name="probe",
    )(me, *pieces, probes.reshape(cells, cols))

    def over_space(x):
        bit = 1
        while bit < patches:
            x = x + swap(x, "space", bit)
            bit *= 2
        return x

    probe_sum = over_space(probe_sum)

    blocks = parts * (parts + 1) // 2
    size = blocks * cols // parts
    groups = send_groups(parts)
    sends = pl.pallas_call(
        functools.partial(gram_kernel, parts),
        out_shape=[shape(len(g), size, cols) for g in groups],
        in_specs=[scalars()] + [whole()] * parts,
        out_specs=[whole()] * len(groups),
        scratch_shapes=[pltpu.VMEM((piece, parts * cols), F32), pltpu.VMEM((blocks * cols, cols), F32)],
        compiler_params=params(),
        name="gram",
    )(me, *factors)
    sends = list(sends)
    for step in range(len(groups) - 1):
        got = swap(sends[step], "tm", 1 << step)
        order = [k ^ (1 << step) for k in groups[step]]
        for later in range(step + 1, len(groups)):
            pick = [order.index(k) for k in groups[later]]
            sends[later] = sends[later] + jnp.stack([got[i] for i in pick])
    gram_piece = over_space(sends[-1][0])

    have, bit = {0: gram_piece}, parts // 2
    while bit:
        have.update({k ^ bit: swap(x, "tm", bit) for k, x in list(have.items())})
        bit //= 2

    width = cols // parts
    sent = pl.pallas_call(
        functools.partial(merge_kernel, parts),
        out_shape=[shape(width, piece + cols)] * parts,
        in_specs=[scalars()] + [whole()] * (2 * parts + 1),
        out_specs=[whole()] * parts,
        scratch_shapes=[
            pltpu.VMEM((blocks * cols, cols), F32),
            pltpu.VMEM((parts * cols, cols), F32),
            pltpu.VMEM((cols, piece + cols), F32),
        ],
        compiler_params=params(),
        name="merge",
    )(me, *[have[k] for k in range(parts)], *factors, probe_sum)
    last = [sent[0]] + [swap(sent[k], "tm", k) for k in range(1, parts)]

    basis, coefficients = pl.pallas_call(
        functools.partial(final_kernel, parts),
        out_shape=(shape(cells, width), shape(width, cols)),
        in_specs=[scalars()] + [whole()] * parts,
        out_specs=(whole(), whole()),
        compiler_params=params(),
        name="final",
    )(me, *last)
    return basis.reshape(half_rows, half_cols, width), coefficients


def solution(mesh):
    placed = (P("space", None, "tm"), P("space", None), P(), P(), P("space", None, None))
    return jax.shard_map(
        local,
        mesh=mesh,
        in_specs=placed,
        out_specs=(P("space", None, "tm"), P("tm", None)),
        check_vma=False,
    )
```

```python
import functools

import jax
import jax.numpy as jnp
from jax import lax
from jax.experimental import pallas as pl
from jax.experimental.pallas import tpu as pltpu
from jax.sharding import PartitionSpec as P

SIGN_STEPS = 8
TAPS = 6
CHUNK = 8
exact = lax.Precision.HIGHEST
F32 = jnp.float32
VMEM_LIMIT = 48 * 1024 * 1024


def params():
    return pltpu.CompilerParams(vmem_limit_bytes=VMEM_LIMIT)


def whole():
    return pl.BlockSpec(memory_space=pltpu.VMEM)


def scalars():
    return pl.BlockSpec(memory_space=pltpu.SMEM)


def swap(x, axis, mask):
    count = lax.axis_size(axis)
    return lax.ppermute(x, axis, [(i, i ^ mask) for i in range(count)])


def swap_both(x, mask):
    parts, patches = lax.axis_size("tm"), lax.axis_size("space")
    route = []
    for t in range(parts):
        for s in range(patches):
            there = (t ^ (mask % parts)) * patches + (s ^ (mask // parts))
            route.append((t * patches + s, there))
    return lax.ppermute(x, ("tm", "space"), route)


def shift_rows(x, by):
    edge = jnp.zeros((1, x.shape[1]), x.dtype)
    if by > 0:
        return jnp.concatenate([edge, x[:-1]], axis=0)
    return jnp.concatenate([x[1:], edge], axis=0)


def narrow_row(snap_ref, x, mask_even, mask_odd, taps):
    half = snap_ref.shape[1] // 2
    even = snap_ref[x, pl.ds(0, half, stride=2), :] * mask_even
    odd = snap_ref[x, pl.ds(1, half, stride=2), :] * mask_odd
    before = taps[0] * even + taps[1] * odd
    here = taps[2] * even + taps[3] * odd
    after = taps[4] * even + taps[5] * odd
    return shift_rows(before, 1) + here + shift_rows(after, -1)


def filter_kernel(parts, me_ref, rtaps_ref, ctaps_ref, snap_hbm, mask_ref, *rest):
    bigs, (small_ref, up_ref, down_ref) = rest[:parts], rest[parts:parts + 3]
    snaps, sems, mask_t, narrowed, filtered = rest[parts + 3:]
    rows, cells = snaps.shape[0], narrowed.shape[1]
    chunks = rows // CHUNK

    def fetch(c):
        at = pl.ds(c * CHUNK, CHUNK)
        return pltpu.make_async_copy(snap_hbm.at[at], snaps.at[at], sems.at[c])

    for c in range(chunks):
        fetch(c).start()
    ctaps = [ctaps_ref[k] for k in range(TAPS)]
    rtaps = [rtaps_ref[k] for k in range(TAPS)]
    edge = jnp.zeros((2,) + narrowed.shape[1:], F32)
    narrowed[0:2] = edge
    narrowed[rows + 2:rows + 4] = edge

    def narrow(c, carry):
        fetch(c).wait()
        base = pl.multiple_of(c * CHUNK, CHUNK)
        mask_t[...] = mask_ref[pl.ds(base, CHUNK), :].astype(F32).T
        even = mask_t[pl.ds(0, cells, stride=2), :]
        odd = mask_t[pl.ds(1, cells, stride=2), :]
        for x in range(CHUNK):
            row = narrow_row(snaps, base + x, even[:, x:x + 1], odd[:, x:x + 1], ctaps)
            narrowed[2 + base + x] = row
        return carry

    lax.fori_loop(0, chunks, narrow, 0)
    for i in range(rows // 2):
        total = rtaps[0] * narrowed[2 * i]
        for k in range(1, TAPS):
            total = total + rtaps[k] * narrowed[2 * i + k]
        filtered[i * cells:(i + 1) * cells, :] = total
    up_ref[...] = rtaps[4] * narrowed[2] + rtaps[5] * narrowed[3]
    down_ref[...] = rtaps[0] * narrowed[rows] + rtaps[1] * narrowed[rows + 1]
    me = me_ref[0]
    piece = filtered.shape[0] // parts
    for k in range(parts):
        inner = pl.multiple_of((me ^ k) * piece + cells, 8)
        bigs[k][...] = filtered[pl.ds(inner, piece - 2 * cells), :]
    for d in range(parts):
        small_ref[2 * d * cells:(2 * d + 1) * cells, :] = filtered[d * piece:d * piece + cells, :]
        small_ref[(2 * d + 1) * cells:(2 * d + 2) * cells, :] = filtered[(d + 1) * piece - cells:(d + 1) * piece, :]


def edge_kernel(parts, me_ref, small_ref, above_ref, below_ref, *rest):
    outs, (held,) = rest[:parts], rest[parts:]
    held[...] = small_ref[...]
    cells = above_ref.shape[0]
    size = held.shape[0]
    held[:cells, :] = held[:cells, :] + above_ref[...]
    held[size - cells:, :] = held[size - cells:, :] + below_ref[...]
    me = me_ref[0]
    for k in range(parts):
        outs[k][...] = held[pl.ds(pl.multiple_of((me ^ k) * 2 * cells, 8), 2 * cells), :]


def probe_kernel(parts, me_ref, *refs):
    bigs, smalls, probes_ref, out_ref = refs[:parts], refs[parts:2 * parts], refs[2 * parts], refs[2 * parts + 1]
    me = me_ref[0]
    cells = smalls[0].shape[0] // 2
    inner = bigs[0].shape[0]
    piece = inner + 2 * cells
    total = None
    for k in range(parts):
        base = (me ^ k) * piece
        first = probes_ref[pl.ds(pl.multiple_of(base, 8), cells), :]
        middle = probes_ref[pl.ds(pl.multiple_of(base + cells, 8), inner), :]
        last = probes_ref[pl.ds(pl.multiple_of(base + cells + inner, 8), cells), :]
        mine = jnp.concatenate([bigs[k][...], smalls[k][...]], axis=0)
        there = jnp.concatenate([middle, first, last], axis=0)
        term = exact_dot(mine, there, ((0,), (0,)))
        total = term if total is None else total + term
    out_ref[...] = total


def block_order(parts):
    return [(a, b) for a in range(parts) for b in range(a, parts)]


def gram_kernel(parts, span, me_ref, *refs):
    bigs, smalls = refs[:parts], refs[parts:2 * parts]
    send_ref, keep_ref, wide, flat = refs[2 * parts:]
    me, owner = me_ref[0], me_ref[1]
    inner, cols = bigs[0].shape
    for k in range(parts):
        at = pl.ds(pl.multiple_of((me ^ k) * cols, cols), cols)
        wide[:inner, at] = bigs[k][...]
        wide[inner:, at] = smalls[k][...]
    where = {ab: j for j, ab in enumerate(block_order(parts))}
    for a in range(0, parts, 2):
        left = wide[:, a * cols:(a + 2) * cols]
        for b in range(a, parts, 2):
            right = wide[:, b * cols:(b + 2) * cols]
            prod = exact_dot(left, right, ((0,), (0,)))
            for i in range(2):
                for j in range(2):
                    if (a + i, b + j) in where:
                        at = where[a + i, b + j] * cols
                        flat[at:at + cols, :] = prod[i * cols:(i + 1) * cols, j * cols:(j + 1) * cols]
    size = flat.shape[0] // (parts * span)
    for k in range(parts * span):
        out = send_ref if k % 2 else keep_ref
        out[k // 2] = flat[pl.ds(pl.multiple_of((owner ^ k) * size, 8), size), :]


def split(x):
    high = x.astype(jnp.bfloat16)
    return high, (x - high.astype(F32)).astype(jnp.bfloat16)


def dot(a, b, dims):
    return lax.dot_general(a, b, (dims, ((), ())), preferred_element_type=F32)


def dot_parts(a, b, dims=((1,), (0,))):
    (ah, al), (bh, bl) = a, b
    return dot(ah, bh, dims) + (dot(ah, bl, dims) + dot(al, bh, dims))


def exact_dot(a, b, dims=((1,), (0,))):
    return lax.dot_general(a, b, (dims, ((), ())), precision=exact, preferred_element_type=F32)


def combine_of(grams):
    order = grams[0].shape[0]
    diagonal = lax.broadcasted_iota(jnp.int32, (order, order), 0) == lax.broadcasted_iota(jnp.int32, (order, order), 1)
    signs = []
    for gram in grams:
        mean = jnp.sum(jnp.where(diagonal, gram, 0.0)) / order
        shifted = jnp.where(diagonal, gram - mean, gram)
        signs.append(shifted / jnp.sqrt(jnp.sum(shifted * shifted, keepdims=True) + 1e-6))
    for _ in range(SIGN_STEPS):
        halves = [split(y) for y in signs]
        squares = [split(dot_parts(y, y)) for y in halves]
        cubes = [dot_parts(y, s) for y, s in zip(halves, squares)]
        signs = [1.5 * y - 0.5 * c for y, c in zip(signs, cubes)]
    half = order // 2
    combines = []
    for y in signs:
        projector = 0.5 * (jnp.where(diagonal, 1.0, 0.0) + y)
        combines.append(projector[:, :half] + projector[:, half:])
    return combines


def merge_kernel(parts, span, me_ref, even_ref, odd_ref, wide_ref, probe_ref, *refs):
    outs, (flat, weight, turned) = refs[:parts], refs[parts:]
    me, owner = me_ref[0], me_ref[1]
    size, cols = even_ref.shape[1:]
    for k in range(parts * span):
        source = odd_ref if k % 2 else even_ref
        flat[pl.ds(pl.multiple_of((owner ^ k) * size, 8), size), :] = source[k // 2]
    blocks = {ab: flat[j * cols:(j + 1) * cols, :] for j, ab in enumerate(block_order(parts))}
    weights, count = None, parts
    while count > 1:
        grams = []
        for p in range(0, count, 2):
            low = jnp.concatenate([blocks[p, p], blocks[p, p + 1]], axis=1)
            high = jnp.concatenate([blocks[p, p + 1].T, blocks[p + 1, p + 1]], axis=1)
            grams.append(jnp.concatenate([low, high], axis=0))
        combines = combine_of(grams)
        if weights is None:
            weights = combines
        else:
            per = len(weights) // len(combines)
            weights = [
                exact_dot(w, combines[i // per][(i % per) * cols:(i % per + 1) * cols, :])
                for i, w in enumerate(weights)
            ]
            weights = [jnp.concatenate(weights[i:i + per], axis=0) for i in range(0, len(weights), per)]
        merged = {}
        if count > 2:
            for p in range(count // 2):
                for q in range(p, count // 2):
                    if p == q:
                        cross = grams[p]
                    else:
                        cross = jnp.concatenate([
                            jnp.concatenate([blocks[2 * p + i, 2 * q], blocks[2 * p + i, 2 * q + 1]], axis=1)
                            for i in range(2)
                        ], axis=0)
                    right = exact_dot(cross, combines[q])
                    merged[p, q] = exact_dot(combines[p], right, ((0,), (0,)))
        blocks, count = merged, count // 2
    weight[...] = weights[0]
    total = dot_parts(split(wide_ref[...]), split(weight[...]))
    rows = total.shape[0]
    turned[:, :rows] = total.T
    mine = weight[pl.ds(pl.multiple_of(me * cols, cols), cols), :]
    turned[:, rows:] = exact_dot(mine, probe_ref[...], ((0,), (0,)))
    width = cols // parts
    for k in range(parts):
        outs[k][...] = turned[pl.ds(pl.multiple_of((me ^ k) * width, 8), width), :]


def final_kernel(parts, me_ref, *refs):
    pieces, (basis_ref, coef_ref) = refs[:parts], refs[parts:]
    me = me_ref[0]
    per, cells = basis_ref.shape[0] // parts, basis_ref.shape[2]
    order = list(range(1, per - 1)) + [0, per - 1]
    total = None
    for k in range(parts):
        base = (me ^ k) * per
        for at, i in enumerate(order):
            basis_ref[base + i] = pieces[k][:, at * cells:(at + 1) * cells]
        tail = pieces[k][:, per * cells:]
        total = tail if total is None else total + tail
    coef_ref[...] = total


def shape(*dims):
    return jax.ShapeDtypeStruct(dims, F32)


def local(snapshots, land_mask, taps_rows, taps_cols, probes):
    rows, grid_cols, cols = snapshots.shape
    half_rows, half_cols = rows // 2, grid_cols // 2
    parts, patches = lax.axis_size("tm"), lax.axis_size("space")
    cells = half_rows * half_cols
    piece = cells // parts
    inner = piece - 2 * half_cols
    span = 2 if patches > 1 else 1
    position, patch = lax.axis_index("tm"), lax.axis_index("space")
    me = jnp.stack([position, position + parts * (patch % span)]).astype(jnp.int32)

    outs = pl.pallas_call(
        functools.partial(filter_kernel, parts),
        out_shape=[shape(inner, cols)] * parts + [shape(2 * parts * half_cols, cols)] + [shape(half_cols, cols)] * 2,
        in_specs=[scalars(), scalars(), scalars(), pl.BlockSpec(memory_space=pltpu.HBM), whole()],
        out_specs=[whole()] * (parts + 3),
        scratch_shapes=[
            pltpu.VMEM((rows, grid_cols, cols), F32),
            pltpu.SemaphoreType.DMA((rows // CHUNK,)),
            pltpu.VMEM((grid_cols, CHUNK), F32),
            pltpu.VMEM((rows + 4, half_cols, cols), F32),
            pltpu.VMEM((cells, cols), F32),
        ],
        compiler_params=params(),
        name="filter",
    )(me, taps_rows, taps_cols, snapshots, land_mask)
    bigs, (small, to_above, to_below) = outs[:parts], outs[parts:]
    up = [(i, i + 1) for i in range(patches - 1)]
    above = lax.ppermute(to_below, "space", up)
    below = lax.ppermute(to_above, "space", [(j, i) for i, j in up])
    far_bigs = [bigs[0]] + [swap(bigs[k], "tm", k) for k in range(1, parts)]

    smalls = pl.pallas_call(
        functools.partial(edge_kernel, parts),
        out_shape=[shape(2 * half_cols, cols)] * parts,
        in_specs=[scalars()] + [whole()] * 3,
        out_specs=[whole()] * parts,
        scratch_shapes=[pltpu.VMEM((2 * parts * half_cols, cols), F32)],
        compiler_params=params(),
        name="edge",
    )(me, small, above, below)
    far_smalls = [smalls[0]] + [swap(smalls[k], "tm", k) for k in range(1, parts)]

    probe_sum = pl.pallas_call(
        functools.partial(probe_kernel, parts),
        out_shape=shape(cols, cols),
        in_specs=[scalars()] + [whole()] * (2 * parts + 1),
        out_specs=whole(),
        compiler_params=params(),
        cost_estimate=pl.CostEstimate(flops=12 * cells * cols * cols, bytes_accessed=8 * cells * cols, transcendentals=0),
        name="probe",
    )(me, *bigs, *smalls, probes.reshape(cells, cols))
    bits = [1 << b for b in range(patches.bit_length() - 1)]
    for bit in bits[:2]:
        probe_sum = probe_sum + swap(probe_sum, "space", bit)
    probe_sum, *far = lax.optimization_barrier([probe_sum] + far_bigs + far_smalls)

    blocks = parts * (parts + 1) // 2
    shares = parts * span
    size = blocks * cols // shares
    send, keep, wide = pl.pallas_call(
        functools.partial(gram_kernel, parts, span),
        out_shape=[shape(shares // 2, size, cols)] * 2 + [shape(piece, parts * cols)],
        in_specs=[scalars()] + [whole()] * (2 * parts),
        out_specs=[whole()] * 3,
        scratch_shapes=[pltpu.VMEM((blocks * cols, cols), F32)],
        compiler_params=params(),
        name="gram",
    )(me, *far)
    for bit in bits[2:]:
        probe_sum = probe_sum + swap(probe_sum, "space", bit)
    got = swap(send, "tm", 1)
    mine = keep[0] + got[0]
    for h in range(1, shares // 2):
        mine = mine + swap_both(keep[h] + got[h], 2 * h)
    mine, probe_sum = lax.optimization_barrier((mine, probe_sum))
    for bit in bits[1:]:
        mine = mine + swap(mine, "space", bit)
    even = jnp.stack([mine] + [swap_both(mine, 2 * h) for h in range(1, shares // 2)])
    odd = swap(even, "tm", 1)

    width = cols // parts
    sent = pl.pallas_call(
        functools.partial(merge_kernel, parts, span),
        out_shape=[shape(width, piece + cols)] * parts,
        in_specs=[scalars()] + [whole()] * 4,
        out_specs=[whole()] * parts,
        scratch_shapes=[
            pltpu.VMEM((blocks * cols, cols), F32),
            pltpu.VMEM((parts * cols, cols), F32),
            pltpu.VMEM((cols, piece + cols), F32),
        ],
        compiler_params=params(),
        name="merge",
    )(me, even, odd, wide, probe_sum)
    last = [sent[0]] + [swap(sent[k], "tm", k) for k in range(1, parts)]

    basis, coefficients = pl.pallas_call(
        functools.partial(final_kernel, parts),
        out_shape=(shape(half_rows, width, half_cols), shape(width, cols)),
        in_specs=[scalars()] + [whole()] * parts,
        out_specs=(whole(), whole()),
        compiler_params=params(),
        name="final",
    )(me, *last)
    return basis.transpose(0, 2, 1), coefficients


def solution(mesh):
    placed = (P("space", None, "tm"), P("space", None), P(), P(), P("space", None, None))
    return jax.shard_map(
        local,
        mesh=mesh,
        in_specs=placed,
        out_specs=(P("space", None, "tm"), P("tm", None)),
        check_vma=False,
    )
```

```python
import functools

import jax
import jax.numpy as jnp
from jax import lax
from jax.experimental import pallas as pl
from jax.experimental.pallas import tpu as pltpu
from jax.sharding import PartitionSpec as P

SIGN_STEPS = 8
TAPS = 6
CHUNK = 8
exact = lax.Precision.HIGHEST
F32 = jnp.float32
VMEM_LIMIT = 48 * 1024 * 1024
FULL_VMEM = 60 * 1024 * 1024


def params(limit=VMEM_LIMIT):
    return pltpu.CompilerParams(vmem_limit_bytes=limit)


def whole():
    return pl.BlockSpec(memory_space=pltpu.VMEM)


def scalars():
    return pl.BlockSpec(memory_space=pltpu.SMEM)


def swap(x, axis, mask):
    count = lax.axis_size(axis)
    return lax.ppermute(x, axis, [(i, i ^ mask) for i in range(count)])


def swap_both(x, mask):
    parts, patches = lax.axis_size("tm"), lax.axis_size("space")
    route = []
    for t in range(parts):
        for s in range(patches):
            there = (t ^ (mask % parts)) * patches + (s ^ (mask // parts))
            route.append((t * patches + s, there))
    return lax.ppermute(x, ("tm", "space"), route)


def shift_rows(x, by):
    edge = jnp.zeros((1, x.shape[1]), x.dtype)
    if by > 0:
        return jnp.concatenate([edge, x[:-1]], axis=0)
    return jnp.concatenate([x[1:], edge], axis=0)


def narrow_row(snap_ref, x, mask_even, mask_odd, taps):
    half = snap_ref.shape[1] // 2
    even = snap_ref[x, pl.ds(0, half, stride=2), :] * mask_even
    odd = snap_ref[x, pl.ds(1, half, stride=2), :] * mask_odd
    before = taps[0] * even + taps[1] * odd
    here = taps[2] * even + taps[3] * odd
    after = taps[4] * even + taps[5] * odd
    return shift_rows(before, 1) + here + shift_rows(after, -1)


def filter_kernel(parts, me_ref, taps_ref, snap_hbm, mask_ref, *rest):
    bigs, (small_ref, up_ref, down_ref) = rest[:parts], rest[parts:parts + 3]
    snaps, sems, mask_t, narrowed, filtered = rest[parts + 3:]
    rows, cells = snaps.shape[0], narrowed.shape[1]
    chunks = rows // CHUNK

    def fetch(c):
        at = pl.ds(c * CHUNK, CHUNK)
        return pltpu.make_async_copy(snap_hbm.at[at], snaps.at[at], sems.at[c])

    for c in range(chunks):
        fetch(c).start()
    rtaps = [taps_ref[k] for k in range(TAPS)]
    ctaps = [taps_ref[TAPS + k] for k in range(TAPS)]
    edge = jnp.zeros((2,) + narrowed.shape[1:], F32)
    narrowed[0:2] = edge
    narrowed[rows + 2:rows + 4] = edge

    def narrow(c, carry):
        fetch(c).wait()
        base = pl.multiple_of(c * CHUNK, CHUNK)
        mask_t[...] = mask_ref[pl.ds(base, CHUNK), :].astype(F32).T
        even = mask_t[pl.ds(0, cells, stride=2), :]
        odd = mask_t[pl.ds(1, cells, stride=2), :]
        for x in range(CHUNK):
            row = narrow_row(snaps, base + x, even[:, x:x + 1], odd[:, x:x + 1], ctaps)
            narrowed[2 + base + x] = row
        return carry

    lax.fori_loop(0, chunks, narrow, 0)
    for i in range(rows // 2):
        total = rtaps[0] * narrowed[2 * i]
        for k in range(1, TAPS):
            total = total + rtaps[k] * narrowed[2 * i + k]
        filtered[i * cells:(i + 1) * cells, :] = total
    up_ref[...] = rtaps[4] * narrowed[2] + rtaps[5] * narrowed[3]
    down_ref[...] = rtaps[0] * narrowed[rows] + rtaps[1] * narrowed[rows + 1]
    me = me_ref[0]
    piece = filtered.shape[0] // parts
    for k in range(parts):
        inner = pl.multiple_of((me ^ k) * piece + cells, 8)
        bigs[k][...] = filtered[pl.ds(inner, piece - 2 * cells), :]
    for d in range(parts):
        small_ref[2 * d * cells:(2 * d + 1) * cells, :] = filtered[d * piece:d * piece + cells, :]
        small_ref[(2 * d + 1) * cells:(2 * d + 2) * cells, :] = filtered[(d + 1) * piece - cells:(d + 1) * piece, :]


def edge_kernel(parts, me_ref, small_ref, above_ref, below_ref, *rest):
    outs, (held,) = rest[:parts], rest[parts:]
    held[...] = small_ref[...]
    cells = above_ref.shape[0]
    size = held.shape[0]
    held[:cells, :] = held[:cells, :] + above_ref[...]
    held[size - cells:, :] = held[size - cells:, :] + below_ref[...]
    me = me_ref[0]
    for k in range(parts):
        outs[k][...] = held[pl.ds(pl.multiple_of((me ^ k) * 2 * cells, 8), 2 * cells), :]


def probe_kernel(parts, me_ref, *refs):
    bigs, smalls, probes_ref, out_ref = refs[:parts], refs[parts:2 * parts], refs[2 * parts], refs[2 * parts + 1]
    me = me_ref[0]
    cells = smalls[0].shape[0] // 2
    inner = bigs[0].shape[0]
    piece = inner + 2 * cells
    total = None
    for k in range(parts):
        base = (me ^ k) * piece
        first = probes_ref[pl.ds(pl.multiple_of(base, 8), cells), :]
        middle = probes_ref[pl.ds(pl.multiple_of(base + cells, 8), inner), :]
        last = probes_ref[pl.ds(pl.multiple_of(base + cells + inner, 8), cells), :]
        mine = jnp.concatenate([bigs[k][...], smalls[k][...]], axis=0)
        there = jnp.concatenate([middle, first, last], axis=0)
        term = exact_dot(mine, there, ((0,), (0,)))
        total = term if total is None else total + term
    out_ref[...] = total


def block_order(parts):
    return [(a, b) for a in range(parts) for b in range(a, parts)]


def gram_kernel(parts, span, me_ref, *refs):
    bigs, smalls = refs[:parts], refs[parts:2 * parts]
    send_ref, keep_ref, wide, flat = refs[2 * parts:]
    me, owner = me_ref[0], me_ref[1]
    inner, cols = bigs[0].shape
    for k in range(parts):
        at = pl.ds(pl.multiple_of((me ^ k) * cols, cols), cols)
        wide[:inner, at] = bigs[k][...]
        wide[inner:, at] = smalls[k][...]
    where = {ab: j for j, ab in enumerate(block_order(parts))}
    for a in range(0, parts, 2):
        left = wide[:, a * cols:(a + 2) * cols]
        for b in range(a, parts, 2):
            right = wide[:, b * cols:(b + 2) * cols]
            prod = exact_dot(left, right, ((0,), (0,)))
            for i in range(2):
                for j in range(2):
                    if (a + i, b + j) in where:
                        at = where[a + i, b + j] * cols
                        flat[at:at + cols, :] = prod[i * cols:(i + 1) * cols, j * cols:(j + 1) * cols]
    size = flat.shape[0] // (parts * span)
    for k in range(parts * span):
        out = send_ref if k % 2 else keep_ref
        out[k // 2] = flat[pl.ds(pl.multiple_of((owner ^ k) * size, 8), size), :]


def split(x):
    high = x.astype(jnp.bfloat16)
    return high, (x - high.astype(F32)).astype(jnp.bfloat16)


def dot(a, b, dims):
    return lax.dot_general(a, b, (dims, ((), ())), preferred_element_type=F32)


def dot_parts(a, b, dims=((1,), (0,))):
    (ah, al), (bh, bl) = a, b
    rows = ah.shape[0]
    both = dot(jnp.concatenate([ah, al], axis=0), bh, dims)
    return both[:rows] + (dot(ah, bl, dims) + both[rows:])


def exact_dot(a, b, dims=((1,), (0,))):
    return lax.dot_general(a, b, (dims, ((), ())), precision=exact, preferred_element_type=F32)


def combine_of(grams):
    order = grams[0].shape[0]
    diagonal = lax.broadcasted_iota(jnp.int32, (order, order), 0) == lax.broadcasted_iota(jnp.int32, (order, order), 1)
    signs = []
    for gram in grams:
        mean = jnp.sum(jnp.where(diagonal, gram, 0.0)) / order
        shifted = jnp.where(diagonal, gram - mean, gram)
        signs.append(shifted / jnp.sqrt(jnp.sum(shifted * shifted, keepdims=True) + 1e-6))
    for _ in range(SIGN_STEPS):
        halves = [split(y) for y in signs]
        squares = [split(dot_parts(y, y)) for y in halves]
        cubes = [dot_parts(s, y) for y, s in zip(halves, squares)]
        signs = [1.5 * y - 0.5 * c for y, c in zip(signs, cubes)]
    half = order // 2
    combines = []
    for y in signs:
        projector = 0.5 * (jnp.where(diagonal, 1.0, 0.0) + y)
        combines.append(projector[:, :half] + projector[:, half:])
    return combines


def merge_kernel(parts, span, me_ref, even_ref, odd_ref, wide_ref, probe_ref, *refs):
    outs, (flat, weight, turned) = refs[:parts], refs[parts:]
    me, owner = me_ref[0], me_ref[1]
    size, cols = even_ref.shape[1:]
    for k in range(parts * span):
        source = odd_ref if k % 2 else even_ref
        flat[pl.ds(pl.multiple_of((owner ^ k) * size, 8), size), :] = source[k // 2]
    blocks = {ab: flat[j * cols:(j + 1) * cols, :] for j, ab in enumerate(block_order(parts))}
    weights, count = None, parts
    while count > 1:
        grams = []
        for p in range(0, count, 2):
            low = jnp.concatenate([blocks[p, p], blocks[p, p + 1]], axis=1)
            high = jnp.concatenate([blocks[p, p + 1].T, blocks[p + 1, p + 1]], axis=1)
            grams.append(jnp.concatenate([low, high], axis=0))
        combines = combine_of(grams)
        if weights is None:
            weights = combines
        else:
            per = len(weights) // len(combines)
            weights = [
                exact_dot(w, combines[i // per][(i % per) * cols:(i % per + 1) * cols, :])
                for i, w in enumerate(weights)
            ]
            weights = [jnp.concatenate(weights[i:i + per], axis=0) for i in range(0, len(weights), per)]
        merged = {}
        if count > 2:
            for p in range(count // 2):
                for q in range(p, count // 2):
                    if p == q:
                        cross = grams[p]
                    else:
                        cross = jnp.concatenate([
                            jnp.concatenate([blocks[2 * p + i, 2 * q], blocks[2 * p + i, 2 * q + 1]], axis=1)
                            for i in range(2)
                        ], axis=0)
                    right = exact_dot(cross, combines[q])
                    merged[p, q] = exact_dot(combines[p], right, ((0,), (0,)))
        blocks, count = merged, count // 2
    weight[...] = weights[0]
    total = dot_parts(split(wide_ref[...]), split(weight[...]))
    rows = total.shape[0]
    turned[:, :rows] = total.T
    mine = weight[pl.ds(pl.multiple_of(me * cols, cols), cols), :]
    turned[:, rows:] = exact_dot(mine, probe_ref[...], ((0,), (0,)))
    width = cols // parts
    for k in range(parts):
        outs[k][...] = turned[pl.ds(pl.multiple_of((me ^ k) * width, 8), width), :]


def final_kernel(parts, me_ref, *refs):
    pieces, (basis_ref, coef_ref) = refs[:parts], refs[parts:]
    me = me_ref[0]
    per, cells = basis_ref.shape[0] // parts, basis_ref.shape[2]
    order = list(range(1, per - 1)) + [0, per - 1]
    total = None
    for k in range(parts):
        base = (me ^ k) * per
        for at, i in enumerate(order):
            basis_ref[base + i] = pieces[k][:, at * cells:(at + 1) * cells]
        tail = pieces[k][:, per * cells:]
        total = tail if total is None else total + tail
    coef_ref[...] = total


def shape(*dims):
    return jax.ShapeDtypeStruct(dims, F32)


def local(snapshots, land_mask, taps_rows, taps_cols, probes):
    rows, grid_cols, cols = snapshots.shape
    half_rows, half_cols = rows // 2, grid_cols // 2
    parts, patches = lax.axis_size("tm"), lax.axis_size("space")
    cells = half_rows * half_cols
    piece = cells // parts
    inner = piece - 2 * half_cols
    span = 2 if patches > 1 else 1
    position, patch = lax.axis_index("tm"), lax.axis_index("space")
    me = jnp.stack([position, position + parts * (patch % span)]).astype(jnp.int32)

    outs = pl.pallas_call(
        functools.partial(filter_kernel, parts),
        out_shape=[shape(inner, cols)] * parts + [shape(2 * parts * half_cols, cols)] + [shape(half_cols, cols)] * 2,
        in_specs=[scalars(), scalars(), pl.BlockSpec(memory_space=pltpu.HBM), whole()],
        out_specs=[whole()] * (parts + 3),
        scratch_shapes=[
            pltpu.VMEM((rows, grid_cols, cols), F32),
            pltpu.SemaphoreType.DMA((rows // CHUNK,)),
            pltpu.VMEM((grid_cols, CHUNK), F32),
            pltpu.VMEM((rows + 4, half_cols, cols), F32),
            pltpu.VMEM((cells, cols), F32),
        ],
        compiler_params=params(FULL_VMEM),
        name="filter",
    )(me, jnp.concatenate([taps_rows, taps_cols]), snapshots, land_mask)
    bigs, (small, to_above, to_below) = outs[:parts], outs[parts:]
    up = [(i, i + 1) for i in range(patches - 1)]
    above = lax.ppermute(to_below, "space", up)
    below = lax.ppermute(to_above, "space", [(j, i) for i, j in up])
    far_bigs = [bigs[0]] + [swap(bigs[k], "tm", k) for k in range(1, parts)]
    above, below, *far_bigs = lax.optimization_barrier([above, below] + far_bigs)

    smalls = pl.pallas_call(
        functools.partial(edge_kernel, parts),
        out_shape=[shape(2 * half_cols, cols)] * parts,
        in_specs=[scalars()] + [whole()] * 3,
        out_specs=[whole()] * parts,
        scratch_shapes=[pltpu.VMEM((2 * parts * half_cols, cols), F32)],
        compiler_params=params(),
        name="edge",
    )(me, small, above, below)
    far_smalls = [smalls[0]] + [swap(smalls[k], "tm", k) for k in range(1, parts)]

    probe_sum = pl.pallas_call(
        functools.partial(probe_kernel, parts),
        out_shape=shape(cols, cols),
        in_specs=[scalars()] + [whole()] * (2 * parts + 1),
        out_specs=whole(),
        compiler_params=params(),
        cost_estimate=pl.CostEstimate(flops=12 * cells * cols * cols, bytes_accessed=8 * cells * cols, transcendentals=0),
        name="probe",
    )(me, *bigs, *smalls, probes.reshape(cells, cols))
    bits = [1 << b for b in range(patches.bit_length() - 1)]
    for bit in bits[:1]:
        probe_sum = probe_sum + swap(probe_sum, "space", bit)
    probe_sum, *far = lax.optimization_barrier([probe_sum] + far_bigs + far_smalls)

    blocks = parts * (parts + 1) // 2
    shares = parts * span
    size = blocks * cols // shares
    send, keep, wide = pl.pallas_call(
        functools.partial(gram_kernel, parts, span),
        out_shape=[shape(shares // 2, size, cols)] * 2 + [shape(piece, parts * cols)],
        in_specs=[scalars()] + [whole()] * (2 * parts),
        out_specs=[whole()] * 3,
        scratch_shapes=[pltpu.VMEM((blocks * cols, cols), F32)],
        compiler_params=params(),
        name="gram",
    )(me, *far)
    for bit in bits[1:-1]:
        probe_sum = probe_sum + swap(probe_sum, "space", bit)
    got = swap(send, "tm", 1)
    mine = keep[0] + got[0]
    for h in range(1, shares // 2):
        mine = mine + swap_both(keep[h] + got[h], 2 * h)
    mine, probe_sum = lax.optimization_barrier((mine, probe_sum))
    for bit in bits[1:]:
        mine = mine + swap(mine, "space", bit)
    mine, probe_sum = lax.optimization_barrier((mine, probe_sum))
    for bit in bits[1:][-1:]:
        probe_sum = probe_sum + swap(probe_sum, "space", bit)
    even = jnp.stack([mine] + [swap_both(mine, 2 * h) for h in range(1, shares // 2)])
    odd = swap(even, "tm", 1)

    width = cols // parts
    sent = pl.pallas_call(
        functools.partial(merge_kernel, parts, span),
        out_shape=[shape(width, piece + cols)] * parts,
        in_specs=[scalars()] + [whole()] * 4,
        out_specs=[whole()] * parts,
        scratch_shapes=[
            pltpu.VMEM((blocks * cols, cols), F32),
            pltpu.VMEM((parts * cols, cols), F32),
            pltpu.VMEM((cols, piece + cols), F32),
        ],
        compiler_params=params(),
        name="merge",
    )(me, even, odd, wide, probe_sum)
    last = [sent[0]] + [swap(sent[k], "tm", k) for k in range(1, parts)]

    basis, coefficients = pl.pallas_call(
        functools.partial(final_kernel, parts),
        out_shape=(shape(half_rows, width, half_cols), shape(width, cols)),
        in_specs=[scalars()] + [whole()] * parts,
        out_specs=(whole(), whole()),
        compiler_params=params(),
        name="final",
    )(me, *last)
    return basis.transpose(0, 2, 1), coefficients


def solution(mesh):
    placed = (P("space", None, "tm"), P("space", None), P(), P(), P("space", None, None))
    return jax.shard_map(
        local,
        mesh=mesh,
        in_specs=placed,
        out_specs=(P("space", None, "tm"), P("tm", None)),
        check_vma=False,
    )
```

```python
import functools

import jax
import jax.numpy as jnp
from jax import lax
from jax.experimental import pallas as pl
from jax.experimental.pallas import tpu as pltpu
from jax.sharding import PartitionSpec as P

SIGN_STEPS = 8
TAPS = 6
CHUNK = 8
exact = lax.Precision.HIGHEST
F32 = jnp.float32
VMEM_LIMIT = 48 * 1024 * 1024


def params():
    return pltpu.CompilerParams(vmem_limit_bytes=VMEM_LIMIT)


def whole():
    return pl.BlockSpec(memory_space=pltpu.VMEM)


def scalars():
    return pl.BlockSpec(memory_space=pltpu.SMEM)


def swap(x, axis, mask):
    count = lax.axis_size(axis)
    return lax.ppermute(x, axis, [(i, i ^ mask) for i in range(count)])


def swap_both(x, mask):
    parts, patches = lax.axis_size("tm"), lax.axis_size("space")
    route = []
    for t in range(parts):
        for s in range(patches):
            there = (t ^ (mask % parts)) * patches + (s ^ (mask // parts))
            route.append((t * patches + s, there))
    return lax.ppermute(x, ("tm", "space"), route)


def to_edge_owner(x, k):
    parts, patches = lax.axis_size("tm"), lax.axis_size("space")
    route = []
    for s in range(patches - 1):
        route.append((k * patches + s, s + 1))
        route.append(((k ^ (parts - 1)) * patches + s + 1, (parts - 1) * patches + s))
    return lax.ppermute(x, ("tm", "space"), route)


def shift_rows(x, by):
    edge = jnp.zeros((1, x.shape[1]), x.dtype)
    if by > 0:
        return jnp.concatenate([edge, x[:-1]], axis=0)
    return jnp.concatenate([x[1:], edge], axis=0)


def narrow_row(snap_ref, x, mask_even, mask_odd, taps):
    half = snap_ref.shape[1] // 2
    even = snap_ref[x, pl.ds(0, half, stride=2), :] * mask_even
    odd = snap_ref[x, pl.ds(1, half, stride=2), :] * mask_odd
    before = taps[0] * even + taps[1] * odd
    here = taps[2] * even + taps[3] * odd
    after = taps[4] * even + taps[5] * odd
    return shift_rows(before, 1) + here + shift_rows(after, -1)


def filter_kernel(parts, me_ref, taps_ref, snap_hbm, mask_ref, *rest):
    pieces, shares, edges_ref = rest[:parts], rest[parts:2 * parts], rest[2 * parts]
    snaps, sems, mask_t, narrowed, filtered = rest[2 * parts + 1:]
    rows, cells = snaps.shape[0], narrowed.shape[1]
    chunks = rows // CHUNK

    def fetch(c):
        at = pl.ds(c * CHUNK, CHUNK)
        return pltpu.make_async_copy(snap_hbm.at[at], snaps.at[at], sems.at[c])

    for c in range(chunks):
        fetch(c).start()
    rtaps = [taps_ref[k] for k in range(TAPS)]
    ctaps = [taps_ref[TAPS + k] for k in range(TAPS)]
    edge = jnp.zeros((2,) + narrowed.shape[1:], F32)
    narrowed[0:2] = edge
    narrowed[rows + 2:rows + 4] = edge

    def narrow(c, carry):
        fetch(c).wait()
        base = pl.multiple_of(c * CHUNK, CHUNK)
        mask_t[...] = mask_ref[pl.ds(base, CHUNK), :].astype(F32).T
        even = mask_t[pl.ds(0, cells, stride=2), :]
        odd = mask_t[pl.ds(1, cells, stride=2), :]
        for x in range(CHUNK):
            row = narrow_row(snaps, base + x, even[:, x:x + 1], odd[:, x:x + 1], ctaps)
            narrowed[2 + base + x] = row
        return carry

    lax.fori_loop(0, chunks, narrow, 0)
    for i in range(rows // 2):
        total = rtaps[0] * narrowed[2 * i]
        for k in range(1, TAPS):
            total = total + rtaps[k] * narrowed[2 * i + k]
        filtered[i * cells:(i + 1) * cells, :] = total
    edges_ref[:cells, :] = rtaps[0] * narrowed[rows] + rtaps[1] * narrowed[rows + 1]
    edges_ref[cells:, :] = rtaps[4] * narrowed[2] + rtaps[5] * narrowed[3]
    me = me_ref[0]
    size = filtered.shape[0] // parts
    for k in range(parts):
        pieces[k][...] = filtered[pl.ds(pl.multiple_of((me ^ k) * size, 8), size), :]
        which = jnp.where((me ^ k) == 0, 0, 1)
        shares[k][...] = edges_ref[pl.ds(pl.multiple_of(which * cells, 8), cells), :]


def probe_kernel(parts, me_ref, *refs):
    pieces, (edges_ref, probes_ref, below_ref, above_ref, out_ref) = refs[:parts], refs[parts:]
    me = me_ref[0]
    size = pieces[0].shape[0]
    total = exact_dot(edges_ref[...], jnp.concatenate([below_ref[...], above_ref[...]], axis=0), ((0,), (0,)))
    for k in range(parts):
        there = probes_ref[pl.ds(pl.multiple_of((me ^ k) * size, 8), size), :]
        total = total + exact_dot(pieces[k][...], there, ((0,), (0,)))
    out_ref[...] = total


def block_order(parts):
    return [(a, b) for a in range(parts) for b in range(a, parts)]


def gram_kernel(parts, span, me_ref, *refs):
    pieces, shares = refs[:parts], refs[parts:2 * parts]
    send_ref, keep_ref, wide, flat = refs[2 * parts:]
    me, owner = me_ref[0], me_ref[1]
    size, cols = pieces[0].shape
    cells = shares[0].shape[0]
    edge = pl.ds(pl.multiple_of(jnp.where(me == parts - 1, size - cells, 0), 8), cells)
    for k in range(parts):
        at = pl.ds(pl.multiple_of((me ^ k) * cols, cols), cols)
        wide[:, at] = pieces[k][...]
        wide[edge, at] = wide[edge, at] + shares[k][...]
    where = {ab: j for j, ab in enumerate(block_order(parts))}
    for a in range(0, parts, 2):
        left = wide[:, a * cols:(a + 2) * cols]
        for b in range(a, parts, 2):
            right = wide[:, b * cols:(b + 2) * cols]
            prod = exact_dot(left, right, ((0,), (0,)))
            for i in range(2):
                for j in range(2):
                    if (a + i, b + j) in where:
                        at = where[a + i, b + j] * cols
                        flat[at:at + cols, :] = prod[i * cols:(i + 1) * cols, j * cols:(j + 1) * cols]
    size = flat.shape[0] // (parts * span)
    for k in range(parts * span):
        out = send_ref if k % 2 else keep_ref
        out[k // 2] = flat[pl.ds(pl.multiple_of((owner ^ k) * size, 8), size), :]


def split(x):
    high = x.astype(jnp.bfloat16)
    return high, (x - high.astype(F32)).astype(jnp.bfloat16)


def dot(a, b, dims):
    return lax.dot_general(a, b, (dims, ((), ())), preferred_element_type=F32)


def dot_parts(a, b, dims=((1,), (0,))):
    (ah, al), (bh, bl) = a, b
    rows = ah.shape[0]
    both = dot(jnp.concatenate([ah, al], axis=0), bh, dims)
    return both[:rows] + (dot(ah, bl, dims) + both[rows:])


def exact_dot(a, b, dims=((1,), (0,))):
    return lax.dot_general(a, b, (dims, ((), ())), precision=exact, preferred_element_type=F32)


def combine_of(grams):
    order = grams[0].shape[0]
    diagonal = lax.broadcasted_iota(jnp.int32, (order, order), 0) == lax.broadcasted_iota(jnp.int32, (order, order), 1)
    signs = []
    for gram in grams:
        mean = jnp.sum(jnp.where(diagonal, gram, 0.0)) / order
        shifted = jnp.where(diagonal, gram - mean, gram)
        signs.append(shifted / jnp.sqrt(jnp.sum(shifted * shifted, keepdims=True) + 1e-6))
    for _ in range(SIGN_STEPS):
        halves = [split(y) for y in signs]
        squares = [split(dot_parts(y, y)) for y in halves]
        cubes = [dot_parts(s, y) for y, s in zip(halves, squares)]
        signs = [1.5 * y - 0.5 * c for y, c in zip(signs, cubes)]
    half = order // 2
    combines = []
    for y in signs:
        projector = 0.5 * (jnp.where(diagonal, 1.0, 0.0) + y)
        combines.append(projector[:, :half] + projector[:, half:])
    return combines


def merge_kernel(parts, span, me_ref, even_ref, odd_ref, wide_ref, probe_ref, *refs):
    outs, (flat, weight, turned) = refs[:parts], refs[parts:]
    me, owner = me_ref[0], me_ref[1]
    size, cols = even_ref.shape[1:]
    for k in range(parts * span):
        source = odd_ref if k % 2 else even_ref
        flat[pl.ds(pl.multiple_of((owner ^ k) * size, 8), size), :] = source[k // 2]
    blocks = {ab: flat[j * cols:(j + 1) * cols, :] for j, ab in enumerate(block_order(parts))}
    weights, count = None, parts
    while count > 1:
        grams = []
        for p in range(0, count, 2):
            low = jnp.concatenate([blocks[p, p], blocks[p, p + 1]], axis=1)
            high = jnp.concatenate([blocks[p, p + 1].T, blocks[p + 1, p + 1]], axis=1)
            grams.append(jnp.concatenate([low, high], axis=0))
        combines = combine_of(grams)
        if weights is None:
            weights = combines
        else:
            per = len(weights) // len(combines)
            weights = [
                exact_dot(w, combines[i // per][(i % per) * cols:(i % per + 1) * cols, :])
                for i, w in enumerate(weights)
            ]
            weights = [jnp.concatenate(weights[i:i + per], axis=0) for i in range(0, len(weights), per)]
        merged = {}
        if count > 2:
            for p in range(count // 2):
                for q in range(p, count // 2):
                    if p == q:
                        cross = grams[p]
                    else:
                        cross = jnp.concatenate([
                            jnp.concatenate([blocks[2 * p + i, 2 * q], blocks[2 * p + i, 2 * q + 1]], axis=1)
                            for i in range(2)
                        ], axis=0)
                    right = exact_dot(cross, combines[q])
                    merged[p, q] = exact_dot(combines[p], right, ((0,), (0,)))
        blocks, count = merged, count // 2
    weight[...] = weights[0]
    total = dot_parts(split(wide_ref[...]), split(weight[...]))
    rows = total.shape[0]
    turned[:, :rows] = total.T
    mine = weight[pl.ds(pl.multiple_of(me * cols, cols), cols), :]
    turned[:, rows:] = exact_dot(mine, probe_ref[...], ((0,), (0,)))
    width = cols // parts
    for k in range(parts):
        outs[k][...] = turned[pl.ds(pl.multiple_of((me ^ k) * width, 8), width), :]


def final_kernel(parts, me_ref, *refs):
    pieces, (basis_ref, coef_ref) = refs[:parts], refs[parts:]
    me = me_ref[0]
    per, cells = basis_ref.shape[0] // parts, basis_ref.shape[2]
    total = None
    for k in range(parts):
        base = (me ^ k) * per
        for i in range(per):
            basis_ref[base + i] = pieces[k][:, i * cells:(i + 1) * cells]
        tail = pieces[k][:, per * cells:]
        total = tail if total is None else total + tail
    coef_ref[...] = total


def shape(*dims):
    return jax.ShapeDtypeStruct(dims, F32)


def local(snapshots, land_mask, taps_rows, taps_cols, probes):
    rows, grid_cols, cols = snapshots.shape
    half_rows, half_cols = rows // 2, grid_cols // 2
    parts, patches = lax.axis_size("tm"), lax.axis_size("space")
    cells = half_rows * half_cols
    piece = cells // parts
    span = 2 if patches > 1 else 1
    position, patch = lax.axis_index("tm"), lax.axis_index("space")
    me = jnp.stack([position, position + parts * (patch % span)]).astype(jnp.int32)

    outs = pl.pallas_call(
        functools.partial(filter_kernel, parts),
        out_shape=[shape(piece, cols)] * parts + [shape(half_cols, cols)] * parts + [shape(2 * half_cols, cols)],
        in_specs=[scalars(), scalars(), pl.BlockSpec(memory_space=pltpu.HBM), whole()],
        out_specs=[whole()] * (2 * parts + 1),
        scratch_shapes=[
            pltpu.VMEM((rows, grid_cols, cols), F32),
            pltpu.SemaphoreType.DMA((rows // CHUNK,)),
            pltpu.VMEM((grid_cols, CHUNK), F32),
            pltpu.VMEM((rows + 4, half_cols, cols), F32),
            pltpu.VMEM((cells, cols), F32),
        ],
        compiler_params=params(),
        name="filter",
    )(me, jnp.concatenate([taps_rows, taps_cols]), pltpu.with_memory_space_constraint(snapshots, pltpu.HBM), land_mask)
    pieces, shares, edges = outs[:parts], outs[parts:2 * parts], outs[2 * parts]
    far = [pieces[0]] + [swap(pieces[k], "tm", k) for k in range(1, parts)]
    far += [to_edge_owner(shares[k], k) for k in range(parts)]

    up = [(i, i + 1) for i in range(patches - 1)]
    probes_below = lax.ppermute(probes[0], "space", [(j, i) for i, j in up])
    probes_above = lax.ppermute(probes[-1], "space", up)
    probe_sum = pl.pallas_call(
        functools.partial(probe_kernel, parts),
        out_shape=shape(cols, cols),
        in_specs=[scalars()] + [whole()] * (parts + 4),
        out_specs=whole(),
        compiler_params=params(),
        name="probe",
    )(me, *pieces, edges, probes.reshape(cells, cols), probes_below, probes_above)
    bits = [1 << b for b in range(patches.bit_length() - 1)]
    for bit in bits[:1]:
        probe_sum = probe_sum + swap(probe_sum, "space", bit)
    probe_sum, *far = lax.optimization_barrier([probe_sum] + far)

    blocks = parts * (parts + 1) // 2
    owners = parts * span
    size = blocks * cols // owners
    send, keep, wide = pl.pallas_call(
        functools.partial(gram_kernel, parts, span),
        out_shape=[shape(owners // 2, size, cols)] * 2 + [shape(piece, parts * cols)],
        in_specs=[scalars()] + [whole()] * (2 * parts),
        out_specs=[whole()] * 3,
        scratch_shapes=[pltpu.VMEM((blocks * cols, cols), F32)],
        compiler_params=params(),
        name="gram",
    )(me, *far)
    for bit in bits[1:-1]:
        probe_sum = probe_sum + swap(probe_sum, "space", bit)
    got = swap(send, "tm", 1)
    mine = keep[0] + got[0]
    for h in range(1, owners // 2):
        mine = mine + swap_both(keep[h] + got[h], 2 * h)
    mine, probe_sum = lax.optimization_barrier((mine, probe_sum))
    for bit in bits[1:]:
        mine = mine + swap(mine, "space", bit)
    mine, probe_sum = lax.optimization_barrier((mine, probe_sum))
    for bit in bits[1:][-1:]:
        probe_sum = probe_sum + swap(probe_sum, "space", bit)
    even = [mine] + [swap_both(mine, 2 * h) for h in range(1, owners // 2)]
    probe_sum, *even = lax.optimization_barrier([probe_sum] + even)
    even = jnp.stack(even)
    odd = swap(even, "tm", 1)

    width = cols // parts
    sent = pl.pallas_call(
        functools.partial(merge_kernel, parts, span),
        out_shape=[shape(width, piece + cols)] * parts,
        in_specs=[scalars()] + [whole()] * 4,
        out_specs=[whole()] * parts,
        scratch_shapes=[
            pltpu.VMEM((blocks * cols, cols), F32),
            pltpu.VMEM((parts * cols, cols), F32),
            pltpu.VMEM((cols, piece + cols), F32),
        ],
        compiler_params=params(),
        name="merge",
    )(me, even, odd, wide, probe_sum)
    last = [sent[0]] + [swap(sent[k], "tm", k) for k in range(1, parts)]

    basis, coefficients = pl.pallas_call(
        functools.partial(final_kernel, parts),
        out_shape=(shape(half_rows, width, half_cols), shape(width, cols)),
        in_specs=[scalars()] + [whole()] * parts,
        out_specs=(whole(), whole()),
        compiler_params=params(),
        name="final",
    )(me, *last)
    return basis.transpose(0, 2, 1), coefficients


def solution(mesh):
    placed = (P("space", None, "tm"), P("space", None), P(), P(), P("space", None, None))
    return jax.shard_map(
        local,
        mesh=mesh,
        in_specs=placed,
        out_specs=(P("space", None, "tm"), P("tm", None)),
        check_vma=False,
    )
```

```python
import functools

import jax
import jax.numpy as jnp
from jax import lax
from jax.experimental import pallas as pl
from jax.experimental.pallas import tpu as pltpu
from jax.sharding import PartitionSpec as P

SIGN_STEPS = 8
TAPS = 6
CHUNK = 8
exact = lax.Precision.HIGHEST
F32 = jnp.float32
VMEM_LIMIT = 48 * 1024 * 1024


def params():
    return pltpu.CompilerParams(vmem_limit_bytes=VMEM_LIMIT)


def whole():
    return pl.BlockSpec(memory_space=pltpu.VMEM)


def scalars():
    return pl.BlockSpec(memory_space=pltpu.SMEM)


def swap(x, axis, mask):
    count = lax.axis_size(axis)
    return lax.ppermute(x, axis, [(i, i ^ mask) for i in range(count)])


def swap_both(x, mask):
    parts, patches = lax.axis_size("tm"), lax.axis_size("space")
    route = []
    for t in range(parts):
        for s in range(patches):
            there = (t ^ (mask % parts)) * patches + (s ^ (mask // parts))
            route.append((t * patches + s, there))
    return lax.ppermute(x, ("tm", "space"), route)


def shift_rows(x, by):
    edge = jnp.zeros((1, x.shape[1]), x.dtype)
    if by > 0:
        return jnp.concatenate([edge, x[:-1]], axis=0)
    return jnp.concatenate([x[1:], edge], axis=0)


def narrow_row(snap_ref, x, mask_even, mask_odd, taps):
    half = snap_ref.shape[1] // 2
    even = snap_ref[x, pl.ds(0, half, stride=2), :] * mask_even
    odd = snap_ref[x, pl.ds(1, half, stride=2), :] * mask_odd
    before = taps[0] * even + taps[1] * odd
    here = taps[2] * even + taps[3] * odd
    after = taps[4] * even + taps[5] * odd
    return shift_rows(before, 1) + here + shift_rows(after, -1)


def mask_columns(mask, mask_t, cells):
    mask_t[...] = mask.astype(F32).T
    return mask_t[pl.ds(0, cells, stride=2), :], mask_t[pl.ds(1, cells, stride=2), :]


def edge_kernel(rtaps_ref, ctaps_ref, first_ref, last_ref, mask_first_ref, mask_last_ref, up_ref, down_ref, mask_t):
    ctaps = [ctaps_ref[k] for k in range(TAPS)]
    cells = up_ref.shape[0]
    for out, snaps, mask_ref, taps, at in (
        (up_ref, first_ref, mask_first_ref, (rtaps_ref[4], rtaps_ref[5]), 0),
        (down_ref, last_ref, mask_last_ref, (rtaps_ref[0], rtaps_ref[1]), CHUNK - 2),
    ):
        even, odd = mask_columns(mask_ref[...], mask_t, cells)
        total = taps[0] * narrow_row(snaps, 0, even[:, at:at + 1], odd[:, at:at + 1], ctaps)
        out[...] = total + taps[1] * narrow_row(snaps, 1, even[:, at + 1:at + 2], odd[:, at + 1:at + 2], ctaps)


def filter_kernel(parts, me_ref, rtaps_ref, ctaps_ref, snap_hbm, mask_ref, *rest):
    pieces, (snaps, sems, mask_t, narrowed, filtered) = rest[:parts], rest[parts:]
    rows, cells = snaps.shape[0], narrowed.shape[1]
    chunks = rows // CHUNK

    def fetch(c):
        at = pl.ds(c * CHUNK, CHUNK)
        return pltpu.make_async_copy(snap_hbm.at[at], snaps.at[at], sems.at[c])

    for c in range(chunks):
        fetch(c).start()
    rtaps = [rtaps_ref[k] for k in range(TAPS)]
    ctaps = [ctaps_ref[k] for k in range(TAPS)]
    edge = jnp.zeros((2,) + narrowed.shape[1:], F32)
    narrowed[0:2] = edge
    narrowed[rows + 2:rows + 4] = edge

    def narrow(c, carry):
        fetch(c).wait()
        base = pl.multiple_of(c * CHUNK, CHUNK)
        even, odd = mask_columns(mask_ref[pl.ds(base, CHUNK), :], mask_t, cells)
        for x in range(CHUNK):
            row = narrow_row(snaps, base + x, even[:, x:x + 1], odd[:, x:x + 1], ctaps)
            narrowed[2 + base + x] = row
        return carry

    lax.fori_loop(0, chunks, narrow, 0)
    for i in range(rows // 2):
        total = rtaps[0] * narrowed[2 * i]
        for k in range(1, TAPS):
            total = total + rtaps[k] * narrowed[2 * i + k]
        filtered[i * cells:(i + 1) * cells, :] = total
    me = me_ref[0]
    size = filtered.shape[0] // parts
    for k in range(parts):
        pieces[k][...] = filtered[pl.ds(pl.multiple_of((me ^ k) * size, 8), size), :]


def halo_kernel(parts, me_ref, above_ref, below_ref, *refs):
    outs = refs[parts:]
    me = me_ref[0]
    cells = above_ref.shape[0]
    for k in range(parts):
        outs[k][...] = refs[k][...]

        @pl.when((me ^ k) == 0)
        def _():
            outs[k][:cells, :] = outs[k][:cells, :] + above_ref[...]

        @pl.when((me ^ k) == parts - 1)
        def _():
            outs[k][-cells:, :] = outs[k][-cells:, :] + below_ref[...]


def block_order(parts):
    return [(a, b) for a in range(parts) for b in range(a, parts)] + [(a, parts) for a in range(parts)]


def gram_kernel(parts, span, me_ref, probes_ref, *refs):
    pieces, (send_ref, keep_ref, wide, flat) = refs[:parts], refs[parts:]
    me, owner = me_ref[0], me_ref[1]
    size, cols = pieces[0].shape
    for k in range(parts):
        wide[:, pl.ds(pl.multiple_of((me ^ k) * cols, cols), cols)] = pieces[k][...]
    where = {ab: j for j, ab in enumerate(block_order(parts))}
    for a in range(0, parts, 2):
        left = wide[:, a * cols:(a + 2) * cols]
        for b in range(a, parts + 2, 2):
            if b < parts:
                right = wide[:, b * cols:(b + 2) * cols]
            else:
                right = probes_ref[pl.ds(pl.multiple_of(me * size, 8), size), :]
            prod = exact_dot(left, right, ((0,), (0,)))
            for i in range(2):
                for j in range(right.shape[1] // cols):
                    if (a + i, b + j) in where:
                        at = where[a + i, b + j] * cols
                        flat[at:at + cols, :] = prod[i * cols:(i + 1) * cols, j * cols:(j + 1) * cols]
    share = flat.shape[0] // (parts * span)
    for k in range(parts * span):
        out = send_ref if k % 2 else keep_ref
        out[k // 2] = flat[pl.ds(pl.multiple_of((owner ^ k) * share, 8), share), :]


def split(x):
    high = x.astype(jnp.bfloat16)
    return high, (x - high.astype(F32)).astype(jnp.bfloat16)


def dot(a, b, dims):
    return lax.dot_general(a, b, (dims, ((), ())), preferred_element_type=F32)


def dot_parts(a, b, dims=((1,), (0,))):
    (ah, al), (bh, bl) = a, b
    rows = ah.shape[0]
    both = dot(jnp.concatenate([ah, al], axis=0), bh, dims)
    return both[:rows] + (dot(ah, bl, dims) + both[rows:])


def exact_dot(a, b, dims=((1,), (0,))):
    return lax.dot_general(a, b, (dims, ((), ())), precision=exact, preferred_element_type=F32)


def combine_of(grams):
    order = grams[0].shape[0]
    diagonal = lax.broadcasted_iota(jnp.int32, (order, order), 0) == lax.broadcasted_iota(jnp.int32, (order, order), 1)
    signs = []
    for gram in grams:
        mean = jnp.sum(jnp.where(diagonal, gram, 0.0)) / order
        shifted = jnp.where(diagonal, gram - mean, gram)
        signs.append(shifted / jnp.sqrt(jnp.sum(shifted * shifted, keepdims=True) + 1e-6))
    for _ in range(SIGN_STEPS):
        halves = [split(y) for y in signs]
        squares = [split(dot_parts(y, y)) for y in halves]
        cubes = [dot_parts(s, y) for y, s in zip(halves, squares)]
        signs = [1.5 * y - 0.5 * c for y, c in zip(signs, cubes)]
    half = order // 2
    combines = []
    for y in signs:
        projector = 0.5 * (jnp.where(diagonal, 1.0, 0.0) + y)
        combines.append(projector[:, :half] + projector[:, half:])
    return combines


def merge_kernel(parts, span, me_ref, even_ref, odd_ref, wide_ref, out_ref, coef_ref, flat, weight, turned):
    me, owner = me_ref[0], me_ref[1]
    size, cols = even_ref.shape[1:]
    for k in range(parts * span):
        source = odd_ref if k % 2 else even_ref
        flat[pl.ds(pl.multiple_of((owner ^ k) * size, 8), size), :] = source[k // 2]
    blocks = {ab: flat[j * cols:(j + 1) * cols, :] for j, ab in enumerate(block_order(parts))}
    weights, count = None, parts
    while count > 1:
        grams = []
        for p in range(0, count, 2):
            low = jnp.concatenate([blocks[p, p], blocks[p, p + 1]], axis=1)
            high = jnp.concatenate([blocks[p, p + 1].T, blocks[p + 1, p + 1]], axis=1)
            grams.append(jnp.concatenate([low, high], axis=0))
        combines = combine_of(grams)
        if weights is None:
            weights = combines
        else:
            per = len(weights) // len(combines)
            weights = [
                exact_dot(w, combines[i // per][(i % per) * cols:(i % per + 1) * cols, :])
                for i, w in enumerate(weights)
            ]
            weights = [jnp.concatenate(weights[i:i + per], axis=0) for i in range(0, len(weights), per)]
        merged = {}
        if count > 2:
            for p in range(count // 2):
                for q in range(p, count // 2):
                    if p == q:
                        cross = grams[p]
                    else:
                        cross = jnp.concatenate([
                            jnp.concatenate([blocks[2 * p + i, 2 * q], blocks[2 * p + i, 2 * q + 1]], axis=1)
                            for i in range(2)
                        ], axis=0)
                    right = exact_dot(cross, combines[q])
                    merged[p, q] = exact_dot(combines[p], right, ((0,), (0,)))
        blocks, count = merged, count // 2
    weight[...] = weights[0]
    total = dot_parts(split(wide_ref[...]), split(weight[...]))
    width = cols // parts
    turned_basis = total.T
    for d in range(parts):
        out_ref[d] = turned_basis[d * width:(d + 1) * width, :]
    turned[...] = exact_dot(weight[...], flat[-parts * cols:, :], ((0,), (0,)))
    coef_ref[...] = turned[pl.ds(pl.multiple_of(me * width, 8), width), :]


def final_kernel(pieces_ref, basis_ref):
    parts = pieces_ref.shape[0]
    per, cells = basis_ref.shape[0] // parts, basis_ref.shape[2]
    for t in range(parts):
        for i in range(per):
            basis_ref[t * per + i] = pieces_ref[t, :, i * cells:(i + 1) * cells]


def shape(*dims):
    return jax.ShapeDtypeStruct(dims, F32)


def local(snapshots, land_mask, taps_rows, taps_cols, probes):
    rows, grid_cols, cols = snapshots.shape
    half_rows, half_cols = rows // 2, grid_cols // 2
    parts, patches = lax.axis_size("tm"), lax.axis_size("space")
    cells = half_rows * half_cols
    piece = cells // parts
    span = 2 if patches > 1 else 1
    position, patch = lax.axis_index("tm"), lax.axis_index("space")
    me = jnp.stack([position, position + parts * (patch % span)]).astype(jnp.int32)

    snapshots, land_mask, taps_rows, taps_cols = (
        pltpu.with_memory_space_constraint(x, pltpu.HBM) for x in (snapshots, land_mask, taps_rows, taps_cols)
    )

    row_block, mask_block = (2, grid_cols, cols), (CHUNK, grid_cols)
    to_above, to_below = pl.pallas_call(
        edge_kernel,
        out_shape=[shape(half_cols, cols)] * 2,
        grid=(1,),
        in_specs=[
            scalars(), scalars(),
            pl.BlockSpec(row_block, lambda i: (0, 0, 0)),
            pl.BlockSpec(row_block, lambda i: (rows // 2 - 1, 0, 0)),
            pl.BlockSpec(mask_block, lambda i: (0, 0)),
            pl.BlockSpec(mask_block, lambda i: (rows // CHUNK - 1, 0)),
        ],
        out_specs=[pl.BlockSpec((half_cols, cols), lambda i: (0, 0))] * 2,
        scratch_shapes=[pltpu.VMEM((grid_cols, CHUNK), F32)],
        compiler_params=params(),
        name="edge",
    )(taps_rows, taps_cols, snapshots, snapshots, land_mask, land_mask)
    up = [(i, i + 1) for i in range(patches - 1)]
    above = lax.ppermute(to_below, "space", up)
    below = lax.ppermute(to_above, "space", [(j, i) for i, j in up])

    pieces = pl.pallas_call(
        functools.partial(filter_kernel, parts),
        out_shape=[shape(piece, cols)] * parts,
        in_specs=[scalars(), scalars(), scalars(), pl.BlockSpec(memory_space=pltpu.HBM), whole()],
        out_specs=[whole()] * parts,
        scratch_shapes=[
            pltpu.VMEM((rows, grid_cols, cols), F32),
            pltpu.SemaphoreType.DMA((rows // CHUNK,)),
            pltpu.VMEM((grid_cols, CHUNK), F32),
            pltpu.VMEM((rows + 4, half_cols, cols), F32),
            pltpu.VMEM((cells, cols), F32),
        ],
        compiler_params=params(),
        cost_estimate=pl.CostEstimate(flops=0, bytes_accessed=4 * snapshots.size, transcendentals=0),
        name="filter",
    )(me, taps_rows, taps_cols, snapshots, land_mask)
    pieces = pl.pallas_call(
        functools.partial(halo_kernel, parts),
        out_shape=[shape(piece, cols)] * parts,
        in_specs=[scalars()] + [whole()] * (parts + 2),
        out_specs=[whole()] * parts,
        input_output_aliases={3 + k: k for k in range(parts)},
        compiler_params=params(),
        name="halo",
    )(me, above, below, *pieces)
    far = [pieces[0]] + [swap(pieces[k], "tm", k) for k in range(1, parts)]

    blocks = len(block_order(parts))
    owners = parts * span
    size = blocks * cols // owners
    send, keep, wide = pl.pallas_call(
        functools.partial(gram_kernel, parts, span),
        out_shape=[shape(owners // 2, size, cols)] * 2 + [shape(piece, parts * cols)],
        in_specs=[scalars()] + [whole()] * (parts + 1),
        out_specs=[whole()] * 3,
        scratch_shapes=[pltpu.VMEM((blocks * cols, cols), F32)],
        compiler_params=params(),
        name="gram",
    )(me, probes.reshape(cells, cols), *far)
    got = swap(send, "tm", 1)
    mine = keep[0] + got[0]
    for h in range(1, owners // 2):
        mine = mine + swap_both(keep[h] + got[h], 2 * h)
    bits = [1 << b for b in range(1, patches.bit_length() - 1)]
    for bit in bits:
        mine = mine + swap(mine, "space", bit)
    even = jnp.stack([mine] + [swap_both(mine, 2 * h) for h in range(1, owners // 2)])
    odd = swap(even, "tm", 1)

    width = cols // parts
    sent, coefficients = pl.pallas_call(
        functools.partial(merge_kernel, parts, span),
        out_shape=[shape(parts, width, piece), shape(width, cols)],
        in_specs=[scalars()] + [whole()] * 3,
        out_specs=[whole()] * 2,
        scratch_shapes=[
            pltpu.VMEM((blocks * cols, cols), F32),
            pltpu.VMEM((parts * cols, cols), F32),
            pltpu.VMEM((cols, cols), F32),
        ],
        compiler_params=params(),
        name="merge",
    )(me, even, odd, wide)
    last = lax.all_to_all(sent, "tm", 0, 0)

    basis = pl.pallas_call(
        final_kernel,
        out_shape=shape(half_rows, width, half_cols),
        in_specs=[whole()],
        out_specs=whole(),
        compiler_params=params(),
        name="final",
    )(last)
    return basis.transpose(0, 2, 1), coefficients


def solution(mesh):
    placed = (P("space", None, "tm"), P("space", None), P(), P(), P("space", None, None))
    return jax.shard_map(
        local,
        mesh=mesh,
        in_specs=placed,
        out_specs=(P("space", None, "tm"), P("tm", None)),
        check_vma=False,
    )
```

```python
import functools

import jax
import jax.numpy as jnp
from jax import lax
from jax.experimental import pallas as pl
from jax.experimental.pallas import tpu as pltpu
from jax.sharding import PartitionSpec as P

SIGN_STEPS = 8
TAPS = 6
CHUNK = 8
exact = lax.Precision.HIGHEST
F32 = jnp.float32
VMEM_LIMIT = 48 * 1024 * 1024


def params():
    return pltpu.CompilerParams(vmem_limit_bytes=VMEM_LIMIT)


def whole():
    return pl.BlockSpec(memory_space=pltpu.VMEM)


def scalars():
    return pl.BlockSpec(memory_space=pltpu.SMEM)


def swap(x, axis, mask):
    count = lax.axis_size(axis)
    return lax.ppermute(x, axis, [(i, i ^ mask) for i in range(count)])


def swap_both(x, mask):
    parts, patches = lax.axis_size("tm"), lax.axis_size("space")
    route = []
    for t in range(parts):
        for s in range(patches):
            there = (t ^ (mask % parts)) * patches + (s ^ (mask // parts))
            route.append((t * patches + s, there))
    return lax.ppermute(x, ("tm", "space"), route)


def shift_rows(x, by):
    edge = jnp.zeros((1, x.shape[1]), x.dtype)
    if by > 0:
        return jnp.concatenate([edge, x[:-1]], axis=0)
    return jnp.concatenate([x[1:], edge], axis=0)


def mask_columns(mask, mask_t):
    mask_t[...] = mask.astype(F32).T
    return mask_t[...]


def narrowed_row(held, taps):
    half = held.shape[0] // 2
    even = held[pl.ds(0, half, stride=2), :]
    odd = held[pl.ds(1, half, stride=2), :]
    before = taps[0] * even + taps[1] * odd
    here = taps[2] * even + taps[3] * odd
    after = taps[4] * even + taps[5] * odd
    return shift_rows(before, 1) + here + shift_rows(after, -1)


def edge_kernel(rtaps_ref, ctaps_ref, first_ref, last_ref, mask_first_ref, mask_last_ref, up_ref, down_ref, mask_t, held):
    ctaps = [ctaps_ref[k] for k in range(TAPS)]
    for out, snaps, mask_ref, taps, at in (
        (up_ref, first_ref, mask_first_ref, (rtaps_ref[4], rtaps_ref[5]), 0),
        (down_ref, last_ref, mask_last_ref, (rtaps_ref[0], rtaps_ref[1]), CHUNK - 2),
    ):
        mask = mask_columns(mask_ref[...], mask_t)
        held[...] = taps[0] * (snaps[0] * mask[:, at:at + 1]) + taps[1] * (snaps[1] * mask[:, at + 1:at + 2])
        out[...] = narrowed_row(held, ctaps)


def filter_kernel(parts, other, me_ref, rtaps_ref, ctaps_ref, snap_hbm, mask_ref, *rest):
    count = parts // 2
    pieces, (ocean, sems, mask_t, held, filtered) = rest[:count], rest[count:]
    rows, grid_cols = ocean.shape[0] - 4, ocean.shape[1]
    cells = grid_cols // 2
    me = me_ref[0]
    side = me // count
    if other:
        side = 1 - side
    chunks = (rows // 2 + 2 + CHUNK - 1) // CHUNK
    start = side * (rows - chunks * CHUNK)

    def fetch(c):
        at = pl.multiple_of(start + c * CHUNK, CHUNK)
        return pltpu.make_async_copy(snap_hbm.at[pl.ds(at, CHUNK)], ocean.at[pl.ds(at + 2, CHUNK)], sems.at[c])

    for c in range(chunks):
        fetch(c).start()
    rtaps = [rtaps_ref[k] for k in range(TAPS)]
    ctaps = [ctaps_ref[k] for k in range(TAPS)]
    edge = jnp.zeros((2,) + ocean.shape[1:], F32)
    ocean[0:2] = edge
    ocean[rows + 2:rows + 4] = edge

    def mask_chunk(c, carry):
        fetch(c).wait()
        base = pl.multiple_of(start + c * CHUNK, CHUNK)
        mask = mask_columns(mask_ref[pl.ds(base, CHUNK), :], mask_t)
        for x in range(CHUNK):
            ocean[base + 2 + x] = ocean[base + 2 + x] * mask[:, x:x + 1]
        return carry

    lax.fori_loop(0, chunks, mask_chunk, 0)
    first = side * (rows // 2)
    for i in range(rows // 4):
        total = rtaps[0] * ocean[first + 2 * i]
        for k in range(1, TAPS):
            total = total + rtaps[k] * ocean[first + 2 * i + k]
        held[i % 2] = total
        filtered[i * cells:(i + 1) * cells, :] = narrowed_row(held.at[i % 2], ctaps)
    size = filtered.shape[0] // count
    for k in range(count):
        at = ((me ^ k) % count) * size
        pieces[k][...] = filtered[pl.ds(pl.multiple_of(at, 8), size), :]


def halo_kernel(parts, offset, me_ref, above_ref, below_ref, *refs):
    outs = refs[len(refs) // 2:]
    me = me_ref[0]
    cells = above_ref.shape[0]
    for k, out in enumerate(outs):
        out[...] = refs[k][...]

        @pl.when((me ^ (k + offset)) == 0)
        def _():
            out[:cells, :] = out[:cells, :] + above_ref[...]

        @pl.when((me ^ (k + offset)) == parts - 1)
        def _():
            out[-cells:, :] = out[-cells:, :] + below_ref[...]


def block_order(parts):
    return [(a, b) for a in range(parts) for b in range(a, parts)] + [(a, parts) for a in range(parts)]


def gram_kernel(parts, span, me_ref, probes_ref, *refs):
    pieces, (send_ref, keep_ref, wide, flat) = refs[:parts], refs[parts:]
    me, owner = me_ref[0], me_ref[1]
    size, cols = pieces[0].shape
    for k in range(parts):
        wide[:, pl.ds(pl.multiple_of((me ^ k) * cols, cols), cols)] = pieces[k][...]
    where = {ab: j for j, ab in enumerate(block_order(parts))}
    sides = [split(wide[:, a * cols:(a + 2) * cols]) for a in range(0, parts, 2)]
    sides.append(split(probes_ref[pl.ds(pl.multiple_of(me * size, 8), size), :]))
    for a in range(0, parts, 2):
        for b in range(a, parts + 2, 2):
            right = sides[b // 2]
            prod = dot_parts(sides[a // 2], right, ((0,), (0,)))
            for i in range(2):
                for j in range(right[0].shape[1] // cols):
                    if (a + i, b + j) in where:
                        at = where[a + i, b + j] * cols
                        flat[at:at + cols, :] = prod[i * cols:(i + 1) * cols, j * cols:(j + 1) * cols]
    share = flat.shape[0] // (parts * span)
    for k in range(parts * span):
        out = send_ref if k % 2 else keep_ref
        out[k // 2] = flat[pl.ds(pl.multiple_of((owner ^ k) * share, 8), share), :]


def split(x):
    high = x.astype(jnp.bfloat16)
    return high, (x - high.astype(F32)).astype(jnp.bfloat16)


def dot(a, b, dims):
    return lax.dot_general(a, b, (dims, ((), ())), preferred_element_type=F32)


def dot_parts(a, b, dims=((1,), (0,))):
    (ah, al), (bh, bl) = a, b
    free = 1 - dims[0][0]
    rows = ah.shape[free]
    both = dot(jnp.concatenate([ah, al], axis=free), bh, dims)
    return both[:rows] + (dot(ah, bl, dims) + both[rows:])


def exact_dot(a, b, dims=((1,), (0,))):
    return lax.dot_general(a, b, (dims, ((), ())), precision=exact, preferred_element_type=F32)


def combine_of(grams):
    order = grams[0].shape[0]
    diagonal = lax.broadcasted_iota(jnp.int32, (order, order), 0) == lax.broadcasted_iota(jnp.int32, (order, order), 1)
    signs = []
    for gram in grams:
        mean = jnp.sum(jnp.where(diagonal, gram, 0.0)) / order
        shifted = jnp.where(diagonal, gram - mean, gram)
        signs.append(shifted / jnp.sqrt(jnp.sum(shifted * shifted, keepdims=True) + 1e-6))
    for _ in range(SIGN_STEPS):
        halves = [split(y) for y in signs]
        squares = [split(dot_parts(y, y)) for y in halves]
        cubes = [dot_parts(s, y) for y, s in zip(halves, squares)]
        signs = [1.5 * y - 0.5 * c for y, c in zip(signs, cubes)]
    half = order // 2
    combines = []
    for y in signs:
        projector = 0.5 * (jnp.where(diagonal, 1.0, 0.0) + y)
        combines.append(projector[:, :half] + projector[:, half:])
    return combines


def merge_kernel(parts, span, me_ref, even_ref, odd_ref, wide_ref, *refs):
    outs, (coef_ref, flat, weight, turned) = refs[:parts], refs[parts:]
    me, owner = me_ref[0], me_ref[1]
    size, cols = even_ref.shape[1:]
    for k in range(parts * span):
        source = odd_ref if k % 2 else even_ref
        flat[pl.ds(pl.multiple_of((owner ^ k) * size, 8), size), :] = source[k // 2]
    blocks = {ab: flat[j * cols:(j + 1) * cols, :] for j, ab in enumerate(block_order(parts))}
    weights, count = None, parts
    while count > 1:
        grams = []
        for p in range(0, count, 2):
            low = jnp.concatenate([blocks[p, p], blocks[p, p + 1]], axis=1)
            high = jnp.concatenate([blocks[p, p + 1].T, blocks[p + 1, p + 1]], axis=1)
            grams.append(jnp.concatenate([low, high], axis=0))
        combines = combine_of(grams)
        if weights is None:
            weights = combines
        else:
            per = len(weights) // len(combines)
            weights = [
                exact_dot(w, combines[i // per][(i % per) * cols:(i % per + 1) * cols, :])
                for i, w in enumerate(weights)
            ]
            weights = [jnp.concatenate(weights[i:i + per], axis=0) for i in range(0, len(weights), per)]
        merged = {}
        if count > 2:
            for p in range(count // 2):
                for q in range(p, count // 2):
                    if p == q:
                        cross = grams[p]
                    else:
                        cross = jnp.concatenate([
                            jnp.concatenate([blocks[2 * p + i, 2 * q], blocks[2 * p + i, 2 * q + 1]], axis=1)
                            for i in range(2)
                        ], axis=0)
                    right = exact_dot(cross, combines[q])
                    merged[p, q] = exact_dot(combines[p], right, ((0,), (0,)))
        blocks, count = merged, count // 2
    weight[...] = weights[0]
    total = dot_parts(split(wide_ref[...]), split(weight[...]))
    width = cols // parts
    rows = total.shape[0]
    turned[:, :rows] = total.T
    turned[:, rows:] = exact_dot(weight[...], flat[-parts * cols:, :], ((0,), (0,)))
    for k in range(parts):
        outs[k][...] = turned[pl.ds(pl.multiple_of((me ^ k) * width, 8), width), :rows]
    coef_ref[...] = turned[pl.ds(pl.multiple_of(me * width, 8), width), rows:]


def final_kernel(parts, me_ref, *refs):
    pieces, basis_ref = refs[:parts], refs[parts]
    me = me_ref[0]
    per, cells = basis_ref.shape[0] // parts, basis_ref.shape[2]
    for k in range(parts):
        base = (me ^ k) * per
        for i in range(per):
            basis_ref[base + i] = pieces[k][:, i * cells:(i + 1) * cells]


def shape(*dims):
    return jax.ShapeDtypeStruct(dims, F32)


def local(snapshots, land_mask, taps_rows, taps_cols, probes):
    rows, grid_cols, cols = snapshots.shape
    half_rows, half_cols = rows // 2, grid_cols // 2
    parts, patches = lax.axis_size("tm"), lax.axis_size("space")
    cells = half_rows * half_cols
    piece = cells // parts
    span = 2 if patches > 1 else 1
    position, patch = lax.axis_index("tm"), lax.axis_index("space")
    me = jnp.stack([position, position + parts * (patch % span)]).astype(jnp.int32)

    snapshots, land_mask, taps_rows, taps_cols = (
        pltpu.with_memory_space_constraint(x, pltpu.HBM) for x in (snapshots, land_mask, taps_rows, taps_cols)
    )

    row_block, mask_block = (2, grid_cols, cols), (CHUNK, grid_cols)
    to_above, to_below = pl.pallas_call(
        edge_kernel,
        out_shape=[shape(half_cols, cols)] * 2,
        grid=(1,),
        in_specs=[
            scalars(), scalars(),
            pl.BlockSpec(row_block, lambda i: (0, 0, 0)),
            pl.BlockSpec(row_block, lambda i: (rows // 2 - 1, 0, 0)),
            pl.BlockSpec(mask_block, lambda i: (0, 0)),
            pl.BlockSpec(mask_block, lambda i: (rows // CHUNK - 1, 0)),
        ],
        out_specs=[pl.BlockSpec((half_cols, cols), lambda i: (0, 0))] * 2,
        scratch_shapes=[pltpu.VMEM((grid_cols, CHUNK), F32), pltpu.VMEM((grid_cols, cols), F32)],
        compiler_params=params(),
        name="edge",
    )(taps_rows, taps_cols, snapshots, snapshots, land_mask, land_mask)
    up = [(i, i + 1) for i in range(patches - 1)]
    above = lax.ppermute(to_below, "space", up)
    below = lax.ppermute(to_above, "space", [(j, i) for i, j in up])

    count = parts // 2
    chunks = (rows // 2 + 2 + CHUNK - 1) // CHUNK

    def half_of_rows(other, after):
        halves = pl.pallas_call(
            functools.partial(filter_kernel, parts, other),
            out_shape=[shape(piece, cols)] * count,
            in_specs=[scalars(), scalars(), scalars(), pl.BlockSpec(memory_space=pltpu.HBM), whole()],
            out_specs=[whole()] * count,
            scratch_shapes=[
                pltpu.VMEM((rows + 4, grid_cols, cols), F32),
                pltpu.SemaphoreType.DMA((chunks,)),
                pltpu.VMEM((grid_cols, CHUNK), F32),
                pltpu.VMEM((2, grid_cols, cols), F32),
                pltpu.VMEM((cells // 2, cols), F32),
            ],
            compiler_params=params(),
            cost_estimate=pl.CostEstimate(flops=0, bytes_accessed=4 * snapshots.size, transcendentals=0),
            name="filter",
        )(after, taps_rows, taps_cols, snapshots, land_mask)
        return pl.pallas_call(
            functools.partial(halo_kernel, parts, count if other else 0),
            out_shape=[shape(piece, cols)] * count,
            in_specs=[scalars()] + [whole()] * (count + 2),
            out_specs=[whole()] * count,
            input_output_aliases={3 + k: k for k in range(count)},
            compiler_params=params(),
            name="halo",
        )(me, above, below, *halves)

    leaving = half_of_rows(True, me)
    far = [swap(leaving[k], "tm", k + count) for k in range(count)]
    after, *leaving = lax.optimization_barrier([me] + list(leaving))
    staying = half_of_rows(False, after)
    far = [staying[0]] + [swap(staying[k], "tm", k) for k in range(1, count)] + far

    blocks = len(block_order(parts))
    owners = parts * span
    size = blocks * cols // owners
    send, keep, wide = pl.pallas_call(
        functools.partial(gram_kernel, parts, span),
        out_shape=[shape(owners // 2, size, cols)] * 2 + [shape(piece, parts * cols)],
        in_specs=[scalars()] + [whole()] * (parts + 1),
        out_specs=[whole()] * 3,
        scratch_shapes=[pltpu.VMEM((blocks * cols, cols), F32)],
        compiler_params=params(),
        name="gram",
    )(me, probes.reshape(cells, cols), *far)
    got = swap(send, "tm", 1)
    mine = keep[0] + got[0]
    for h in range(1, owners // 2):
        mine = mine + swap_both(keep[h] + got[h], 2 * h)
    bits = [1 << b for b in range(1, patches.bit_length() - 1)]
    for bit in bits:
        mine = mine + swap(mine, "space", bit)
    even = jnp.stack([mine] + [swap_both(mine, 2 * h) for h in range(1, owners // 2)])
    odd = swap(even, "tm", 1)

    width = cols // parts
    *sent, coefficients = pl.pallas_call(
        functools.partial(merge_kernel, parts, span),
        out_shape=[shape(width, piece)] * parts + [shape(width, cols)],
        in_specs=[scalars()] + [whole()] * 3,
        out_specs=[whole()] * (parts + 1),
        scratch_shapes=[
            pltpu.VMEM((blocks * cols, cols), F32),
            pltpu.VMEM((parts * cols, cols), F32),
            pltpu.VMEM((cols, piece + cols), F32),
        ],
        compiler_params=params(),
        name="merge",
    )(me, even, odd, wide)
    last = [sent[0]] + [swap(sent[k], "tm", k) for k in range(1, parts)]

    basis = pl.pallas_call(
        functools.partial(final_kernel, parts),
        out_shape=shape(half_rows, width, half_cols),
        in_specs=[scalars()] + [whole()] * parts,
        out_specs=whole(),
        compiler_params=params(),
        name="final",
    )(me, *last)
    return basis.transpose(0, 2, 1), coefficients


def solution(mesh):
    placed = (P("space", None, "tm"), P("space", None), P(), P(), P("space", None, None))
    return jax.shard_map(
        local,
        mesh=mesh,
        in_specs=placed,
        out_specs=(P("space", None, "tm"), P("tm", None)),
        check_vma=False,
    )
```

```python
import functools

import jax
import jax.numpy as jnp
from jax import lax
from jax.experimental import pallas as pl
from jax.experimental.pallas import tpu as pltpu
from jax.sharding import PartitionSpec as P

SIGN_STEPS = 8
TAPS = 6
CHUNK = 8
ROW_BLOCKS = 2
F32 = jnp.float32
VMEM_LIMIT = 48 * 1024 * 1024


def params():
    return pltpu.CompilerParams(vmem_limit_bytes=VMEM_LIMIT)


def whole():
    return pl.BlockSpec(memory_space=pltpu.VMEM)


def scalars():
    return pl.BlockSpec(memory_space=pltpu.SMEM)


def swap(x, axis, mask):
    count = lax.axis_size(axis)
    return lax.ppermute(x, axis, [(i, i ^ mask) for i in range(count)])


def swap_both(x, mask):
    parts, patches = lax.axis_size("tm"), lax.axis_size("space")
    route = []
    for t in range(parts):
        for s in range(patches):
            there = (t ^ (mask % parts)) * patches + (s ^ (mask // parts))
            route.append((t * patches + s, there))
    return lax.ppermute(x, ("tm", "space"), route)


def shift_rows(x, by):
    edge = jnp.zeros((1, x.shape[1]), x.dtype)
    if by > 0:
        return jnp.concatenate([edge, x[:-1]], axis=0)
    return jnp.concatenate([x[1:], edge], axis=0)


def mask_columns(mask, mask_t):
    mask_t[...] = mask.astype(F32).T
    half = mask.shape[1] // 2
    return mask_t[pl.ds(0, half, stride=2), :], mask_t[pl.ds(1, half, stride=2), :]


def narrowed_row(snaps, x, mask, taps):
    half = snaps.shape[1] // 2
    even = snaps[x, pl.ds(0, half, stride=2), :] * mask[0]
    odd = snaps[x, pl.ds(1, half, stride=2), :] * mask[1]
    before = taps[0] * even + taps[1] * odd
    here = taps[2] * even + taps[3] * odd
    after = taps[4] * even + taps[5] * odd
    return shift_rows(before, 1) + here + shift_rows(after, -1)


def edge_kernel(rtaps_ref, ctaps_ref, first_ref, last_ref, mask_first_ref, mask_last_ref, up_ref, down_ref, mask_t):
    ctaps = [ctaps_ref[k] for k in range(TAPS)]
    for out, snaps, mask_ref, taps, at in (
        (up_ref, first_ref, mask_first_ref, (rtaps_ref[4], rtaps_ref[5]), 0),
        (down_ref, last_ref, mask_last_ref, (rtaps_ref[0], rtaps_ref[1]), CHUNK - 2),
    ):
        masks = mask_columns(mask_ref[...], mask_t)
        rows = [narrowed_row(snaps, x, [m[:, at + x:at + x + 1] for m in masks], ctaps) for x in range(2)]
        out[...] = taps[0] * rows[0] + taps[1] * rows[1]


def filter_kernel(parts, other, me_ref, rtaps_ref, ctaps_ref, snaps, mask_ref, *rest):
    count = parts // 2
    pieces, (mask_t, narrowed, filtered) = rest[:count], rest[count:]
    rows, cells = narrowed.shape[0] - 4, narrowed.shape[1]
    me = me_ref[0]
    side = me // count
    if other:
        side = 1 - side
    chunks = (rows // 2 + 2 + CHUNK - 1) // CHUNK
    start = side * (rows - chunks * CHUNK)

    rtaps = [rtaps_ref[k] for k in range(TAPS)]
    ctaps = [ctaps_ref[k] for k in range(TAPS)]
    edge = jnp.zeros((2,) + narrowed.shape[1:], F32)
    narrowed[0:2] = edge
    narrowed[rows + 2:rows + 4] = edge

    def narrow(c, carry):
        base = pl.multiple_of(start + c * CHUNK, CHUNK)
        masks = mask_columns(mask_ref[pl.ds(base, CHUNK), :], mask_t)
        for x in range(CHUNK):
            row = narrowed_row(snaps, base + x, [m[:, x:x + 1] for m in masks], ctaps)
            narrowed[base + 2 + x] = row
        return carry

    lax.fori_loop(0, chunks, narrow, 0)
    first = side * (rows // 2)
    for i in range(rows // 4):
        total = rtaps[0] * narrowed[first + 2 * i]
        for k in range(1, TAPS):
            total = total + rtaps[k] * narrowed[first + 2 * i + k]
        filtered[i * cells:(i + 1) * cells, :] = total
    size = filtered.shape[0] // count
    for k in range(count):
        at = ((me ^ k) % count) * size
        pieces[k][...] = filtered[pl.ds(pl.multiple_of(at, 8), size), :]


def halo_kernel(parts, offset, me_ref, above_ref, below_ref, *refs):
    outs = refs[len(refs) // 2:]
    me = me_ref[0]
    cells = above_ref.shape[0]
    for k, out in enumerate(outs):
        out[...] = refs[k][...]

        @pl.when((me ^ (k + offset)) == 0)
        def _():
            out[:cells, :] = out[:cells, :] + above_ref[...]

        @pl.when((me ^ (k + offset)) == parts - 1)
        def _():
            out[-cells:, :] = out[-cells:, :] + below_ref[...]


def block_order(parts):
    return [(a, b) for a in range(parts) for b in range(a, parts)] + [(a, parts) for a in range(parts)]


def gram_kernel(parts, span, me_ref, probes_ref, *refs):
    pieces, (send_ref, keep_ref, wide, flat) = refs[:parts], refs[parts:]
    me, owner = me_ref[0], me_ref[1]
    size, cols = pieces[0].shape
    for k in range(parts):
        wide[:, pl.ds(pl.multiple_of((me ^ k) * cols, cols), cols)] = pieces[k][...]
    where = {ab: j for j, ab in enumerate(block_order(parts))}
    sides = [split(wide[:, a * cols:(a + 2) * cols]) for a in range(0, parts, 2)]
    sides.append(split(probes_ref[pl.ds(pl.multiple_of(me * size, 8), size), :]))
    for a in range(0, parts, 2):
        for b in range(a, parts + 2, 2):
            right = sides[b // 2]
            prod = dot_parts(sides[a // 2], right, ((0,), (0,)))
            for i in range(2):
                for j in range(right[0].shape[1] // cols):
                    if (a + i, b + j) in where:
                        at = where[a + i, b + j] * cols
                        flat[at:at + cols, :] = prod[i * cols:(i + 1) * cols, j * cols:(j + 1) * cols]
    share = flat.shape[0] // (parts * span)
    for k in range(parts * span):
        out = send_ref if k % 2 else keep_ref
        out[k // 2] = flat[pl.ds(pl.multiple_of((owner ^ k) * share, 8), share), :]


def split(x):
    high = x.astype(jnp.bfloat16)
    return high, (x - high.astype(F32)).astype(jnp.bfloat16)


def dot(a, b, dims):
    return lax.dot_general(a, b, (dims, ((), ())), preferred_element_type=F32)


def dot_parts(a, b, dims=((1,), (0,))):
    (ah, al), (bh, bl) = a, b
    free = 1 - dims[0][0]
    rows = ah.shape[free]
    both = dot(jnp.concatenate([ah, al], axis=free), bh, dims)
    return both[:rows] + (dot(ah, bl, dims) + both[rows:])


def split_dot(a, b, dims=((1,), (0,))):
    return dot_parts(split(a), split(b), dims)


def next_sign(y):
    whole_y = split(y)
    size = y.shape[0] // ROW_BLOCKS
    blocks = []
    for at in range(0, y.shape[0], size):
        square = dot_parts([part[at:at + size] for part in whole_y], whole_y)
        blocks.append(1.5 * y[at:at + size] - 0.5 * dot_parts(split(square), whole_y))
    return jnp.concatenate(blocks, axis=0)


def combine_of(grams):
    order = grams[0].shape[0]
    diagonal = lax.broadcasted_iota(jnp.int32, (order, order), 0) == lax.broadcasted_iota(jnp.int32, (order, order), 1)
    signs = []
    for gram in grams:
        mean = jnp.sum(jnp.where(diagonal, gram, 0.0)) / order
        shifted = jnp.where(diagonal, gram - mean, gram)
        signs.append(shifted / jnp.sqrt(jnp.sum(shifted * shifted, keepdims=True) + 1e-6))
    for _ in range(SIGN_STEPS):
        signs = [next_sign(y) for y in signs]
    half = order // 2
    combines = []
    for y in signs:
        projector = 0.5 * (jnp.where(diagonal, 1.0, 0.0) + y)
        combines.append(projector[:, :half] + projector[:, half:])
    return combines


def merge_kernel(parts, span, me_ref, even_ref, odd_ref, wide_ref, *refs):
    outs, (coef_ref, flat, weight, turned) = refs[:parts], refs[parts:]
    me, owner = me_ref[0], me_ref[1]
    size, cols = even_ref.shape[1:]
    for k in range(parts * span):
        source = odd_ref if k % 2 else even_ref
        flat[pl.ds(pl.multiple_of((owner ^ k) * size, 8), size), :] = source[k // 2]
    blocks = {ab: flat[j * cols:(j + 1) * cols, :] for j, ab in enumerate(block_order(parts))}
    weights, count = None, parts
    while count > 1:
        grams = []
        for p in range(0, count, 2):
            low = jnp.concatenate([blocks[p, p], blocks[p, p + 1]], axis=1)
            high = jnp.concatenate([blocks[p, p + 1].T, blocks[p + 1, p + 1]], axis=1)
            grams.append(jnp.concatenate([low, high], axis=0))
        combines = combine_of(grams)
        if weights is None:
            weights = combines
        else:
            per = len(weights) // len(combines)
            weights = [
                split_dot(w, combines[i // per][(i % per) * cols:(i % per + 1) * cols, :])
                for i, w in enumerate(weights)
            ]
            weights = [jnp.concatenate(weights[i:i + per], axis=0) for i in range(0, len(weights), per)]
        merged = {}
        if count > 2:
            for p in range(count // 2):
                for q in range(p, count // 2):
                    if p == q:
                        cross = grams[p]
                    else:
                        cross = jnp.concatenate([
                            jnp.concatenate([blocks[2 * p + i, 2 * q], blocks[2 * p + i, 2 * q + 1]], axis=1)
                            for i in range(2)
                        ], axis=0)
                    right = split_dot(cross, combines[q])
                    merged[p, q] = split_dot(combines[p], right, ((0,), (0,)))
        blocks, count = merged, count // 2
    weight[...] = weights[0]
    total = dot_parts(split(wide_ref[...]), split(weight[...]))
    width = cols // parts
    rows = total.shape[0]
    turned[:, :rows] = total.T
    turned[:, rows:] = split_dot(weight[...], flat[-parts * cols:, :], ((0,), (0,)))
    for k in range(parts):
        outs[k][...] = turned[pl.ds(pl.multiple_of((me ^ k) * width, 8), width), :rows]
    coef_ref[...] = turned[pl.ds(pl.multiple_of(me * width, 8), width), rows:]


def final_kernel(parts, me_ref, *refs):
    pieces, basis_ref = refs[:parts], refs[parts]
    me = me_ref[0]
    per, cells = basis_ref.shape[0] // parts, basis_ref.shape[2]
    for k in range(parts):
        base = (me ^ k) * per
        for i in range(per):
            basis_ref[base + i] = pieces[k][:, i * cells:(i + 1) * cells]


def shape(*dims):
    return jax.ShapeDtypeStruct(dims, F32)


def local(snapshots, land_mask, taps_rows, taps_cols, probes):
    rows, grid_cols, cols = snapshots.shape
    half_rows, half_cols = rows // 2, grid_cols // 2
    parts, patches = lax.axis_size("tm"), lax.axis_size("space")
    cells = half_rows * half_cols
    piece = cells // parts
    span = 2 if patches > 1 else 1
    position, patch = lax.axis_index("tm"), lax.axis_index("space")
    me = jnp.stack([position, position + parts * (patch % span)]).astype(jnp.int32)

    held = snapshots
    snapshots, land_mask, taps_rows, taps_cols = (
        pltpu.with_memory_space_constraint(x, pltpu.HBM) for x in (snapshots, land_mask, taps_rows, taps_cols)
    )

    row_block, mask_block = (2, grid_cols, cols), (CHUNK, grid_cols)
    to_above, to_below = pl.pallas_call(
        edge_kernel,
        out_shape=[shape(half_cols, cols)] * 2,
        grid=(1,),
        in_specs=[
            scalars(), scalars(),
            pl.BlockSpec(row_block, lambda i: (0, 0, 0)),
            pl.BlockSpec(row_block, lambda i: (rows // 2 - 1, 0, 0)),
            pl.BlockSpec(mask_block, lambda i: (0, 0)),
            pl.BlockSpec(mask_block, lambda i: (rows // CHUNK - 1, 0)),
        ],
        out_specs=[pl.BlockSpec((half_cols, cols), lambda i: (0, 0))] * 2,
        scratch_shapes=[pltpu.VMEM((grid_cols, CHUNK), F32)],
        compiler_params=params(),
        name="edge",
    )(taps_rows, taps_cols, snapshots, snapshots, land_mask, land_mask)
    up = [(i, i + 1) for i in range(patches - 1)]
    above = lax.ppermute(to_below, "space", up)
    below = lax.ppermute(to_above, "space", [(j, i) for i, j in up])

    count = parts // 2

    def half_of_rows(other, after):
        halves = pl.pallas_call(
            functools.partial(filter_kernel, parts, other),
            out_shape=[shape(piece, cols)] * count,
            in_specs=[scalars(), scalars(), scalars(), whole(), whole()],
            out_specs=[whole()] * count,
            scratch_shapes=[
                pltpu.VMEM((grid_cols, CHUNK), F32),
                pltpu.VMEM((rows + 4, half_cols, cols), F32),
                pltpu.VMEM((cells // 2, cols), F32),
            ],
            compiler_params=params(),
            cost_estimate=pl.CostEstimate(flops=0, bytes_accessed=4 * snapshots.size, transcendentals=0),
            name="filter",
        )(after, taps_rows, taps_cols, held, land_mask)
        return pl.pallas_call(
            functools.partial(halo_kernel, parts, count if other else 0),
            out_shape=[shape(piece, cols)] * count,
            in_specs=[scalars()] + [whole()] * (count + 2),
            out_specs=[whole()] * count,
            input_output_aliases={3 + k: k for k in range(count)},
            compiler_params=params(),
            name="halo",
        )(me, above, below, *halves)

    leaving = half_of_rows(True, me)
    far = [swap(leaving[k], "tm", k + count) for k in range(count)]
    after, *leaving = lax.optimization_barrier([me] + list(leaving))
    staying = half_of_rows(False, after)
    far = [staying[0]] + [swap(staying[k], "tm", k) for k in range(1, count)] + far

    blocks = len(block_order(parts))
    owners = parts * span
    size = blocks * cols // owners
    send, keep, wide = pl.pallas_call(
        functools.partial(gram_kernel, parts, span),
        out_shape=[shape(owners // 2, size, cols)] * 2 + [shape(piece, parts * cols)],
        in_specs=[scalars()] + [whole()] * (parts + 1),
        out_specs=[whole()] * 3,
        scratch_shapes=[pltpu.VMEM((blocks * cols, cols), F32)],
        compiler_params=params(),
        name="gram",
    )(me, probes.reshape(cells, cols), *far)
    got = swap(send, "tm", 1)
    mine = keep[0] + got[0]
    for h in range(1, owners // 2):
        mine = mine + swap_both(keep[h] + got[h], 2 * h)
    bits = [1 << b for b in range(1, patches.bit_length() - 1)]
    for bit in bits:
        mine = mine + swap(mine, "space", bit)
    even = jnp.stack([mine] + [swap_both(mine, 2 * h) for h in range(1, owners // 2)])
    odd = swap(even, "tm", 1)

    width = cols // parts
    *sent, coefficients = pl.pallas_call(
        functools.partial(merge_kernel, parts, span),
        out_shape=[shape(width, piece)] * parts + [shape(width, cols)],
        in_specs=[scalars()] + [whole()] * 3,
        out_specs=[whole()] * (parts + 1),
        scratch_shapes=[
            pltpu.VMEM((blocks * cols, cols), F32),
            pltpu.VMEM((parts * cols, cols), F32),
            pltpu.VMEM((cols, piece + cols), F32),
        ],
        compiler_params=params(),
        name="merge",
    )(me, even, odd, wide)
    last = [sent[0]] + [swap(sent[k], "tm", k) for k in range(1, parts)]

    basis = pl.pallas_call(
        functools.partial(final_kernel, parts),
        out_shape=shape(half_rows, width, half_cols),
        in_specs=[scalars()] + [whole()] * parts,
        out_specs=whole(),
        compiler_params=params(),
        name="final",
    )(me, *last)
    return basis.transpose(0, 2, 1), coefficients


def solution(mesh):
    placed = (P("space", None, "tm"), P("space", None), P(), P(), P("space", None, None))
    return jax.shard_map(
        local,
        mesh=mesh,
        in_specs=placed,
        out_specs=(P("space", None, "tm"), P("tm", None)),
        check_vma=False,
    )
```

```python
import functools

import jax
import jax.numpy as jnp
from jax import lax
from jax.experimental import pallas as pl
from jax.experimental.pallas import tpu as pltpu
from jax.sharding import PartitionSpec as P

SIGN_STEPS = 8
TAPS = 6
CHUNK = 8
ROW_BLOCKS = 4
F32 = jnp.float32
VMEM_LIMIT = 48 * 1024 * 1024


def params():
    return pltpu.CompilerParams(vmem_limit_bytes=VMEM_LIMIT)


def whole():
    return pl.BlockSpec(memory_space=pltpu.VMEM)


def scalars():
    return pl.BlockSpec(memory_space=pltpu.SMEM)


def swap(x, axis, mask):
    count = lax.axis_size(axis)
    return lax.ppermute(x, axis, [(i, i ^ mask) for i in range(count)])


def swap_both(x, mask):
    parts, patches = lax.axis_size("tm"), lax.axis_size("space")
    route = []
    for t in range(parts):
        for s in range(patches):
            there = (t ^ (mask % parts)) * patches + (s ^ (mask // parts))
            route.append((t * patches + s, there))
    return lax.ppermute(x, ("tm", "space"), route)


def shift_rows(x, by):
    edge = jnp.zeros((1, x.shape[1]), x.dtype)
    if by > 0:
        return jnp.concatenate([edge, x[:-1]], axis=0)
    return jnp.concatenate([x[1:], edge], axis=0)


def mask_columns(mask, mask_t):
    mask_t[...] = mask.astype(F32).T
    half = mask.shape[1] // 2
    return mask_t[pl.ds(0, half, stride=2), :], mask_t[pl.ds(1, half, stride=2), :]


def narrowed_row(snaps, x, mask, taps):
    half = snaps.shape[1] // 2
    even = snaps[x, pl.ds(0, half, stride=2), :] * mask[0]
    odd = snaps[x, pl.ds(1, half, stride=2), :] * mask[1]
    before = taps[0] * even + taps[1] * odd
    here = taps[2] * even + taps[3] * odd
    after = taps[4] * even + taps[5] * odd
    return shift_rows(before, 1) + here + shift_rows(after, -1)


def edge_kernel(rtaps_ref, ctaps_ref, first_ref, last_ref, mask_first_ref, mask_last_ref, up_ref, down_ref, mask_t):
    ctaps = [ctaps_ref[k] for k in range(TAPS)]
    for out, snaps, mask_ref, taps, at in (
        (up_ref, first_ref, mask_first_ref, (rtaps_ref[4], rtaps_ref[5]), 0),
        (down_ref, last_ref, mask_last_ref, (rtaps_ref[0], rtaps_ref[1]), CHUNK - 2),
    ):
        masks = mask_columns(mask_ref[...], mask_t)
        rows = [narrowed_row(snaps, x, [m[:, at + x:at + x + 1] for m in masks], ctaps) for x in range(2)]
        out[...] = taps[0] * rows[0] + taps[1] * rows[1]


def filter_kernel(parts, me_ref, rtaps_ref, ctaps_ref, snap_hbm, mask_ref, *rest):
    pieces, (snaps, sems, mask_t, narrowed, filtered) = rest[:parts], rest[parts:]
    rows, cells = narrowed.shape[0] - 4, narrowed.shape[1]
    me = me_ref[0]
    chunks = rows // CHUNK

    def fetch(c):
        at = pl.ds(c * CHUNK, CHUNK)
        return pltpu.make_async_copy(snap_hbm.at[at], snaps.at[at], sems.at[c])

    for c in range(chunks):
        fetch(c).start()

    rtaps = [rtaps_ref[k] for k in range(TAPS)]
    ctaps = [ctaps_ref[k] for k in range(TAPS)]
    edge = jnp.zeros((2,) + narrowed.shape[1:], F32)
    narrowed[0:2] = edge
    narrowed[rows + 2:rows + 4] = edge

    def narrow(c, carry):
        fetch(c).wait()
        base = pl.multiple_of(c * CHUNK, CHUNK)
        masks = mask_columns(mask_ref[pl.ds(base, CHUNK), :], mask_t)
        for x in range(CHUNK):
            row = narrowed_row(snaps, base + x, [m[:, x:x + 1] for m in masks], ctaps)
            narrowed[base + 2 + x] = row
        return carry

    lax.fori_loop(0, chunks, narrow, 0)
    for i in range(rows // 2):
        total = rtaps[0] * narrowed[2 * i]
        for k in range(1, TAPS):
            total = total + rtaps[k] * narrowed[2 * i + k]
        filtered[i * cells:(i + 1) * cells, :] = total
    size = filtered.shape[0] // parts
    for k in range(parts):
        pieces[k][...] = filtered[pl.ds(pl.multiple_of((me ^ k) * size, 8), size), :]


def halo_kernel(parts, me_ref, above_ref, below_ref, *refs):
    outs = refs[len(refs) // 2:]
    me = me_ref[0]
    cells = above_ref.shape[0]
    for k, out in enumerate(outs):
        out[...] = refs[k][...]

        @pl.when((me ^ k) == 0)
        def _():
            out[:cells, :] = out[:cells, :] + above_ref[...]

        @pl.when((me ^ k) == parts - 1)
        def _():
            out[-cells:, :] = out[-cells:, :] + below_ref[...]


def cross_order(parts):
    return [(a, b) for p in range(0, parts, 2) for q in range(p + 2, parts, 2) for a in (p, p + 1) for b in (q, q + 1)]


def pair_kernel(parts, span, me_ref, probes_ref, *refs):
    half = parts // 2
    mine, theirs, (send_ref, keep_ref, wide, there, flat) = refs[:half], refs[half:2 * half], refs[2 * half:]
    me, owner = me_ref[0], me_ref[2]
    size, cols = mine[0].shape
    low = pl.ds(pl.multiple_of((me % 2) * cols, cols), cols)
    high = pl.ds(pl.multiple_of((1 - me % 2) * cols, cols), cols)
    for h in range(half):
        at = pl.ds(h * size, size)
        wide[at, low] = mine[h][...]
        wide[at, high] = theirs[h][...]
        there[at, :] = probes_ref[pl.ds(pl.multiple_of((me ^ 2 * h) * size, 8), size), :]
    left = split(wide[...])
    gram = dot_parts(left, left, ((0,), (0,)))
    flat[:cols, :] = gram[:cols, :cols]
    flat[cols:2 * cols, :] = gram[:cols, cols:]
    flat[2 * cols:3 * cols, :] = gram[cols:, cols:]
    flat[3 * cols:, :] = dot_parts(left, split(there[...]), ((0,), (0,)))
    give(owner, flat, send_ref, keep_ref)


def give(owner, flat, send_ref, keep_ref):
    count = 2 * send_ref.shape[0]
    share = flat.shape[0] // count
    for k in range(count):
        out = send_ref if k % 2 else keep_ref
        out[k // 2] = flat[pl.ds(pl.multiple_of((owner ^ k) * share, 8), share), :]


def cross_kernel(parts, me_ref, *refs):
    pieces, (send_ref, keep_ref, wide, flat) = refs[:parts], refs[parts:]
    me, owner = me_ref[0], me_ref[1]
    cols = pieces[0].shape[1]
    for k in range(parts):
        wide[:, pl.ds(pl.multiple_of((me ^ k) * cols, cols), cols)] = pieces[k][...]
    sides = [split(wide[:, a * cols:(a + 2) * cols]) for a in range(0, parts, 2)]
    where = {ab: j for j, ab in enumerate(cross_order(parts))}
    for a in range(0, parts, 2):
        for b in range(a + 2, parts, 2):
            prod = dot_parts(sides[a // 2], sides[b // 2], ((0,), (0,)))
            for i in range(2):
                for j in range(2):
                    at = where[a + i, b + j] * cols
                    flat[at:at + cols, :] = prod[i * cols:(i + 1) * cols, j * cols:(j + 1) * cols]
    give(owner, flat, send_ref, keep_ref)


def split(x):
    high = x.astype(jnp.bfloat16)
    return high, (x - high.astype(F32)).astype(jnp.bfloat16)


def dot(a, b, dims):
    return lax.dot_general(a, b, (dims, ((), ())), preferred_element_type=F32)


def dot_parts(a, b, dims=((1,), (0,))):
    (ah, al), (bh, bl) = a, b
    free = 1 - dims[0][0]
    rows = ah.shape[free]
    both = dot(jnp.concatenate([ah, al], axis=free), bh, dims)
    return both[:rows] + (dot(ah, bl, dims) + both[rows:])


def split_dot(a, b, dims=((1,), (0,))):
    return dot_parts(split(a), split(b), dims)


def next_sign(y):
    whole_y = split(y)
    size = y.shape[0] // ROW_BLOCKS
    blocks = []
    for at in range(0, y.shape[0], size):
        square = dot_parts([part[at:at + size] for part in whole_y], whole_y)
        blocks.append(1.5 * y[at:at + size] - 0.5 * dot_parts(split(square), whole_y))
    return jnp.concatenate(blocks, axis=0)


def combine_of(grams):
    order = grams[0].shape[0]
    diagonal = lax.broadcasted_iota(jnp.int32, (order, order), 0) == lax.broadcasted_iota(jnp.int32, (order, order), 1)
    signs = []
    for gram in grams:
        mean = jnp.sum(jnp.where(diagonal, gram, 0.0)) / order
        shifted = jnp.where(diagonal, gram - mean, gram)
        signs.append(shifted / jnp.sqrt(jnp.sum(shifted * shifted, keepdims=True) + 1e-6))
    for _ in range(SIGN_STEPS):
        signs = [next_sign(y) for y in signs]
    half = order // 2
    combines = []
    for y in signs:
        projector = 0.5 * (jnp.where(diagonal, 1.0, 0.0) + y)
        combines.append(projector[:, :half] + projector[:, half:])
    return combines


def merge_kernel(parts, span, me_ref, even_ref, odd_ref, wide_ref, *refs):
    outs, (coef_ref, pairs, cross, weight, turned) = refs[:parts], refs[parts:]
    me, owner = me_ref[0], me_ref[1]
    cols = even_ref.shape[2]
    pair_share, cross_share = pairs.shape[1] // (2 * span), cross.shape[0] // (parts * span)
    for k in range(parts * span):
        source = (odd_ref if k % 2 else even_ref).at[k // 2]
        there = owner ^ k
        place = there % 2 + 2 * (there // parts)
        at = pl.ds(pl.multiple_of(place * pair_share, 8), pair_share)
        pairs[(there % parts) // 2, at, :] = source[:pair_share, :]
        cross[pl.ds(pl.multiple_of(there * cross_share, 8), cross_share), :] = source[pair_share:, :]
    blocks = {ab: cross[j * cols:(j + 1) * cols, :] for j, ab in enumerate(cross_order(parts))}
    for p in range(parts // 2):
        for j, ab in enumerate(((2 * p, 2 * p), (2 * p, 2 * p + 1), (2 * p + 1, 2 * p + 1))):
            blocks[ab] = pairs[p, j * cols:(j + 1) * cols, :]
    products = jnp.concatenate([pairs[p, 3 * cols:, :] for p in range(parts // 2)], axis=0)
    weights, count = None, parts
    while count > 1:
        grams = []
        for p in range(0, count, 2):
            low = jnp.concatenate([blocks[p, p], blocks[p, p + 1]], axis=1)
            high = jnp.concatenate([blocks[p, p + 1].T, blocks[p + 1, p + 1]], axis=1)
            grams.append(jnp.concatenate([low, high], axis=0))
        combines = combine_of(grams)
        if weights is None:
            weights = combines
        else:
            per = len(weights) // len(combines)
            weights = [
                split_dot(w, combines[i // per][(i % per) * cols:(i % per + 1) * cols, :])
                for i, w in enumerate(weights)
            ]
            weights = [jnp.concatenate(weights[i:i + per], axis=0) for i in range(0, len(weights), per)]
        merged = {}
        if count > 2:
            for p in range(count // 2):
                for q in range(p, count // 2):
                    if p == q:
                        cross = grams[p]
                    else:
                        cross = jnp.concatenate([
                            jnp.concatenate([blocks[2 * p + i, 2 * q], blocks[2 * p + i, 2 * q + 1]], axis=1)
                            for i in range(2)
                        ], axis=0)
                    right = split_dot(cross, combines[q])
                    merged[p, q] = split_dot(combines[p], right, ((0,), (0,)))
        blocks, count = merged, count // 2
    weight[...] = weights[0]
    total = dot_parts(split(wide_ref[...]), split(weight[...]))
    width = cols // parts
    rows = total.shape[0]
    turned[:, :rows] = total.T
    turned[:, rows:] = split_dot(weight[...], products, ((0,), (0,)))
    for k in range(parts):
        outs[k][...] = turned[pl.ds(pl.multiple_of((me ^ k) * width, 8), width), :rows]
    coef_ref[...] = turned[pl.ds(pl.multiple_of(me * width, 8), width), rows:]


def final_kernel(parts, me_ref, *refs):
    pieces, basis_ref = refs[:parts], refs[parts]
    me = me_ref[0]
    per, cells = basis_ref.shape[0] // parts, basis_ref.shape[2]
    for k in range(parts):
        base = (me ^ k) * per
        for i in range(per):
            basis_ref[base + i] = pieces[k][:, i * cells:(i + 1) * cells]


def shape(*dims):
    return jax.ShapeDtypeStruct(dims, F32)


def local(snapshots, land_mask, taps_rows, taps_cols, probes):
    rows, grid_cols, cols = snapshots.shape
    half_rows, half_cols = rows // 2, grid_cols // 2
    parts, patches = lax.axis_size("tm"), lax.axis_size("space")
    cells = half_rows * half_cols
    piece = cells // parts
    span = 2 if patches > 1 else 1
    position, patch = lax.axis_index("tm"), lax.axis_index("space")
    here = patch % span
    me = jnp.stack([position, position + parts * here, position % 2 + 2 * here]).astype(jnp.int32)

    snapshots, land_mask, taps_rows, taps_cols = (
        pltpu.with_memory_space_constraint(x, pltpu.HBM) for x in (snapshots, land_mask, taps_rows, taps_cols)
    )

    row_block, mask_block = (2, grid_cols, cols), (CHUNK, grid_cols)
    to_above, to_below = pl.pallas_call(
        edge_kernel,
        out_shape=[shape(half_cols, cols)] * 2,
        grid=(1,),
        in_specs=[
            scalars(), scalars(),
            pl.BlockSpec(row_block, lambda i: (0, 0, 0)),
            pl.BlockSpec(row_block, lambda i: (rows // 2 - 1, 0, 0)),
            pl.BlockSpec(mask_block, lambda i: (0, 0)),
            pl.BlockSpec(mask_block, lambda i: (rows // CHUNK - 1, 0)),
        ],
        out_specs=[pl.BlockSpec((half_cols, cols), lambda i: (0, 0))] * 2,
        scratch_shapes=[pltpu.VMEM((grid_cols, CHUNK), F32)],
        compiler_params=params(),
        name="edge",
    )(taps_rows, taps_cols, snapshots, snapshots, land_mask, land_mask)
    up = [(i, i + 1) for i in range(patches - 1)]
    above = lax.ppermute(to_below, "space", up)
    below = lax.ppermute(to_above, "space", [(j, i) for i, j in up])

    pieces = pl.pallas_call(
        functools.partial(filter_kernel, parts),
        out_shape=[shape(piece, cols)] * parts,
        in_specs=[scalars(), scalars(), scalars(), pl.BlockSpec(memory_space=pltpu.HBM), whole()],
        out_specs=[whole()] * parts,
        scratch_shapes=[
            pltpu.VMEM((rows, grid_cols, cols), F32),
            pltpu.SemaphoreType.DMA((rows // CHUNK,)),
            pltpu.VMEM((grid_cols, CHUNK), F32),
            pltpu.VMEM((rows + 4, half_cols, cols), F32),
            pltpu.VMEM((cells, cols), F32),
        ],
        compiler_params=params(),
        cost_estimate=pl.CostEstimate(flops=0, bytes_accessed=4 * snapshots.size, transcendentals=0),
        name="filter",
    )(me, taps_rows, taps_cols, snapshots, land_mask)
    kept = pl.pallas_call(
        functools.partial(halo_kernel, parts),
        out_shape=[shape(piece, cols)] * parts,
        in_specs=[scalars()] + [whole()] * (parts + 2),
        out_specs=[whole()] * parts,
        input_output_aliases={3 + k: k for k in range(parts)},
        compiler_params=params(),
        name="halo",
    )(me, above, below, *pieces)
    theirs = {k: swap(kept[k + 1], "tm", 1) for k in range(0, parts, 2)}
    far = {0: kept[0], 1: theirs[0]}
    for k in range(2, parts, 2):
        far[k] = swap(kept[k], "tm", k)
        far[k + 1] = swap(theirs[k], "tm", k)

    owners = 2 * span
    size = 5 * cols // owners
    send, keep = pl.pallas_call(
        functools.partial(pair_kernel, parts, span),
        out_shape=[shape(span, size, cols)] * 2,
        in_specs=[scalars()] + [whole()] * (parts + 1),
        out_specs=[whole()] * 2,
        scratch_shapes=[
            pltpu.VMEM((cells // 2, 2 * cols), F32),
            pltpu.VMEM((cells // 2, cols), F32),
            pltpu.VMEM((5 * cols, cols), F32),
        ],
        compiler_params=params(),
        cost_estimate=pl.CostEstimate(flops=0, bytes_accessed=0, transcendentals=0),
        name="pair",
    )(me, probes.reshape(cells, cols), *[kept[k] for k in range(0, parts, 2)], *[theirs[k] for k in range(0, parts, 2)])
    got = swap(send, "tm", 1)
    got, *waited = lax.optimization_barrier([got] + [far[k] for k in range(2, parts)])
    far.update(zip(range(2, parts), waited))
    pair_share = keep[0] + got[0]
    for h in range(1, span):
        pair_share = pair_share + swap(keep[h] + got[h], "space", h)

    blocks = len(cross_order(parts))
    owners = parts * span
    size = blocks * cols // owners
    send, keep, wide = pl.pallas_call(
        functools.partial(cross_kernel, parts),
        out_shape=[shape(owners // 2, size, cols)] * 2 + [shape(piece, parts * cols)],
        in_specs=[scalars()] + [whole()] * parts,
        out_specs=[whole()] * 3,
        scratch_shapes=[pltpu.VMEM((blocks * cols, cols), F32)],
        compiler_params=params(),
        cost_estimate=pl.CostEstimate(flops=0, bytes_accessed=0, transcendentals=0),
        name="cross",
    )(me, *[far[k] for k in range(parts)])
    got = swap(send, "tm", 1)
    mine = keep[0] + got[0]
    for h in range(1, owners // 2):
        mine = mine + swap_both(keep[h] + got[h], 2 * h)
    mine = jnp.concatenate([pair_share, mine], axis=0)
    bits = [1 << b for b in range(1, patches.bit_length() - 1)]
    for bit in bits:
        mine = mine + swap(mine, "space", bit)
    even = jnp.stack([mine] + [swap_both(mine, 2 * h) for h in range(1, owners // 2)])
    odd = swap(even, "tm", 1)

    width = cols // parts
    *sent, coefficients = pl.pallas_call(
        functools.partial(merge_kernel, parts, span),
        out_shape=[shape(width, piece)] * parts + [shape(width, cols)],
        in_specs=[scalars()] + [whole()] * 3,
        out_specs=[whole()] * (parts + 1),
        scratch_shapes=[
            pltpu.VMEM((parts // 2, 5 * cols, cols), F32),
            pltpu.VMEM((blocks * cols, cols), F32),
            pltpu.VMEM((parts * cols, cols), F32),
            pltpu.VMEM((cols, piece + cols), F32),
        ],
        compiler_params=params(),
        name="merge",
    )(me, even, odd, wide)
    last = [sent[0]] + [swap(sent[k], "tm", k) for k in range(1, parts)]

    basis = pl.pallas_call(
        functools.partial(final_kernel, parts),
        out_shape=shape(half_rows, width, half_cols),
        in_specs=[scalars()] + [whole()] * parts,
        out_specs=whole(),
        compiler_params=params(),
        name="final",
    )(me, *last)
    return basis.transpose(0, 2, 1), coefficients


def solution(mesh):
    placed = (P("space", None, "tm"), P("space", None), P(), P(), P("space", None, None))
    return jax.shard_map(
        local,
        mesh=mesh,
        in_specs=placed,
        out_specs=(P("space", None, "tm"), P("tm", None)),
        check_vma=False,
    )
```

```python
import functools

import jax
import jax.numpy as jnp
from jax import lax
from jax.experimental import pallas as pl
from jax.experimental.pallas import tpu as pltpu
from jax.sharding import PartitionSpec as P

SIGN_STEPS = 8
TAPS = 6
CHUNK = 8
ROW_BLOCKS = 2
F32 = jnp.float32
VMEM_LIMIT = 48 * 1024 * 1024


def params():
    return pltpu.CompilerParams(vmem_limit_bytes=VMEM_LIMIT)


def whole():
    return pl.BlockSpec(memory_space=pltpu.VMEM)


def scalars():
    return pl.BlockSpec(memory_space=pltpu.SMEM)


def swap(x, axis, mask):
    count = lax.axis_size(axis)
    return lax.ppermute(x, axis, [(i, i ^ mask) for i in range(count)])


def swap_both(x, mask):
    parts, patches = lax.axis_size("tm"), lax.axis_size("space")
    route = []
    for t in range(parts):
        for s in range(patches):
            there = (t ^ (mask % parts)) * patches + (s ^ (mask // parts))
            route.append((t * patches + s, there))
    return lax.ppermute(x, ("tm", "space"), route)


def shift_rows(x, by):
    edge = jnp.zeros((1, x.shape[1]), x.dtype)
    if by > 0:
        return jnp.concatenate([edge, x[:-1]], axis=0)
    return jnp.concatenate([x[1:], edge], axis=0)


def mask_columns(mask, mask_t):
    mask_t[...] = mask.astype(F32).T
    half = mask.shape[1] // 2
    return mask_t[pl.ds(0, half, stride=2), :], mask_t[pl.ds(1, half, stride=2), :]


def narrowed_row(snaps, x, mask, taps):
    half = snaps.shape[1] // 2
    even = snaps[x, pl.ds(0, half, stride=2), :] * mask[0]
    odd = snaps[x, pl.ds(1, half, stride=2), :] * mask[1]
    before = taps[0] * even + taps[1] * odd
    here = taps[2] * even + taps[3] * odd
    after = taps[4] * even + taps[5] * odd
    return shift_rows(before, 1) + here + shift_rows(after, -1)


def edge_kernel(rtaps_ref, ctaps_ref, first_ref, last_ref, mask_first_ref, mask_last_ref, up_ref, down_ref, mask_t):
    ctaps = [ctaps_ref[k] for k in range(TAPS)]
    for out, snaps, mask_ref, taps, at in (
        (up_ref, first_ref, mask_first_ref, (rtaps_ref[4], rtaps_ref[5]), 0),
        (down_ref, last_ref, mask_last_ref, (rtaps_ref[0], rtaps_ref[1]), CHUNK - 2),
    ):
        masks = mask_columns(mask_ref[...], mask_t)
        rows = [narrowed_row(snaps, x, [m[:, at + x:at + x + 1] for m in masks], ctaps) for x in range(2)]
        out[...] = taps[0] * rows[0] + taps[1] * rows[1]


def filter_kernel(parts, rtaps_ref, ctaps_ref, snap_hbm, mask_ref, *rest):
    pieces, (snaps, sems, mask_t, spread, narrowed, filtered) = rest[:parts], rest[parts:]
    rows, cells = narrowed.shape[0] - 4, narrowed.shape[1]
    me = lax.axis_index("tm")
    chunks = rows // CHUNK

    def fetch(c):
        at = pl.ds(c * CHUNK, CHUNK)
        return pltpu.make_async_copy(snap_hbm.at[at], snaps.at[at], sems.at[c])

    for c in range(chunks):
        fetch(c).start()

    rtaps = [rtaps_ref[k] for k in range(TAPS)]
    ctaps = [ctaps_ref[k] for k in range(TAPS)]
    edge = jnp.zeros((2,) + narrowed.shape[1:], F32)
    narrowed[0:2] = edge
    narrowed[rows + 2:rows + 4] = edge

    masks = mask_columns(mask_ref[...], mask_t)
    for x in range(rows):
        for j, mask in enumerate(masks):
            spread[x, j] = jnp.broadcast_to(mask[:, x:x + 1], (cells, narrowed.shape[2]))

    def narrow(c, carry):
        fetch(c).wait()
        base = pl.multiple_of(c * CHUNK, CHUNK)
        for x in range(CHUNK):
            row = narrowed_row(snaps, base + x, spread[base + x], ctaps)
            narrowed[base + 2 + x] = row
        return carry

    lax.fori_loop(0, chunks, narrow, 0)
    for i in range(rows // 2):
        total = rtaps[0] * narrowed[2 * i]
        for k in range(1, TAPS):
            total = total + rtaps[k] * narrowed[2 * i + k]
        filtered[i * cells:(i + 1) * cells, :] = total
    size = filtered.shape[0] // parts
    for k in range(parts):
        pieces[k][...] = filtered[pl.ds(pl.multiple_of((me ^ k) * size, 8), size), :]


def halo_kernel(parts, above_ref, below_ref, *refs):
    outs = refs[len(refs) // 2:]
    me = lax.axis_index("tm")
    cells = above_ref.shape[0]
    for k, out in enumerate(outs):
        out[...] = refs[k][...]

        @pl.when((me ^ k) == 0)
        def _():
            out[:cells, :] = out[:cells, :] + above_ref[...]

        @pl.when((me ^ k) == parts - 1)
        def _():
            out[-cells:, :] = out[-cells:, :] + below_ref[...]


def cross_order(parts):
    return [(a, b) for p in range(0, parts, 2) for q in range(p + 2, parts, 2) for a in (p, p + 1) for b in (q, q + 1)]


def pair_kernel(parts, span, probes_ref, *refs):
    half = parts // 2
    owners = 2 * span
    mine, theirs, refs = refs[:half], refs[half:2 * half], refs[2 * half:]
    outs, (wide, there, flat) = refs[:owners], refs[owners:]
    me, owner = positions(2, span)
    size, cols = mine[0].shape
    low = pl.ds(pl.multiple_of((me % 2) * cols, cols), cols)
    high = pl.ds(pl.multiple_of((1 - me % 2) * cols, cols), cols)
    for h in range(half):
        at = pl.ds(h * size, size)
        wide[at, low] = mine[h][...]
        wide[at, high] = theirs[h][...]
        there[at, :] = probes_ref[pl.ds(pl.multiple_of((me ^ 2 * h) * size, 8), size), :]
    left = split(wide[...])
    gram = dot_parts(left, left, ((0,), (0,)))
    flat[:cols, :] = gram[:cols, :cols]
    flat[cols:2 * cols, :] = gram[:cols, cols:]
    flat[2 * cols:3 * cols, :] = gram[cols:, cols:]
    flat[3 * cols:, :] = dot_parts(left, split(there[...]), ((0,), (0,)))
    share = flat.shape[0] // owners
    for k, out in enumerate(outs):
        out[...] = flat[pl.ds(pl.multiple_of((owner ^ k) * share, 8), share), :]


def positions(count, span):
    me = lax.axis_index("tm")
    return me, me % count + count * (lax.axis_index("space") % span)


def give(owner, flat, send_ref, keep_ref):
    count = 2 * send_ref.shape[0]
    share = flat.shape[0] // count
    for k in range(count):
        out = send_ref if k % 2 else keep_ref
        out[k // 2] = flat[pl.ds(pl.multiple_of((owner ^ k) * share, 8), share), :]


def cross_kernel(parts, span, *refs):
    pieces, (send_ref, keep_ref, wide, flat) = refs[:parts], refs[parts:]
    me, owner = positions(parts, span)
    cols = pieces[0].shape[1]
    for k in range(parts):
        wide[:, pl.ds(pl.multiple_of((me ^ k) * cols, cols), cols)] = pieces[k][...]
    sides = [split(wide[:, a * cols:(a + 2) * cols]) for a in range(0, parts, 2)]
    where = {ab: j for j, ab in enumerate(cross_order(parts))}
    for a in range(0, parts, 2):
        for b in range(a + 2, parts, 2):
            prod = dot_parts(sides[a // 2], sides[b // 2], ((0,), (0,)))
            for i in range(2):
                for j in range(2):
                    at = where[a + i, b + j] * cols
                    flat[at:at + cols, :] = prod[i * cols:(i + 1) * cols, j * cols:(j + 1) * cols]
    give(owner, flat, send_ref, keep_ref)


def split(x):
    high = x.astype(jnp.bfloat16)
    return high, (x - high.astype(F32)).astype(jnp.bfloat16)


def dot(a, b, dims):
    return lax.dot_general(a, b, (dims, ((), ())), preferred_element_type=F32)


def dot_parts(a, b, dims=((1,), (0,))):
    (ah, al), (bh, bl) = a, b
    left = jnp.concatenate([ah, ah, al], axis=dims[0][0])
    return dot(left, jnp.concatenate([bh, bl, bh], axis=dims[1][0]), dims)


def split_dot(a, b, dims=((1,), (0,))):
    return dot_parts(split(a), split(b), dims)


def next_sign(y):
    whole_y = split(y)
    size = y.shape[0] // ROW_BLOCKS
    blocks = []
    for at in range(0, y.shape[0], size):
        square = dot_parts([part[at:at + size] for part in whole_y], whole_y)
        blocks.append(1.5 * y[at:at + size] - 0.5 * dot_parts(split(square), whole_y))
    return jnp.concatenate(blocks, axis=0)


def combine_of(grams):
    order = grams[0].shape[0]
    diagonal = lax.broadcasted_iota(jnp.int32, (order, order), 0) == lax.broadcasted_iota(jnp.int32, (order, order), 1)
    signs = []
    for gram in grams:
        mean = jnp.sum(jnp.where(diagonal, gram, 0.0)) / order
        shifted = jnp.where(diagonal, gram - mean, gram)
        signs.append(shifted / jnp.sqrt(jnp.sum(shifted * shifted, keepdims=True) + 1e-6))
    for _ in range(SIGN_STEPS):
        signs = [next_sign(y) for y in signs]
    half = order // 2
    combines = []
    for y in signs:
        projector = 0.5 * (jnp.where(diagonal, 1.0, 0.0) + y)
        combines.append(projector[:, :half] + projector[:, half:])
    return combines


def merge_kernel(parts, span, even_ref, odd_ref, wide_ref, *refs):
    outs, (coef_ref, pairs, cross, weight, turned) = refs[:parts], refs[parts:]
    me, owner = positions(parts, span)
    cols = even_ref.shape[2]
    pair_share, cross_share = pairs.shape[1] // (2 * span), cross.shape[0] // (parts * span)
    for k in range(parts * span):
        source = (odd_ref if k % 2 else even_ref).at[k // 2]
        there = owner ^ k
        place = there % 2 + 2 * (there // parts)
        at = pl.ds(pl.multiple_of(place * pair_share, 8), pair_share)
        pairs[(there % parts) // 2, at, :] = source[:pair_share, :]
        cross[pl.ds(pl.multiple_of(there * cross_share, 8), cross_share), :] = source[pair_share:, :]
    blocks = {ab: cross[j * cols:(j + 1) * cols, :] for j, ab in enumerate(cross_order(parts))}
    for p in range(parts // 2):
        for j, ab in enumerate(((2 * p, 2 * p), (2 * p, 2 * p + 1), (2 * p + 1, 2 * p + 1))):
            blocks[ab] = pairs[p, j * cols:(j + 1) * cols, :]
    products = jnp.concatenate([pairs[p, 3 * cols:, :] for p in range(parts // 2)], axis=0)
    weights, count = None, parts
    while count > 1:
        grams = []
        for p in range(0, count, 2):
            low = jnp.concatenate([blocks[p, p], blocks[p, p + 1]], axis=1)
            high = jnp.concatenate([blocks[p, p + 1].T, blocks[p + 1, p + 1]], axis=1)
            grams.append(jnp.concatenate([low, high], axis=0))
        combines = combine_of(grams)
        if weights is None:
            weights = combines
        else:
            per = len(weights) // len(combines)
            weights = [
                split_dot(w, combines[i // per][(i % per) * cols:(i % per + 1) * cols, :])
                for i, w in enumerate(weights)
            ]
            weights = [jnp.concatenate(weights[i:i + per], axis=0) for i in range(0, len(weights), per)]
        merged = {}
        if count > 2:
            for p in range(count // 2):
                for q in range(p, count // 2):
                    if p == q:
                        cross = grams[p]
                    else:
                        cross = jnp.concatenate([
                            jnp.concatenate([blocks[2 * p + i, 2 * q], blocks[2 * p + i, 2 * q + 1]], axis=1)
                            for i in range(2)
                        ], axis=0)
                    right = split_dot(cross, combines[q])
                    merged[p, q] = split_dot(combines[p], right, ((0,), (0,)))
        blocks, count = merged, count // 2
    weight[...] = weights[0]
    total = dot_parts(split(wide_ref[...]), split(weight[...]))
    width = cols // parts
    rows = total.shape[0]
    turned[:, :rows] = total.T
    turned[:, rows:] = split_dot(weight[...], products, ((0,), (0,)))
    for k in range(parts):
        outs[k][...] = turned[pl.ds(pl.multiple_of((me ^ k) * width, 8), width), :rows]
    coef_ref[...] = turned[pl.ds(pl.multiple_of(me * width, 8), width), rows:]


def final_kernel(parts, *refs):
    pieces, basis_ref = refs[:parts], refs[parts]
    me = lax.axis_index("tm")
    per, cells = basis_ref.shape[0] // parts, basis_ref.shape[2]
    for k in range(parts):
        base = (me ^ k) * per
        for i in range(per):
            basis_ref[base + i] = pieces[k][:, i * cells:(i + 1) * cells]


def shape(*dims):
    return jax.ShapeDtypeStruct(dims, F32)


def local(snapshots, land_mask, taps_rows, taps_cols, probes):
    rows, grid_cols, cols = snapshots.shape
    half_rows, half_cols = rows // 2, grid_cols // 2
    parts, patches = lax.axis_size("tm"), lax.axis_size("space")
    cells = half_rows * half_cols
    piece = cells // parts
    span = 2 if patches > 1 else 1

    snapshots, land_mask, taps_rows, taps_cols = (
        pltpu.with_memory_space_constraint(x, pltpu.HBM) for x in (snapshots, land_mask, taps_rows, taps_cols)
    )

    row_block, mask_block = (2, grid_cols, cols), (CHUNK, grid_cols)
    to_above, to_below = pl.pallas_call(
        edge_kernel,
        out_shape=[shape(half_cols, cols)] * 2,
        grid=(1,),
        in_specs=[
            scalars(), scalars(),
            pl.BlockSpec(row_block, lambda i: (0, 0, 0)),
            pl.BlockSpec(row_block, lambda i: (rows // 2 - 1, 0, 0)),
            pl.BlockSpec(mask_block, lambda i: (0, 0)),
            pl.BlockSpec(mask_block, lambda i: (rows // CHUNK - 1, 0)),
        ],
        out_specs=[pl.BlockSpec((half_cols, cols), lambda i: (0, 0))] * 2,
        scratch_shapes=[pltpu.VMEM((grid_cols, CHUNK), F32)],
        compiler_params=params(),
        name="edge",
    )(taps_rows, taps_cols, snapshots, snapshots, land_mask, land_mask)
    up = [(i, i + 1) for i in range(patches - 1)]
    above = lax.ppermute(to_below, "space", up)
    below = lax.ppermute(to_above, "space", [(j, i) for i, j in up])

    pieces = pl.pallas_call(
        functools.partial(filter_kernel, parts),
        out_shape=[shape(piece, cols)] * parts,
        in_specs=[scalars(), scalars(), pl.BlockSpec(memory_space=pltpu.HBM), whole()],
        out_specs=[whole()] * parts,
        scratch_shapes=[
            pltpu.VMEM((rows, grid_cols, cols), F32),
            pltpu.SemaphoreType.DMA((rows // CHUNK,)),
            pltpu.VMEM((grid_cols, rows), F32),
            pltpu.VMEM((rows, 2, half_cols, cols), F32),
            pltpu.VMEM((rows + 4, half_cols, cols), F32),
            pltpu.VMEM((cells, cols), F32),
        ],
        compiler_params=params(),
        cost_estimate=pl.CostEstimate(flops=0, bytes_accessed=4 * snapshots.size, transcendentals=0),
        name="filter",
    )(taps_rows, taps_cols, snapshots, land_mask)
    kept = pl.pallas_call(
        functools.partial(halo_kernel, parts),
        out_shape=[shape(piece, cols)] * parts,
        in_specs=[whole()] * (parts + 2),
        out_specs=[whole()] * parts,
        input_output_aliases={2 + k: k for k in range(parts)},
        compiler_params=params(),
        name="halo",
    )(above, below, *pieces)
    theirs = {k: swap(kept[k + 1], "tm", 1) for k in range(0, parts, 2)}
    far = {0: kept[0], 1: theirs[0]}
    for k in range(2, parts, 2):
        far[k] = swap(kept[k], "tm", k)
        far[k + 1] = swap(theirs[k], "tm", k)

    owners = 2 * span
    sums = pl.pallas_call(
        functools.partial(pair_kernel, parts, span),
        out_shape=[shape(5 * cols // owners, cols)] * owners,
        in_specs=[whole()] * (parts + 1),
        out_specs=[whole()] * owners,
        scratch_shapes=[
            pltpu.VMEM((cells // 2, 2 * cols), F32),
            pltpu.VMEM((cells // 2, cols), F32),
            pltpu.VMEM((5 * cols, cols), F32),
        ],
        compiler_params=params(),
        cost_estimate=pl.CostEstimate(flops=0, bytes_accessed=0, transcendentals=0),
        name="pair",
    )(probes.reshape(cells, cols), *[kept[k] for k in range(0, parts, 2)], *[theirs[k] for k in range(0, parts, 2)])
    got = [swap_both(sums[j], j % 2 + parts * (j // 2)) for j in range(1, owners)]
    tied = lax.optimization_barrier(got + [far[k] for k in range(2, parts)])
    got = tied[:owners - 1]
    far.update(zip(range(2, parts), tied[owners - 1:]))
    pair_share = sums[0]
    for x in got:
        pair_share = pair_share + x
    bits = [1 << b for b in range(1, patches.bit_length() - 1)]

    blocks = len(cross_order(parts))
    owners = parts * span
    size = blocks * cols // owners
    send, keep, wide = pl.pallas_call(
        functools.partial(cross_kernel, parts, span),
        out_shape=[shape(owners // 2, size, cols)] * 2 + [shape(piece, parts * cols)],
        in_specs=[whole()] * parts,
        out_specs=[whole()] * 3,
        scratch_shapes=[pltpu.VMEM((blocks * cols, cols), F32)],
        compiler_params=params(),
        cost_estimate=pl.CostEstimate(flops=0, bytes_accessed=0, transcendentals=0),
        name="cross",
    )(*[far[k] for k in range(parts)])
    got = swap(send, "tm", 1)
    mine = keep[0] + got[0]
    for h in range(1, owners // 2):
        mine = mine + swap_both(keep[h] + got[h], 2 * h)
    mine = jnp.concatenate([pair_share, mine], axis=0)
    for bit in bits:
        mine = mine + swap(mine, "space", bit)
    even = jnp.stack([mine] + [swap_both(mine, 2 * h) for h in range(1, owners // 2)])
    odd = swap(even, "tm", 1)

    width = cols // parts
    *sent, coefficients = pl.pallas_call(
        functools.partial(merge_kernel, parts, span),
        out_shape=[shape(width, piece)] * parts + [shape(width, cols)],
        in_specs=[whole()] * 3,
        out_specs=[whole()] * (parts + 1),
        scratch_shapes=[
            pltpu.VMEM((parts // 2, 5 * cols, cols), F32),
            pltpu.VMEM((blocks * cols, cols), F32),
            pltpu.VMEM((parts * cols, cols), F32),
            pltpu.VMEM((cols, piece + cols), F32),
        ],
        compiler_params=params(),
        name="merge",
    )(even, odd, wide)
    last = [sent[0]] + [swap(sent[k], "tm", k) for k in range(1, parts)]

    basis = pl.pallas_call(
        functools.partial(final_kernel, parts),
        out_shape=shape(half_rows, width, half_cols),
        in_specs=[whole()] * parts,
        out_specs=whole(),
        compiler_params=params(),
        name="final",
    )(*last)
    return basis.transpose(0, 2, 1), coefficients


def solution(mesh):
    placed = (P("space", None, "tm"), P("space", None), P(), P(), P("space", None, None))
    return jax.shard_map(
        local,
        mesh=mesh,
        in_specs=placed,
        out_specs=(P("space", None, "tm"), P("tm", None)),
        check_vma=False,
    )
```

```python
import functools

import jax
import jax.numpy as jnp
from jax import lax
from jax.experimental import pallas as pl
from jax.experimental.pallas import tpu as pltpu
from jax.sharding import PartitionSpec as P

SIGN_STEPS = 8
TAPS = 6
CHUNK = 8
ROW_BLOCKS = 1
F32 = jnp.float32
VMEM_LIMIT = 48 * 1024 * 1024


def params():
    return pltpu.CompilerParams(vmem_limit_bytes=VMEM_LIMIT)


def whole():
    return pl.BlockSpec(memory_space=pltpu.VMEM)


def scalars():
    return pl.BlockSpec(memory_space=pltpu.SMEM)


def swap(x, axis, mask):
    count = lax.axis_size(axis)
    return lax.ppermute(x, axis, [(i, i ^ mask) for i in range(count)])


def swap_both(x, mask):
    parts, patches = lax.axis_size("tm"), lax.axis_size("space")
    route = []
    for t in range(parts):
        for s in range(patches):
            there = (t ^ (mask % parts)) * patches + (s ^ (mask // parts))
            route.append((t * patches + s, there))
    return lax.ppermute(x, ("tm", "space"), route)


def shift_rows(x, by):
    edge = jnp.zeros((1, x.shape[1]), x.dtype)
    if by > 0:
        return jnp.concatenate([edge, x[:-1]], axis=0)
    return jnp.concatenate([x[1:], edge], axis=0)


def mask_columns(mask, mask_t):
    mask_t[...] = mask.astype(F32).T
    half = mask.shape[1] // 2
    return mask_t[pl.ds(0, half, stride=2), :], mask_t[pl.ds(1, half, stride=2), :]


def narrowed_row(snaps, x, mask, taps):
    half = snaps.shape[1] // 2
    even = snaps[x, pl.ds(0, half, stride=2), :] * mask[0]
    odd = snaps[x, pl.ds(1, half, stride=2), :] * mask[1]
    before = taps[0] * even + taps[1] * odd
    here = taps[2] * even + taps[3] * odd
    after = taps[4] * even + taps[5] * odd
    return shift_rows(before, 1) + here + shift_rows(after, -1)


def edge_kernel(rtaps_ref, ctaps_ref, first_ref, last_ref, mask_first_ref, mask_last_ref, near_ref, far_ref, mask_t):
    ctaps = [ctaps_ref[k] for k in range(TAPS)]
    even = lax.axis_index("space") % 2 == 0
    shares = []
    for snaps, mask_ref, taps, at in (
        (first_ref, mask_first_ref, (rtaps_ref[4], rtaps_ref[5]), 0),
        (last_ref, mask_last_ref, (rtaps_ref[0], rtaps_ref[1]), CHUNK - 2),
    ):
        masks = mask_columns(mask_ref[...], mask_t)
        rows = [narrowed_row(snaps, x, [m[:, at + x:at + x + 1] for m in masks], ctaps) for x in range(2)]
        shares.append(taps[0] * rows[0] + taps[1] * rows[1])
    up, down = shares
    near_ref[...] = jnp.where(even, down, up)
    far_ref[...] = jnp.where(even, up, down)


def filter_kernel(parts, rtaps_ref, ctaps_ref, snap_hbm, mask_ref, *rest):
    pieces, (snaps, sems, mask_t, spread, narrowed, filtered) = rest[:parts], rest[parts:]
    rows, cells = narrowed.shape[0] - 4, narrowed.shape[1]
    me = lax.axis_index("tm")
    chunks = rows // CHUNK

    def fetch(c):
        at = pl.ds(c * CHUNK, CHUNK)
        return pltpu.make_async_copy(snap_hbm.at[at], snaps.at[at], sems.at[c])

    for c in range(chunks):
        fetch(c).start()

    rtaps = [rtaps_ref[k] for k in range(TAPS)]
    ctaps = [ctaps_ref[k] for k in range(TAPS)]
    edge = jnp.zeros((2,) + narrowed.shape[1:], F32)
    narrowed[0:2] = edge
    narrowed[rows + 2:rows + 4] = edge

    masks = mask_columns(mask_ref[...], mask_t)
    for x in range(rows):
        for j, mask in enumerate(masks):
            spread[x, j] = jnp.broadcast_to(mask[:, x:x + 1], (cells, narrowed.shape[2]))

    def narrow(c, carry):
        fetch(c).wait()
        base = pl.multiple_of(c * CHUNK, CHUNK)
        for x in range(CHUNK):
            row = narrowed_row(snaps, base + x, spread[base + x], ctaps)
            narrowed[base + 2 + x] = row
        return carry

    lax.fori_loop(0, chunks, narrow, 0)
    for i in range(rows // 2):
        total = rtaps[0] * narrowed[2 * i]
        for k in range(1, TAPS):
            total = total + rtaps[k] * narrowed[2 * i + k]
        filtered[i * cells:(i + 1) * cells, :] = total
    size = filtered.shape[0] // parts
    for k in range(parts):
        pieces[k][...] = filtered[pl.ds(pl.multiple_of((me ^ k) * size, 8), size), :]


def halo_kernel(parts, near_ref, far_ref, *refs):
    outs = refs[len(refs) // 2:]
    me = lax.axis_index("tm")
    cells = near_ref.shape[0]
    even = lax.axis_index("space") % 2 == 0
    above = jnp.where(even, far_ref[...], near_ref[...])
    below = jnp.where(even, near_ref[...], far_ref[...])
    for k, out in enumerate(outs):
        out[...] = refs[k][...]

        @pl.when((me ^ k) == 0)
        def _():
            out[:cells, :] = out[:cells, :] + above

        @pl.when((me ^ k) == parts - 1)
        def _():
            out[-cells:, :] = out[-cells:, :] + below


def cross_order(parts):
    return [(a, b) for p in range(0, parts, 2) for q in range(p + 2, parts, 2) for a in (p, p + 1) for b in (q, q + 1)]


def pair_kernel(parts, span, probes_ref, *refs):
    half = parts // 2
    owners = 2 * span
    mine, theirs, refs = refs[:half], refs[half:2 * half], refs[2 * half:]
    outs, (wide, there, flat) = refs[:owners], refs[owners:]
    me, owner = positions(2, span)
    size, cols = mine[0].shape
    low = pl.ds(pl.multiple_of((me % 2) * cols, cols), cols)
    high = pl.ds(pl.multiple_of((1 - me % 2) * cols, cols), cols)
    for h in range(half):
        at = pl.ds(h * size, size)
        wide[at, low] = mine[h][...]
        wide[at, high] = theirs[h][...]
        there[at, :] = probes_ref[pl.ds(pl.multiple_of((me ^ 2 * h) * size, 8), size), :]
    left = split(wide[...])
    gram = dot_parts(left, left, ((0,), (0,)))
    flat[:cols, :] = gram[:cols, :cols]
    flat[cols:2 * cols, :] = gram[:cols, cols:]
    flat[2 * cols:3 * cols, :] = gram[cols:, cols:]
    flat[3 * cols:, :] = dot_parts(left, split(there[...]), ((0,), (0,)))
    share = flat.shape[0] // owners
    for k, out in enumerate(outs):
        out[...] = flat[pl.ds(pl.multiple_of((owner ^ k) * share, 8), share), :]


def positions(count, span):
    me = lax.axis_index("tm")
    return me, me % count + count * (lax.axis_index("space") % span)


def give(owner, flat, send_ref, keep_ref):
    count = 2 * send_ref.shape[0]
    share = flat.shape[0] // count
    for k in range(count):
        out = send_ref if k % 2 else keep_ref
        out[k // 2] = flat[pl.ds(pl.multiple_of((owner ^ k) * share, 8), share), :]


def cross_kernel(parts, span, *refs):
    pieces, (send_ref, keep_ref, high_ref, low_ref, wide, flat) = refs[:parts], refs[parts:]
    me, owner = positions(parts, span)
    cols = pieces[0].shape[1]
    for k in range(parts):
        wide[:, pl.ds(pl.multiple_of((me ^ k) * cols, cols), cols)] = pieces[k][...]
    sides = [split(wide[:, a * cols:(a + 2) * cols]) for a in range(0, parts, 2)]
    for at, (high, low) in enumerate(sides):
        high_ref[:, 2 * at * cols:2 * (at + 1) * cols] = high
        low_ref[:, 2 * at * cols:2 * (at + 1) * cols] = low
    where = {ab: j for j, ab in enumerate(cross_order(parts))}
    for a in range(0, parts, 2):
        for b in range(a + 2, parts, 2):
            prod = dot_parts(sides[a // 2], sides[b // 2], ((0,), (0,)))
            for i in range(2):
                for j in range(2):
                    at = where[a + i, b + j] * cols
                    flat[at:at + cols, :] = prod[i * cols:(i + 1) * cols, j * cols:(j + 1) * cols]
    give(owner, flat, send_ref, keep_ref)


def split(x):
    high = x.astype(jnp.bfloat16)
    return high, (x - high.astype(F32)).astype(jnp.bfloat16)


def dot(a, b, dims):
    return lax.dot_general(a, b, (dims, ((), ())), preferred_element_type=F32)


def dot_parts(a, b, dims=((1,), (0,))):
    (ah, al), (bh, bl) = a, b
    left = jnp.concatenate([ah, ah, al], axis=dims[0][0])
    return dot(left, jnp.concatenate([bh, bl, bh], axis=dims[1][0]), dims)


def split_dot(a, b, dims=((1,), (0,))):
    return dot_parts(split(a), split(b), dims)


def next_sign(y):
    whole_y = split(y)
    size = y.shape[0] // ROW_BLOCKS
    blocks = []
    for at in range(0, y.shape[0], size):
        square = dot_parts([part[at:at + size] for part in whole_y], whole_y)
        blocks.append(1.5 * y[at:at + size] - 0.5 * dot_parts(split(square), whole_y))
    return jnp.concatenate(blocks, axis=0)


def combine_of(grams):
    order = grams[0].shape[0]
    diagonal = lax.broadcasted_iota(jnp.int32, (order, order), 0) == lax.broadcasted_iota(jnp.int32, (order, order), 1)
    signs = []
    for gram in grams:
        mean = jnp.sum(jnp.where(diagonal, gram, 0.0)) / order
        shifted = jnp.where(diagonal, gram - mean, gram)
        signs.append(shifted / jnp.sqrt(jnp.sum(shifted * shifted, keepdims=True) + 1e-6))
    for _ in range(SIGN_STEPS):
        signs = [next_sign(y) for y in signs]
    half = order // 2
    combines = []
    for y in signs:
        projector = 0.5 * (jnp.where(diagonal, 1.0, 0.0) + y)
        combines.append(projector[:, :half] + projector[:, half:])
    return combines


def merge_kernel(parts, span, even_ref, odd_ref, high_ref, low_ref, *refs):
    outs, (weight_ref, product_ref, pairs, cross, turned) = refs[:parts], refs[parts:]
    me, owner = positions(parts, span)
    cols = even_ref.shape[2]
    pair_share, cross_share = pairs.shape[1] // (2 * span), cross.shape[0] // (parts * span)
    for k in range(parts * span):
        source = (odd_ref if k % 2 else even_ref).at[k // 2]
        there = owner ^ k
        place = there % 2 + 2 * (there // parts)
        at = pl.ds(pl.multiple_of(place * pair_share, 8), pair_share)
        pairs[(there % parts) // 2, at, :] = source[:pair_share, :]
        cross[pl.ds(pl.multiple_of(there * cross_share, 8), cross_share), :] = source[pair_share:, :]
    blocks = {ab: cross[j * cols:(j + 1) * cols, :] for j, ab in enumerate(cross_order(parts))}
    for p in range(parts // 2):
        for j, ab in enumerate(((2 * p, 2 * p), (2 * p, 2 * p + 1), (2 * p + 1, 2 * p + 1))):
            blocks[ab] = pairs[p, j * cols:(j + 1) * cols, :]
        product_ref[2 * p * cols:2 * (p + 1) * cols, :] = pairs[p, 3 * cols:, :]
    weights, count = None, parts
    while count > 1:
        grams = []
        for p in range(0, count, 2):
            low = jnp.concatenate([blocks[p, p], blocks[p, p + 1]], axis=1)
            high = jnp.concatenate([blocks[p, p + 1].T, blocks[p + 1, p + 1]], axis=1)
            grams.append(jnp.concatenate([low, high], axis=0))
        combines = combine_of(grams)
        if weights is None:
            weights = combines
        else:
            per = len(weights) // len(combines)
            weights = [
                split_dot(w, combines[i // per][(i % per) * cols:(i % per + 1) * cols, :])
                for i, w in enumerate(weights)
            ]
            weights = [jnp.concatenate(weights[i:i + per], axis=0) for i in range(0, len(weights), per)]
        merged = {}
        if count > 2:
            for p in range(count // 2):
                for q in range(p, count // 2):
                    if p == q:
                        cross = grams[p]
                    else:
                        cross = jnp.concatenate([
                            jnp.concatenate([blocks[2 * p + i, 2 * q], blocks[2 * p + i, 2 * q + 1]], axis=1)
                            for i in range(2)
                        ], axis=0)
                    right = split_dot(cross, combines[q])
                    merged[p, q] = split_dot(combines[p], right, ((0,), (0,)))
        blocks, count = merged, count // 2
    weight_ref[...] = weights[0]
    width = cols // parts
    turned[...] = dot_parts((high_ref[...], low_ref[...]), split(weights[0])).T
    for k in range(parts):
        outs[k][...] = turned[pl.ds(pl.multiple_of((me ^ k) * width, 8), width), :]


def coefficient_kernel(parts, weight_ref, product_ref, coef_ref, held):
    held[...] = split_dot(weight_ref[...], product_ref[...], ((0,), (0,)))
    width = coef_ref.shape[0]
    coef_ref[...] = held[pl.ds(pl.multiple_of(lax.axis_index("tm") * width, 8), width), :]


def final_kernel(parts, *refs):
    pieces, basis_ref = refs[:parts], refs[parts]
    me = lax.axis_index("tm")
    per, cells = basis_ref.shape[0] // parts, basis_ref.shape[2]
    for k in range(parts):
        base = (me ^ k) * per
        for i in range(per):
            basis_ref[base + i] = pieces[k][:, i * cells:(i + 1) * cells]


def shape(*dims):
    return jax.ShapeDtypeStruct(dims, F32)


def local(snapshots, land_mask, taps_rows, taps_cols, probes):
    rows, grid_cols, cols = snapshots.shape
    half_rows, half_cols = rows // 2, grid_cols // 2
    parts, patches = lax.axis_size("tm"), lax.axis_size("space")
    cells = half_rows * half_cols
    piece = cells // parts
    span = 2 if patches > 1 else 1

    snapshots, land_mask, taps_rows, taps_cols = (
        pltpu.with_memory_space_constraint(x, pltpu.HBM) for x in (snapshots, land_mask, taps_rows, taps_cols)
    )

    row_block, mask_block = (2, grid_cols, cols), (CHUNK, grid_cols)
    to_near, to_far = pl.pallas_call(
        edge_kernel,
        out_shape=[shape(half_cols, cols)] * 2,
        grid=(1,),
        in_specs=[
            scalars(), scalars(),
            pl.BlockSpec(row_block, lambda i: (0, 0, 0)),
            pl.BlockSpec(row_block, lambda i: (rows // 2 - 1, 0, 0)),
            pl.BlockSpec(mask_block, lambda i: (0, 0)),
            pl.BlockSpec(mask_block, lambda i: (rows // CHUNK - 1, 0)),
        ],
        out_specs=[pl.BlockSpec((half_cols, cols), lambda i: (0, 0))] * 2,
        scratch_shapes=[pltpu.VMEM((grid_cols, CHUNK), F32)],
        compiler_params=params(),
        name="edge",
    )(taps_rows, taps_cols, snapshots, snapshots, land_mask, land_mask)
    near = lax.ppermute(to_near, "space", [(i, i ^ 1) for i in range(patches) if i ^ 1 < patches])
    pairs = [(i, i + 1) for i in range(1, patches - 1, 2)]
    other = lax.ppermute(to_far, "space", pairs + [(j, i) for i, j in pairs])

    pieces = pl.pallas_call(
        functools.partial(filter_kernel, parts),
        out_shape=[shape(piece, cols)] * parts,
        in_specs=[scalars(), scalars(), pl.BlockSpec(memory_space=pltpu.HBM), whole()],
        out_specs=[whole()] * parts,
        scratch_shapes=[
            pltpu.VMEM((rows, grid_cols, cols), F32),
            pltpu.SemaphoreType.DMA((rows // CHUNK,)),
            pltpu.VMEM((grid_cols, rows), F32),
            pltpu.VMEM((rows, 2, half_cols, cols), F32),
            pltpu.VMEM((rows + 4, half_cols, cols), F32),
            pltpu.VMEM((cells, cols), F32),
        ],
        compiler_params=params(),
        cost_estimate=pl.CostEstimate(flops=0, bytes_accessed=4 * snapshots.size, transcendentals=0),
        name="filter",
    )(taps_rows, taps_cols, snapshots, land_mask)
    kept = pl.pallas_call(
        functools.partial(halo_kernel, parts),
        out_shape=[shape(piece, cols)] * parts,
        in_specs=[whole()] * (parts + 2),
        out_specs=[whole()] * parts,
        input_output_aliases={2 + k: k for k in range(parts)},
        compiler_params=params(),
        name="halo",
    )(near, other, *pieces)
    theirs = {k: swap(kept[k + 1], "tm", 1) for k in range(0, parts, 2)}
    far = {0: kept[0], 1: theirs[0]}
    for k in range(2, parts, 2):
        far[k] = swap(kept[k], "tm", k)
        far[k + 1] = swap(theirs[k], "tm", k)

    owners = 2 * span
    sums = pl.pallas_call(
        functools.partial(pair_kernel, parts, span),
        out_shape=[shape(5 * cols // owners, cols)] * owners,
        in_specs=[whole()] * (parts + 1),
        out_specs=[whole()] * owners,
        scratch_shapes=[
            pltpu.VMEM((cells // 2, 2 * cols), F32),
            pltpu.VMEM((cells // 2, cols), F32),
            pltpu.VMEM((5 * cols, cols), F32),
        ],
        compiler_params=params(),
        cost_estimate=pl.CostEstimate(flops=0, bytes_accessed=0, transcendentals=0),
        name="pair",
    )(probes.reshape(cells, cols), *[kept[k] for k in range(0, parts, 2)], *[theirs[k] for k in range(0, parts, 2)])
    got = [swap_both(sums[j], j % 2 + parts * (j // 2)) for j in range(1, owners)]
    tied = lax.optimization_barrier(got + [far[k] for k in range(2, parts)])
    got = tied[:owners - 1]
    far.update(zip(range(2, parts), tied[owners - 1:]))
    pair_share = sums[0]
    for x in got:
        pair_share = pair_share + x
    bits = [1 << b for b in range(1, patches.bit_length() - 1)]

    blocks = len(cross_order(parts))
    owners = parts * span
    size = blocks * cols // owners
    factors = jax.ShapeDtypeStruct((piece, parts * cols), jnp.bfloat16)
    send, keep, high, low = pl.pallas_call(
        functools.partial(cross_kernel, parts, span),
        out_shape=[shape(owners // 2, size, cols)] * 2 + [factors] * 2,
        in_specs=[whole()] * parts,
        out_specs=[whole()] * 4,
        scratch_shapes=[pltpu.VMEM((piece, parts * cols), F32), pltpu.VMEM((blocks * cols, cols), F32)],
        compiler_params=params(),
        cost_estimate=pl.CostEstimate(flops=0, bytes_accessed=0, transcendentals=0),
        name="cross",
    )(*[far[k] for k in range(parts)])
    got = swap(send, "tm", 1)
    mine = keep[0] + got[0]
    for h in range(1, owners // 2):
        mine = mine + swap_both(keep[h] + got[h], 2 * h)
    for bit in bits[:1]:
        pair_share = pair_share + swap(pair_share, "space", bit)
    mine, pair_share = lax.optimization_barrier((mine, pair_share))
    for bit in bits[:1]:
        mine = mine + swap(mine, "space", bit)
    mine = jnp.concatenate([pair_share, mine], axis=0)
    for bit in bits[1:]:
        mine = mine + swap(mine, "space", bit)
    even = jnp.stack([mine] + [swap_both(mine, 2 * h) for h in range(1, owners // 2)])
    odd = swap(even, "tm", 1)

    width = cols // parts
    *sent, weight, products = pl.pallas_call(
        functools.partial(merge_kernel, parts, span),
        out_shape=[shape(width, piece)] * parts + [shape(parts * cols, cols)] * 2,
        in_specs=[whole()] * 4,
        out_specs=[whole()] * (parts + 2),
        scratch_shapes=[
            pltpu.VMEM((parts // 2, 5 * cols, cols), F32),
            pltpu.VMEM((blocks * cols, cols), F32),
            pltpu.VMEM((cols, piece), F32),
        ],
        compiler_params=params(),
        name="merge",
    )(even, odd, high, low)
    coefficients = pl.pallas_call(
        functools.partial(coefficient_kernel, parts),
        out_shape=shape(width, cols),
        in_specs=[whole()] * 2,
        out_specs=whole(),
        scratch_shapes=[pltpu.VMEM((cols, cols), F32)],
        compiler_params=params(),
        name="coefficients",
    )(weight, products)
    last = [sent[0]] + [swap(sent[k], "tm", k) for k in range(1, parts)]

    basis = pl.pallas_call(
        functools.partial(final_kernel, parts),
        out_shape=shape(half_rows, width, half_cols),
        in_specs=[whole()] * parts,
        out_specs=whole(),
        compiler_params=params(),
        name="final",
    )(*last)
    return basis.transpose(0, 2, 1), coefficients


def solution(mesh):
    placed = (P("space", None, "tm"), P("space", None), P(), P(), P("space", None, None))
    return jax.shard_map(
        local,
        mesh=mesh,
        in_specs=placed,
        out_specs=(P("space", None, "tm"), P("tm", None)),
        check_vma=False,
    )
```

```python
import functools

import jax
import jax.numpy as jnp
from jax import lax
from jax.experimental import pallas as pl
from jax.experimental.pallas import tpu as pltpu
from jax.sharding import PartitionSpec as P

SIGN_STEPS = 8
TAPS = 6
CHUNK = 8
ROW_BLOCKS = 2
F32 = jnp.float32
VMEM_LIMIT = 48 * 1024 * 1024


def params():
    return pltpu.CompilerParams(vmem_limit_bytes=VMEM_LIMIT)


def whole():
    return pl.BlockSpec(memory_space=pltpu.VMEM)


def scalars():
    return pl.BlockSpec(memory_space=pltpu.SMEM)


def swap(x, axis, mask):
    count = lax.axis_size(axis)
    return lax.ppermute(x, axis, [(i, i ^ mask) for i in range(count)])


def swap_both(x, mask):
    parts, patches = lax.axis_size("tm"), lax.axis_size("space")
    route = []
    for t in range(parts):
        for s in range(patches):
            there = (t ^ (mask % parts)) * patches + (s ^ (mask // parts))
            route.append((t * patches + s, there))
    return lax.ppermute(x, ("tm", "space"), route)


def shift_rows(x, by):
    edge = jnp.zeros((1, x.shape[1]), x.dtype)
    if by > 0:
        return jnp.concatenate([edge, x[:-1]], axis=0)
    return jnp.concatenate([x[1:], edge], axis=0)


def mask_columns(mask, mask_t):
    mask_t[...] = mask.astype(F32).T
    half = mask.shape[1] // 2
    return mask_t[pl.ds(0, half, stride=2), :], mask_t[pl.ds(1, half, stride=2), :]


def narrowed_row(snaps, x, mask, taps):
    half = snaps.shape[1] // 2
    even = snaps[x, pl.ds(0, half, stride=2), :] * mask[0]
    odd = snaps[x, pl.ds(1, half, stride=2), :] * mask[1]
    before = taps[0] * even + taps[1] * odd
    here = taps[2] * even + taps[3] * odd
    after = taps[4] * even + taps[5] * odd
    return shift_rows(before, 1) + here + shift_rows(after, -1)


def edge_kernel(rtaps_ref, ctaps_ref, first_ref, last_ref, mask_first_ref, mask_last_ref, near_ref, far_ref, mask_t):
    ctaps = [ctaps_ref[k] for k in range(TAPS)]
    even = lax.axis_index("space") % 2 == 0
    shares = []
    for snaps, mask_ref, taps, at in (
        (first_ref, mask_first_ref, (rtaps_ref[4], rtaps_ref[5]), 0),
        (last_ref, mask_last_ref, (rtaps_ref[0], rtaps_ref[1]), CHUNK - 2),
    ):
        masks = mask_columns(mask_ref[...], mask_t)
        rows = [narrowed_row(snaps, x, [m[:, at + x:at + x + 1] for m in masks], ctaps) for x in range(2)]
        shares.append(taps[0] * rows[0] + taps[1] * rows[1])
    up, down = shares
    near_ref[...] = jnp.where(even, down, up)
    far_ref[...] = jnp.where(even, up, down)


def filter_kernel(parts, rtaps_ref, ctaps_ref, snap_hbm, mask_ref, *rest):
    pieces, (snaps, sems, mask_t, spread, narrowed, filtered) = rest[:parts], rest[parts:]
    rows, cells = narrowed.shape[0] - 4, narrowed.shape[1]
    me = lax.axis_index("tm")
    chunks = rows // CHUNK

    def fetch(c):
        at = pl.ds(c * CHUNK, CHUNK)
        return pltpu.make_async_copy(snap_hbm.at[at], snaps.at[at], sems.at[c])

    for c in range(chunks):
        fetch(c).start()

    rtaps = [rtaps_ref[k] for k in range(TAPS)]
    ctaps = [ctaps_ref[k] for k in range(TAPS)]
    edge = jnp.zeros((2,) + narrowed.shape[1:], F32)
    narrowed[0:2] = edge
    narrowed[rows + 2:rows + 4] = edge

    masks = mask_columns(mask_ref[...], mask_t)
    for x in range(rows):
        for j, mask in enumerate(masks):
            spread[x, j] = jnp.broadcast_to(mask[:, x:x + 1], (cells, narrowed.shape[2]))

    def narrow(c, carry):
        fetch(c).wait()
        base = pl.multiple_of(c * CHUNK, CHUNK)
        for x in range(CHUNK):
            row = narrowed_row(snaps, base + x, spread[base + x], ctaps)
            narrowed[base + 2 + x] = row
        return carry

    lax.fori_loop(0, chunks, narrow, 0)
    for i in range(rows // 2):
        total = rtaps[0] * narrowed[2 * i]
        for k in range(1, TAPS):
            total = total + rtaps[k] * narrowed[2 * i + k]
        filtered[i * cells:(i + 1) * cells, :] = total
    size = filtered.shape[0] // parts
    for k in range(parts):
        pieces[k][...] = filtered[pl.ds(pl.multiple_of((me ^ k) * size, 8), size), :]


def halo_kernel(parts, near_ref, far_ref, *refs):
    outs = refs[len(refs) // 2:]
    me = lax.axis_index("tm")
    cells = near_ref.shape[0]
    even = lax.axis_index("space") % 2 == 0
    above = jnp.where(even, far_ref[...], near_ref[...])
    below = jnp.where(even, near_ref[...], far_ref[...])
    for k, out in enumerate(outs):
        out[...] = refs[k][...]

        @pl.when((me ^ k) == 0)
        def _():
            out[:cells, :] = out[:cells, :] + above

        @pl.when((me ^ k) == parts - 1)
        def _():
            out[-cells:, :] = out[-cells:, :] + below


def cross_order(parts):
    return [(a, b) for p in range(0, parts, 2) for q in range(p + 2, parts, 2) for a in (p, p + 1) for b in (q, q + 1)]


def triangle(size):
    return tuple(lax.broadcasted_iota(jnp.int32, (size, size), axis) for axis in range(2))


def pair_rows(cols, owners):
    return 4 * cols + 8 * owners


def pair_kernel(parts, span, probes_ref, *refs):
    half = parts // 2
    owners = 2 * span
    mine, theirs, refs = refs[:half], refs[half:2 * half], refs[2 * half:]
    outs, (wide, there, flat) = refs[:owners], refs[owners:]
    me, owner = positions(2, span)
    size, cols = mine[0].shape
    low = pl.ds(pl.multiple_of((me % 2) * cols, cols), cols)
    high = pl.ds(pl.multiple_of((1 - me % 2) * cols, cols), cols)
    for h in range(half):
        at = pl.ds(h * size, size)
        wide[at, low] = mine[h][...]
        wide[at, high] = theirs[h][...]
        there[at, :] = probes_ref[pl.ds(pl.multiple_of((me ^ 2 * h) * size, 8), size), :]
    left = split(wide[...])
    gram = dot_parts(left, left, ((0,), (0,)))
    first, second = gram[:cols, :cols], gram[cols:, cols:]
    row, col = triangle(cols)
    flat[:cols, :] = gram[:cols, cols:]
    flat[cols:2 * cols, :] = jnp.where(row <= col, first, second)
    flat[2 * cols:4 * cols, :] = dot_parts(left, split(there[...]), ((0,), (0,)))
    diagonal = jnp.sum(jnp.where(row == col, second, 0.0), axis=0, keepdims=True)
    flat[4 * cols:, :] = jnp.broadcast_to(diagonal, (flat.shape[0] - 4 * cols, cols))
    share = flat.shape[0] // owners
    for k, out in enumerate(outs):
        out[...] = flat[pl.ds(pl.multiple_of((owner ^ k) * share, 8), share), :]


def positions(count, span):
    me = lax.axis_index("tm")
    return me, me % count + count * (lax.axis_index("space") % span)


def give(owner, flat, send_ref, keep_ref):
    count = 2 * send_ref.shape[0]
    share = flat.shape[0] // count
    for k in range(count):
        out = send_ref if k % 2 else keep_ref
        out[k // 2] = flat[pl.ds(pl.multiple_of((owner ^ k) * share, 8), share), :]


def cross_kernel(parts, span, *refs):
    pieces, (send_ref, keep_ref, high_ref, low_ref, wide, flat) = refs[:parts], refs[parts:]
    me, owner = positions(parts, span)
    cols = pieces[0].shape[1]
    for k in range(parts):
        wide[:, pl.ds(pl.multiple_of((me ^ k) * cols, cols), cols)] = pieces[k][...]
    sides = [split(wide[:, a * cols:(a + 2) * cols]) for a in range(0, parts, 2)]
    for at, (high, low) in enumerate(sides):
        high_ref[:, 2 * at * cols:2 * (at + 1) * cols] = high
        low_ref[:, 2 * at * cols:2 * (at + 1) * cols] = low
    where = {ab: j for j, ab in enumerate(cross_order(parts))}
    for a in range(0, parts, 2):
        for b in range(a + 2, parts, 2):
            prod = dot_parts(sides[a // 2], sides[b // 2], ((0,), (0,)))
            for i in range(2):
                for j in range(2):
                    at = where[a + i, b + j] * cols
                    flat[at:at + cols, :] = prod[i * cols:(i + 1) * cols, j * cols:(j + 1) * cols]
    give(owner, flat, send_ref, keep_ref)


def split(x):
    high = x.astype(jnp.bfloat16)
    return high, (x - high.astype(F32)).astype(jnp.bfloat16)


def dot(a, b, dims):
    return lax.dot_general(a, b, (dims, ((), ())), preferred_element_type=F32)


def dot_parts(a, b, dims=((1,), (0,))):
    (ah, al), (bh, bl) = a, b
    left = jnp.concatenate([ah, ah, al], axis=dims[0][0])
    return dot(left, jnp.concatenate([bh, bl, bh], axis=dims[1][0]), dims)


def split_dot(a, b, dims=((1,), (0,))):
    return dot_parts(split(a), split(b), dims)


def next_sign(y):
    whole_y = split(y)
    size = y.shape[0] // ROW_BLOCKS
    blocks = []
    for at in range(0, y.shape[0], size):
        square = dot_parts([part[at:at + size] for part in whole_y], whole_y)
        blocks.append(1.5 * y[at:at + size] - 0.5 * dot_parts(split(square), whole_y))
    return jnp.concatenate(blocks, axis=0)


def combine_of(grams):
    order = grams[0].shape[0]
    diagonal = lax.broadcasted_iota(jnp.int32, (order, order), 0) == lax.broadcasted_iota(jnp.int32, (order, order), 1)
    signs = []
    for gram in grams:
        mean = jnp.sum(jnp.where(diagonal, gram, 0.0)) / order
        shifted = jnp.where(diagonal, gram - mean, gram)
        signs.append(shifted / jnp.sqrt(jnp.sum(shifted * shifted, keepdims=True) + 1e-6))
    for _ in range(SIGN_STEPS):
        signs = [next_sign(y) for y in signs]
    half = order // 2
    combines = []
    for y in signs:
        projector = 0.5 * (jnp.where(diagonal, 1.0, 0.0) + y)
        combines.append(projector[:, :half] + projector[:, half:])
    return combines


def merge_kernel(parts, span, even_ref, odd_ref, high_ref, low_ref, *refs):
    outs, (weight_ref, product_ref, pairs, cross, turned) = refs[:parts], refs[parts:]
    me, owner = positions(parts, span)
    cols = even_ref.shape[2]
    pair_share, cross_share = pairs.shape[1] // (2 * span), cross.shape[0] // (parts * span)
    for k in range(parts * span):
        source = (odd_ref if k % 2 else even_ref).at[k // 2]
        there = owner ^ k
        place = there % 2 + 2 * (there // parts)
        at = pl.ds(pl.multiple_of(place * pair_share, 8), pair_share)
        pairs[(there % parts) // 2, at, :] = source[:pair_share, :]
        cross[pl.ds(pl.multiple_of(there * cross_share, 8), cross_share), :] = source[pair_share:, :]
    blocks = {ab: cross[j * cols:(j + 1) * cols, :] for j, ab in enumerate(cross_order(parts))}
    row, col = triangle(cols)
    for p in range(parts // 2):
        packed = pairs[p, cols:2 * cols, :]
        turned_back = packed.T
        blocks[2 * p, 2 * p] = jnp.where(row <= col, packed, turned_back)
        blocks[2 * p, 2 * p + 1] = pairs[p, :cols, :]
        second = jnp.where(row > col, packed, turned_back)
        blocks[2 * p + 1, 2 * p + 1] = jnp.where(row == col, pairs[p, 4 * cols:4 * cols + 1, :], second)
        product_ref[2 * p * cols:2 * (p + 1) * cols, :] = pairs[p, 2 * cols:4 * cols, :]
    weights, count = None, parts
    while count > 1:
        grams = []
        for p in range(0, count, 2):
            low = jnp.concatenate([blocks[p, p], blocks[p, p + 1]], axis=1)
            high = jnp.concatenate([blocks[p, p + 1].T, blocks[p + 1, p + 1]], axis=1)
            grams.append(jnp.concatenate([low, high], axis=0))
        combines = combine_of(grams)
        if weights is None:
            weights = combines
        else:
            per = len(weights) // len(combines)
            weights = [
                split_dot(w, combines[i // per][(i % per) * cols:(i % per + 1) * cols, :])
                for i, w in enumerate(weights)
            ]
            weights = [jnp.concatenate(weights[i:i + per], axis=0) for i in range(0, len(weights), per)]
        merged = {}
        if count > 2:
            for p in range(count // 2):
                for q in range(p, count // 2):
                    if p == q:
                        cross = grams[p]
                    else:
                        cross = jnp.concatenate([
                            jnp.concatenate([blocks[2 * p + i, 2 * q], blocks[2 * p + i, 2 * q + 1]], axis=1)
                            for i in range(2)
                        ], axis=0)
                    right = split_dot(cross, combines[q])
                    merged[p, q] = split_dot(combines[p], right, ((0,), (0,)))
        blocks, count = merged, count // 2
    weight_ref[...] = weights[0]
    width = cols // parts
    turned[...] = dot_parts((high_ref[...], low_ref[...]), split(weights[0])).T
    for k in range(parts):
        outs[k][...] = turned[pl.ds(pl.multiple_of((me ^ k) * width, 8), width), :]


def coefficient_kernel(parts, weight_ref, product_ref, coef_ref, held):
    held[...] = split_dot(weight_ref[...], product_ref[...], ((0,), (0,)))
    width = coef_ref.shape[0]
    coef_ref[...] = held[pl.ds(pl.multiple_of(lax.axis_index("tm") * width, 8), width), :]


def final_kernel(parts, *refs):
    pieces, basis_ref = refs[:parts], refs[parts]
    me = lax.axis_index("tm")
    per, cells = basis_ref.shape[0] // parts, basis_ref.shape[2]
    for k in range(parts):
        base = (me ^ k) * per
        for i in range(per):
            basis_ref[base + i] = pieces[k][:, i * cells:(i + 1) * cells]


def shape(*dims):
    return jax.ShapeDtypeStruct(dims, F32)


def local(snapshots, land_mask, taps_rows, taps_cols, probes):
    rows, grid_cols, cols = snapshots.shape
    half_rows, half_cols = rows // 2, grid_cols // 2
    parts, patches = lax.axis_size("tm"), lax.axis_size("space")
    cells = half_rows * half_cols
    piece = cells // parts
    span = 2 if patches > 1 else 1

    snapshots, land_mask, taps_rows, taps_cols = (
        pltpu.with_memory_space_constraint(x, pltpu.HBM) for x in (snapshots, land_mask, taps_rows, taps_cols)
    )

    row_block, mask_block = (2, grid_cols, cols), (CHUNK, grid_cols)
    to_near, to_far = pl.pallas_call(
        edge_kernel,
        out_shape=[shape(half_cols, cols)] * 2,
        grid=(1,),
        in_specs=[
            scalars(), scalars(),
            pl.BlockSpec(row_block, lambda i: (0, 0, 0)),
            pl.BlockSpec(row_block, lambda i: (rows // 2 - 1, 0, 0)),
            pl.BlockSpec(mask_block, lambda i: (0, 0)),
            pl.BlockSpec(mask_block, lambda i: (rows // CHUNK - 1, 0)),
        ],
        out_specs=[pl.BlockSpec((half_cols, cols), lambda i: (0, 0))] * 2,
        scratch_shapes=[pltpu.VMEM((grid_cols, CHUNK), F32)],
        compiler_params=params(),
        name="edge",
    )(taps_rows, taps_cols, snapshots, snapshots, land_mask, land_mask)
    near = lax.ppermute(to_near, "space", [(i, i ^ 1) for i in range(patches) if i ^ 1 < patches])
    pairs = [(i, i + 1) for i in range(1, patches - 1, 2)]
    other = lax.ppermute(to_far, "space", pairs + [(j, i) for i, j in pairs])

    pieces = pl.pallas_call(
        functools.partial(filter_kernel, parts),
        out_shape=[shape(piece, cols)] * parts,
        in_specs=[scalars(), scalars(), pl.BlockSpec(memory_space=pltpu.HBM), whole()],
        out_specs=[whole()] * parts,
        scratch_shapes=[
            pltpu.VMEM((rows, grid_cols, cols), F32),
            pltpu.SemaphoreType.DMA((rows // CHUNK,)),
            pltpu.VMEM((grid_cols, rows), F32),
            pltpu.VMEM((rows, 2, half_cols, cols), F32),
            pltpu.VMEM((rows + 4, half_cols, cols), F32),
            pltpu.VMEM((cells, cols), F32),
        ],
        compiler_params=params(),
        cost_estimate=pl.CostEstimate(flops=0, bytes_accessed=4 * snapshots.size, transcendentals=0),
        name="filter",
    )(taps_rows, taps_cols, snapshots, land_mask)
    kept = pl.pallas_call(
        functools.partial(halo_kernel, parts),
        out_shape=[shape(piece, cols)] * parts,
        in_specs=[whole()] * (parts + 2),
        out_specs=[whole()] * parts,
        input_output_aliases={2 + k: k for k in range(parts)},
        compiler_params=params(),
        name="halo",
    )(near, other, *pieces)
    theirs = {k: swap(kept[k + 1], "tm", 1) for k in range(0, parts, 2)}
    far = {0: kept[0], 1: theirs[0]}
    for k in range(2, parts, 2):
        far[k] = swap(kept[k], "tm", k)
        far[k + 1] = swap(theirs[k], "tm", k)

    owners = 2 * span
    sums = pl.pallas_call(
        functools.partial(pair_kernel, parts, span),
        out_shape=[shape(pair_rows(cols, owners) // owners, cols)] * owners,
        in_specs=[whole()] * (parts + 1),
        out_specs=[whole()] * owners,
        scratch_shapes=[
            pltpu.VMEM((cells // 2, 2 * cols), F32),
            pltpu.VMEM((cells // 2, cols), F32),
            pltpu.VMEM((pair_rows(cols, owners), cols), F32),
        ],
        compiler_params=params(),
        cost_estimate=pl.CostEstimate(flops=0, bytes_accessed=0, transcendentals=0),
        name="pair",
    )(probes.reshape(cells, cols), *[kept[k] for k in range(0, parts, 2)], *[theirs[k] for k in range(0, parts, 2)])
    got = [swap_both(sums[j], j % 2 + parts * (j // 2)) for j in range(1, owners)]
    tied = lax.optimization_barrier(got + [far[k] for k in range(2, parts)])
    got = tied[:owners - 1]
    far.update(zip(range(2, parts), tied[owners - 1:]))
    pair_share = sums[0]
    for x in got:
        pair_share = pair_share + x
    bits = [1 << b for b in range(1, patches.bit_length() - 1)]

    blocks = len(cross_order(parts))
    owners = parts * span
    size = blocks * cols // owners
    factors = jax.ShapeDtypeStruct((piece, parts * cols), jnp.bfloat16)
    send, keep, high, low = pl.pallas_call(
        functools.partial(cross_kernel, parts, span),
        out_shape=[shape(owners // 2, size, cols)] * 2 + [factors] * 2,
        in_specs=[whole()] * parts,
        out_specs=[whole()] * 4,
        scratch_shapes=[pltpu.VMEM((piece, parts * cols), F32), pltpu.VMEM((blocks * cols, cols), F32)],
        compiler_params=params(),
        cost_estimate=pl.CostEstimate(flops=0, bytes_accessed=0, transcendentals=0),
        name="cross",
    )(*[far[k] for k in range(parts)])
    got = swap(send, "tm", 1)
    mine = keep[0] + got[0]
    for h in range(1, owners // 2):
        mine = mine + swap_both(keep[h] + got[h], 2 * h)
    for bit in bits[:1]:
        pair_share = pair_share + swap(pair_share, "space", bit)
    mine, pair_share = lax.optimization_barrier((mine, pair_share))
    for bit in bits[:1]:
        mine = mine + swap(mine, "space", bit)
    mine = jnp.concatenate([pair_share, mine], axis=0)
    for bit in bits[1:]:
        mine = mine + swap(mine, "space", bit)
    even = jnp.stack([mine] + [swap_both(mine, 2 * h) for h in range(1, owners // 2)])
    odd = swap(even, "tm", 1)

    width = cols // parts
    *sent, weight, products = pl.pallas_call(
        functools.partial(merge_kernel, parts, span),
        out_shape=[shape(width, piece)] * parts + [shape(parts * cols, cols)] * 2,
        in_specs=[whole()] * 4,
        out_specs=[whole()] * (parts + 2),
        scratch_shapes=[
            pltpu.VMEM((parts // 2, pair_rows(cols, 2 * span), cols), F32),
            pltpu.VMEM((blocks * cols, cols), F32),
            pltpu.VMEM((cols, piece), F32),
        ],
        compiler_params=params(),
        name="merge",
    )(even, odd, high, low)
    coefficients = pl.pallas_call(
        functools.partial(coefficient_kernel, parts),
        out_shape=shape(width, cols),
        in_specs=[whole()] * 2,
        out_specs=whole(),
        scratch_shapes=[pltpu.VMEM((cols, cols), F32)],
        compiler_params=params(),
        name="coefficients",
    )(weight, products)
    last = [sent[0]] + [swap(sent[k], "tm", k) for k in range(1, parts)]

    basis = pl.pallas_call(
        functools.partial(final_kernel, parts),
        out_shape=shape(half_rows, width, half_cols),
        in_specs=[whole()] * parts,
        out_specs=whole(),
        compiler_params=params(),
        name="final",
    )(*last)
    return basis.transpose(0, 2, 1), coefficients


def solution(mesh):
    placed = (P("space", None, "tm"), P("space", None), P(), P(), P("space", None, None))
    return jax.shard_map(
        local,
        mesh=mesh,
        in_specs=placed,
        out_specs=(P("space", None, "tm"), P("tm", None)),
        check_vma=False,
    )
```

```python
import functools

import jax
import jax.numpy as jnp
from jax import lax
from jax.experimental import pallas as pl
from jax.experimental.pallas import tpu as pltpu
from jax.sharding import PartitionSpec as P

SIGN_STEPS = 8
TAPS = 6
CHUNK = 8
ROW_BLOCKS = 2
F32 = jnp.float32
VMEM_LIMIT = 48 * 1024 * 1024


def params():
    return pltpu.CompilerParams(vmem_limit_bytes=VMEM_LIMIT)


def whole():
    return pl.BlockSpec(memory_space=pltpu.VMEM)


def scalars():
    return pl.BlockSpec(memory_space=pltpu.SMEM)


def swap(x, axis, mask):
    count = lax.axis_size(axis)
    return lax.ppermute(x, axis, [(i, i ^ mask) for i in range(count)])


def swap_both(x, mask):
    parts, patches = lax.axis_size("tm"), lax.axis_size("space")
    route = []
    for t in range(parts):
        for s in range(patches):
            there = (t ^ (mask % parts)) * patches + (s ^ (mask // parts))
            route.append((t * patches + s, there))
    return lax.ppermute(x, ("tm", "space"), route)


def shift_rows(x, by):
    edge = jnp.zeros((1, x.shape[1]), x.dtype)
    if by > 0:
        return jnp.concatenate([edge, x[:-1]], axis=0)
    return jnp.concatenate([x[1:], edge], axis=0)


def mask_columns(mask, mask_t):
    mask_t[...] = mask.astype(F32).T
    half = mask.shape[1] // 2
    return mask_t[pl.ds(0, half, stride=2), :], mask_t[pl.ds(1, half, stride=2), :]


def narrowed_row(snaps, x, mask, taps):
    half = snaps.shape[1] // 2
    even = snaps[x, pl.ds(0, half, stride=2), :] * mask[0]
    odd = snaps[x, pl.ds(1, half, stride=2), :] * mask[1]
    before = taps[0] * even + taps[1] * odd
    here = taps[2] * even + taps[3] * odd
    after = taps[4] * even + taps[5] * odd
    return shift_rows(before, 1) + here + shift_rows(after, -1)


def edge_kernel(rtaps_ref, ctaps_ref, first_ref, last_ref, mask_first_ref, mask_last_ref, near_ref, far_ref, mask_t):
    ctaps = [ctaps_ref[k] for k in range(TAPS)]
    even = lax.axis_index("space") % 2 == 0
    shares = []
    for snaps, mask_ref, taps, at in (
        (first_ref, mask_first_ref, (rtaps_ref[4], rtaps_ref[5]), 0),
        (last_ref, mask_last_ref, (rtaps_ref[0], rtaps_ref[1]), CHUNK - 2),
    ):
        masks = mask_columns(mask_ref[...], mask_t)
        rows = [narrowed_row(snaps, x, [m[:, at + x:at + x + 1] for m in masks], ctaps) for x in range(2)]
        shares.append(taps[0] * rows[0] + taps[1] * rows[1])
    up, down = shares
    near_ref[...] = jnp.where(even, down, up)
    far_ref[...] = jnp.where(even, up, down)


def filter_kernel(parts, rtaps_ref, ctaps_ref, snap_hbm, mask_ref, *rest):
    pieces, (snaps, sems, mask_t, spread, narrowed, filtered) = rest[:parts], rest[parts:]
    rows, cells = narrowed.shape[0] - 4, narrowed.shape[1]
    me = lax.axis_index("tm")
    chunks = rows // CHUNK

    def fetch(c):
        at = pl.ds(c * CHUNK, CHUNK)
        return pltpu.make_async_copy(snap_hbm.at[at], snaps.at[at], sems.at[c])

    for c in range(chunks):
        fetch(c).start()

    rtaps = [rtaps_ref[k] for k in range(TAPS)]
    ctaps = [ctaps_ref[k] for k in range(TAPS)]
    edge = jnp.zeros((2,) + narrowed.shape[1:], F32)
    narrowed[0:2] = edge
    narrowed[rows + 2:rows + 4] = edge

    masks = mask_columns(mask_ref[...], mask_t)
    for x in range(rows):
        for j, mask in enumerate(masks):
            spread[x, j] = jnp.broadcast_to(mask[:, x:x + 1], (cells, narrowed.shape[2]))

    def narrow(c, carry):
        fetch(c).wait()
        base = pl.multiple_of(c * CHUNK, CHUNK)
        for x in range(CHUNK):
            row = narrowed_row(snaps, base + x, spread[base + x], ctaps)
            narrowed[base + 2 + x] = row
        return carry

    lax.fori_loop(0, chunks, narrow, 0)
    for i in range(rows // 2):
        total = rtaps[0] * narrowed[2 * i]
        for k in range(1, TAPS):
            total = total + rtaps[k] * narrowed[2 * i + k]
        filtered[i * cells:(i + 1) * cells, :] = total
    size = filtered.shape[0] // parts
    for k in range(parts):
        pieces[k][...] = filtered[pl.ds(pl.multiple_of((me ^ k) * size, 8), size), :]


def halo_kernel(parts, near_ref, far_ref, *refs):
    outs = refs[len(refs) // 2:]
    me = lax.axis_index("tm")
    cells = near_ref.shape[0]
    even = lax.axis_index("space") % 2 == 0
    above = jnp.where(even, far_ref[...], near_ref[...])
    below = jnp.where(even, near_ref[...], far_ref[...])
    for k, out in enumerate(outs):
        out[...] = refs[k][...]

        @pl.when((me ^ k) == 0)
        def _():
            out[:cells, :] = out[:cells, :] + above

        @pl.when((me ^ k) == parts - 1)
        def _():
            out[-cells:, :] = out[-cells:, :] + below


def cross_order(parts):
    return [(a, b) for p in range(0, parts, 2) for q in range(p + 2, parts, 2) for a in (p, p + 1) for b in (q, q + 1)]


def triangle(size):
    return tuple(lax.broadcasted_iota(jnp.int32, (size, size), axis) for axis in range(2))


def pair_rows(cols, owners):
    return 4 * cols + 8 * owners


def pair_kernel(parts, span, probes_ref, *refs):
    half = parts // 2
    owners = 2 * span
    mine, theirs, refs = refs[:half], refs[half:2 * half], refs[2 * half:]
    outs, (wide, there, flat) = refs[:owners], refs[owners:]
    me, owner = positions(2, span)
    size, cols = mine[0].shape
    low = pl.ds(pl.multiple_of((me % 2) * cols, cols), cols)
    high = pl.ds(pl.multiple_of((1 - me % 2) * cols, cols), cols)
    for h in range(half):
        at = pl.ds(h * size, size)
        wide[at, low] = mine[h][...]
        wide[at, high] = theirs[h][...]
        there[at, :] = probes_ref[pl.ds(pl.multiple_of((me ^ 2 * h) * size, 8), size), :]
    left = split(wide[...])
    gram = dot_parts(left, left, ((0,), (0,)))
    first, second = gram[:cols, :cols], gram[cols:, cols:]
    row, col = triangle(cols)
    flat[:cols, :] = gram[:cols, cols:]
    flat[cols:2 * cols, :] = jnp.where(row <= col, first, second)
    flat[2 * cols:4 * cols, :] = dot_parts(left, split(there[...]), ((0,), (0,)))
    diagonal = jnp.sum(jnp.where(row == col, second, 0.0), axis=0, keepdims=True)
    flat[4 * cols:, :] = jnp.broadcast_to(diagonal, (flat.shape[0] - 4 * cols, cols))
    share = flat.shape[0] // owners
    for k, out in enumerate(outs):
        out[...] = flat[pl.ds(pl.multiple_of((owner ^ k) * share, 8), share), :]


def positions(count, span):
    me = lax.axis_index("tm")
    return me, me % count + count * (lax.axis_index("space") % span)


def give(owner, flat, send_ref, keep_ref):
    count = 2 * send_ref.shape[0]
    share = flat.shape[0] // count
    for k in range(count):
        out = send_ref if k % 2 else keep_ref
        out[k // 2] = flat[pl.ds(pl.multiple_of((owner ^ k) * share, 8), share), :]


def cross_kernel(parts, span, *refs):
    pieces, (send_ref, keep_ref, high_ref, low_ref, wide, flat) = refs[:parts], refs[parts:]
    me, owner = positions(parts, span)
    cols = pieces[0].shape[1]
    for k in range(parts):
        wide[:, pl.ds(pl.multiple_of((me ^ k) * cols, cols), cols)] = pieces[k][...]
    sides = [split(wide[:, a * cols:(a + 2) * cols]) for a in range(0, parts, 2)]
    for at, (high, low) in enumerate(sides):
        high_ref[:, 2 * at * cols:2 * (at + 1) * cols] = high
        low_ref[:, 2 * at * cols:2 * (at + 1) * cols] = low
    where = {ab: j for j, ab in enumerate(cross_order(parts))}
    for a in range(0, parts, 2):
        for b in range(a + 2, parts, 2):
            prod = dot_parts(sides[a // 2], sides[b // 2], ((0,), (0,)))
            for i in range(2):
                for j in range(2):
                    at = where[a + i, b + j] * cols
                    flat[at:at + cols, :] = prod[i * cols:(i + 1) * cols, j * cols:(j + 1) * cols]
    give(owner, flat, send_ref, keep_ref)


def split(x):
    high = x.astype(jnp.bfloat16)
    return high, (x - high.astype(F32)).astype(jnp.bfloat16)


def dot(a, b, dims):
    return lax.dot_general(a, b, (dims, ((), ())), preferred_element_type=F32)


def dot_parts(a, b, dims=((1,), (0,))):
    (ah, al), (bh, bl) = a, b
    left = jnp.concatenate([ah, ah, al], axis=dims[0][0])
    return dot(left, jnp.concatenate([bh, bl, bh], axis=dims[1][0]), dims)


def split_dot(a, b, dims=((1,), (0,))):
    return dot_parts(split(a), split(b), dims)


def next_sign(y):
    whole_y = split(y)
    size = y.shape[0] // ROW_BLOCKS
    blocks = []
    for at in range(0, y.shape[0], size):
        square = dot_parts([part[at:at + size] for part in whole_y], whole_y)
        blocks.append(1.5 * y[at:at + size] - 0.5 * dot_parts(split(square), whole_y))
    return jnp.concatenate(blocks, axis=0)


def combine_of(grams):
    order = grams[0].shape[0]
    diagonal = lax.broadcasted_iota(jnp.int32, (order, order), 0) == lax.broadcasted_iota(jnp.int32, (order, order), 1)
    signs = []
    for gram in grams:
        mean = jnp.sum(jnp.where(diagonal, gram, 0.0)) / order
        shifted = jnp.where(diagonal, gram - mean, gram)
        signs.append(shifted / jnp.sqrt(jnp.sum(shifted * shifted, keepdims=True) + 1e-6))
    for _ in range(SIGN_STEPS):
        signs = [next_sign(y) for y in signs]
    half = order // 2
    combines = []
    for y in signs:
        projector = 0.5 * (jnp.where(diagonal, 1.0, 0.0) + y)
        combines.append(projector[:, :half] + projector[:, half:])
    return combines


def place_shares(parts, span, even_ref, odd_ref, put):
    _, owner = positions(parts, span)
    for k in range(parts * span):
        put(owner ^ k, (odd_ref if k % 2 else even_ref)[k // 2])


def level_kernel(parts, span, even_ref, odd_ref, combine_ref, square_ref, product_ref, pairs):
    cols = even_ref.shape[2]
    share = pairs.shape[1] // (2 * span)

    def put(there, rows):
        place = there % 2 + 2 * (there // parts)
        pairs[(there % parts) // 2, pl.ds(pl.multiple_of(place * share, 8), share), :] = rows

    place_shares(parts, span, even_ref, odd_ref, put)
    row, col = triangle(cols)
    grams = []
    for p in range(parts // 2):
        packed = pairs[p, cols:2 * cols, :]
        turned_back = packed.T
        first = jnp.where(row <= col, packed, turned_back)
        between = pairs[p, :cols, :]
        second = jnp.where(row > col, packed, turned_back)
        second = jnp.where(row == col, pairs[p, 4 * cols:4 * cols + 1, :], second)
        grams.append(jnp.concatenate([
            jnp.concatenate([first, between], axis=1), jnp.concatenate([between.T, second], axis=1)
        ], axis=0))
        product_ref[2 * p * cols:2 * (p + 1) * cols, :] = pairs[p, 2 * cols:4 * cols, :]
    for p, (gram, combine) in enumerate(zip(grams, combine_of(grams))):
        combine_ref[p] = combine
        square_ref[p] = split_dot(combine, split_dot(gram, combine), ((0,), (0,)))


def merge_kernel(parts, span, even_ref, odd_ref, combine_ref, square_ref, high_ref, low_ref, *refs):
    outs, (weight_ref, cross, turned) = refs[:parts], refs[parts:]
    me = lax.axis_index("tm")
    cols = even_ref.shape[2]
    share = cross.shape[0] // (parts * span)

    def put(there, rows):
        cross[pl.ds(pl.multiple_of(there * share, 8), share), :] = rows

    place_shares(parts, span, even_ref, odd_ref, put)
    where = {ab: j * cols for j, ab in enumerate(cross_order(parts))}
    weights = [combine_ref[p] for p in range(parts // 2)]
    blocks = {(p, p): square_ref[p] for p in range(parts // 2)}
    for p in range(parts // 2):
        for q in range(p + 1, parts // 2):
            between = jnp.concatenate([
                jnp.concatenate([cross[where[a, b]:where[a, b] + cols, :] for b in (2 * q, 2 * q + 1)], axis=1)
                for a in (2 * p, 2 * p + 1)
            ], axis=0)
            blocks[p, q] = split_dot(weights[p], split_dot(between, weights[q]), ((0,), (0,)))
    count = parts // 2
    while count > 1:
        grams = []
        for p in range(0, count, 2):
            low = jnp.concatenate([blocks[p, p], blocks[p, p + 1]], axis=1)
            high = jnp.concatenate([blocks[p, p + 1].T, blocks[p + 1, p + 1]], axis=1)
            grams.append(jnp.concatenate([low, high], axis=0))
        combines = combine_of(grams)
        per = len(weights) // len(combines)
        weights = [
            split_dot(w, combines[i // per][(i % per) * cols:(i % per + 1) * cols, :])
            for i, w in enumerate(weights)
        ]
        weights = [jnp.concatenate(weights[i:i + per], axis=0) for i in range(0, len(weights), per)]
        merged = {}
        if count > 2:
            for p in range(count // 2):
                for q in range(p, count // 2):
                    if p == q:
                        between = grams[p]
                    else:
                        between = jnp.concatenate([
                            jnp.concatenate([blocks[2 * p + i, 2 * q], blocks[2 * p + i, 2 * q + 1]], axis=1)
                            for i in range(2)
                        ], axis=0)
                    right = split_dot(between, combines[q])
                    merged[p, q] = split_dot(combines[p], right, ((0,), (0,)))
        blocks, count = merged, count // 2
    weight_ref[...] = weights[0]
    width = cols // parts
    turned[...] = dot_parts((high_ref[...], low_ref[...]), split(weights[0])).T
    for k in range(parts):
        outs[k][...] = turned[pl.ds(pl.multiple_of((me ^ k) * width, 8), width), :]


def coefficient_kernel(parts, weight_ref, product_ref, coef_ref, held):
    held[...] = split_dot(weight_ref[...], product_ref[...], ((0,), (0,)))
    width = coef_ref.shape[0]
    coef_ref[...] = held[pl.ds(pl.multiple_of(lax.axis_index("tm") * width, 8), width), :]


def final_kernel(parts, *refs):
    pieces, basis_ref = refs[:parts], refs[parts]
    me = lax.axis_index("tm")
    per, cells = basis_ref.shape[0] // parts, basis_ref.shape[2]
    for k in range(parts):
        base = (me ^ k) * per
        for i in range(per):
            basis_ref[base + i] = pieces[k][:, i * cells:(i + 1) * cells]


def shape(*dims):
    return jax.ShapeDtypeStruct(dims, F32)


def local(snapshots, land_mask, taps_rows, taps_cols, probes):
    rows, grid_cols, cols = snapshots.shape
    half_rows, half_cols = rows // 2, grid_cols // 2
    parts, patches = lax.axis_size("tm"), lax.axis_size("space")
    cells = half_rows * half_cols
    piece = cells // parts
    span = 2 if patches > 1 else 1

    snapshots, land_mask, taps_rows, taps_cols = (
        pltpu.with_memory_space_constraint(x, pltpu.HBM) for x in (snapshots, land_mask, taps_rows, taps_cols)
    )

    row_block, mask_block = (2, grid_cols, cols), (CHUNK, grid_cols)
    to_near, to_far = pl.pallas_call(
        edge_kernel,
        out_shape=[shape(half_cols, cols)] * 2,
        grid=(1,),
        in_specs=[
            scalars(), scalars(),
            pl.BlockSpec(row_block, lambda i: (0, 0, 0)),
            pl.BlockSpec(row_block, lambda i: (rows // 2 - 1, 0, 0)),
            pl.BlockSpec(mask_block, lambda i: (0, 0)),
            pl.BlockSpec(mask_block, lambda i: (rows // CHUNK - 1, 0)),
        ],
        out_specs=[pl.BlockSpec((half_cols, cols), lambda i: (0, 0))] * 2,
        scratch_shapes=[pltpu.VMEM((grid_cols, CHUNK), F32)],
        compiler_params=params(),
        name="edge",
    )(taps_rows, taps_cols, snapshots, snapshots, land_mask, land_mask)
    near = lax.ppermute(to_near, "space", [(i, i ^ 1) for i in range(patches) if i ^ 1 < patches])
    pairs = [(i, i + 1) for i in range(1, patches - 1, 2)]
    other = lax.ppermute(to_far, "space", pairs + [(j, i) for i, j in pairs])

    pieces = pl.pallas_call(
        functools.partial(filter_kernel, parts),
        out_shape=[shape(piece, cols)] * parts,
        in_specs=[scalars(), scalars(), pl.BlockSpec(memory_space=pltpu.HBM), whole()],
        out_specs=[whole()] * parts,
        scratch_shapes=[
            pltpu.VMEM((rows, grid_cols, cols), F32),
            pltpu.SemaphoreType.DMA((rows // CHUNK,)),
            pltpu.VMEM((grid_cols, rows), F32),
            pltpu.VMEM((rows, 2, half_cols, cols), F32),
            pltpu.VMEM((rows + 4, half_cols, cols), F32),
            pltpu.VMEM((cells, cols), F32),
        ],
        compiler_params=params(),
        cost_estimate=pl.CostEstimate(flops=0, bytes_accessed=4 * snapshots.size, transcendentals=0),
        name="filter",
    )(taps_rows, taps_cols, snapshots, land_mask)
    kept = pl.pallas_call(
        functools.partial(halo_kernel, parts),
        out_shape=[shape(piece, cols)] * parts,
        in_specs=[whole()] * (parts + 2),
        out_specs=[whole()] * parts,
        input_output_aliases={2 + k: k for k in range(parts)},
        compiler_params=params(),
        name="halo",
    )(near, other, *pieces)
    theirs = {k: swap(kept[k + 1], "tm", 1) for k in range(0, parts, 2)}
    far = {0: kept[0], 1: theirs[0]}
    for k in range(2, parts, 2):
        far[k] = swap(kept[k], "tm", k)
        far[k + 1] = swap(theirs[k], "tm", k)

    owners = 2 * span
    sums = pl.pallas_call(
        functools.partial(pair_kernel, parts, span),
        out_shape=[shape(pair_rows(cols, owners) // owners, cols)] * owners,
        in_specs=[whole()] * (parts + 1),
        out_specs=[whole()] * owners,
        scratch_shapes=[
            pltpu.VMEM((cells // 2, 2 * cols), F32),
            pltpu.VMEM((cells // 2, cols), F32),
            pltpu.VMEM((pair_rows(cols, owners), cols), F32),
        ],
        compiler_params=params(),
        cost_estimate=pl.CostEstimate(flops=0, bytes_accessed=0, transcendentals=0),
        name="pair",
    )(probes.reshape(cells, cols), *[kept[k] for k in range(0, parts, 2)], *[theirs[k] for k in range(0, parts, 2)])
    got = [swap_both(sums[j], j % 2 + parts * (j // 2)) for j in range(1, owners)]
    tied = lax.optimization_barrier(got + [far[k] for k in range(2, parts)])
    got = tied[:owners - 1]
    far.update(zip(range(2, parts), tied[owners - 1:]))
    pair_share = sums[0]
    for x in got:
        pair_share = pair_share + x
    bits = [1 << b for b in range(1, patches.bit_length() - 1)]

    blocks = len(cross_order(parts))
    owners = parts * span
    size = blocks * cols // owners
    factors = jax.ShapeDtypeStruct((piece, parts * cols), jnp.bfloat16)
    send, keep, high, low = pl.pallas_call(
        functools.partial(cross_kernel, parts, span),
        out_shape=[shape(owners // 2, size, cols)] * 2 + [factors] * 2,
        in_specs=[whole()] * parts,
        out_specs=[whole()] * 4,
        scratch_shapes=[pltpu.VMEM((piece, parts * cols), F32), pltpu.VMEM((blocks * cols, cols), F32)],
        compiler_params=params(),
        cost_estimate=pl.CostEstimate(flops=0, bytes_accessed=0, transcendentals=0),
        name="cross",
    )(*[far[k] for k in range(parts)])
    got = swap(send, "tm", 1)
    mine = keep[0] + got[0]
    for h in range(1, owners // 2):
        mine = mine + swap_both(keep[h] + got[h], 2 * h)
    for bit in bits[:1]:
        pair_share = pair_share + swap(pair_share, "space", bit)
    mine, pair_share = lax.optimization_barrier((mine, pair_share))
    for bit in bits[1:]:
        pair_share = pair_share + swap(pair_share, "space", bit)
    for bit in bits[:1]:
        mine = mine + swap(mine, "space", bit)
    mine, pair_share = lax.optimization_barrier((mine, pair_share))
    for bit in bits[1:]:
        mine = mine + swap(mine, "space", bit)

    def spread(x):
        return [x] + [swap_both(x, 2 * h) for h in range(1, owners // 2)]

    def gathered(shares):
        even = jnp.stack(shares)
        return even, swap(even, "tm", 1)

    mine, *pair_shares = lax.optimization_barrier([mine] + spread(pair_share))

    combines, squares, products = pl.pallas_call(
        functools.partial(level_kernel, parts, span),
        out_shape=[shape(parts // 2, 2 * cols, cols), shape(parts // 2, cols, cols), shape(parts * cols, cols)],
        in_specs=[whole()] * 2,
        out_specs=[whole()] * 3,
        scratch_shapes=[pltpu.VMEM((parts // 2, pair_rows(cols, 2 * span), cols), F32)],
        compiler_params=params(),
        cost_estimate=pl.CostEstimate(flops=parts * SIGN_STEPS * 6 * (2 * cols) ** 3, bytes_accessed=0, transcendentals=0),
        name="level",
    )(*gathered(pair_shares))

    combines, *shares = lax.optimization_barrier([combines] + spread(mine))
    width = cols // parts
    *sent, weight = pl.pallas_call(
        functools.partial(merge_kernel, parts, span),
        out_shape=[shape(width, piece)] * parts + [shape(parts * cols, cols)],
        in_specs=[whole()] * 6,
        out_specs=[whole()] * (parts + 1),
        scratch_shapes=[pltpu.VMEM((blocks * cols, cols), F32), pltpu.VMEM((cols, piece), F32)],
        compiler_params=params(),
        name="merge",
    )(*gathered(shares), combines, squares, high, low)
    coefficients = pl.pallas_call(
        functools.partial(coefficient_kernel, parts),
        out_shape=shape(width, cols),
        in_specs=[whole()] * 2,
        out_specs=whole(),
        scratch_shapes=[pltpu.VMEM((cols, cols), F32)],
        compiler_params=params(),
        name="coefficients",
    )(weight, products)
    last = [sent[0]] + [swap(sent[k], "tm", k) for k in range(1, parts)]

    basis = pl.pallas_call(
        functools.partial(final_kernel, parts),
        out_shape=shape(half_rows, width, half_cols),
        in_specs=[whole()] * parts,
        out_specs=whole(),
        compiler_params=params(),
        name="final",
    )(*last)
    return basis.transpose(0, 2, 1), coefficients


def solution(mesh):
    placed = (P("space", None, "tm"), P("space", None), P(), P(), P("space", None, None))
    return jax.shard_map(
        local,
        mesh=mesh,
        in_specs=placed,
        out_specs=(P("space", None, "tm"), P("tm", None)),
        check_vma=False,
    )
```

```python
import functools

import jax
import jax.numpy as jnp
from jax import lax
from jax.experimental import pallas as pl
from jax.experimental.pallas import tpu as pltpu
from jax.sharding import PartitionSpec as P

SIGN_STEPS = 8
TAPS = 6
CHUNK = 8
ROW_BLOCKS = 2
F32 = jnp.float32
VMEM_LIMIT = 48 * 1024 * 1024


def params():
    return pltpu.CompilerParams(vmem_limit_bytes=VMEM_LIMIT)


def whole():
    return pl.BlockSpec(memory_space=pltpu.VMEM)


def scalars():
    return pl.BlockSpec(memory_space=pltpu.SMEM)


def swap(x, axis, mask):
    count = lax.axis_size(axis)
    return lax.ppermute(x, axis, [(i, i ^ mask) for i in range(count)])


def swap_both(x, mask):
    parts, patches = lax.axis_size("tm"), lax.axis_size("space")
    route = []
    for t in range(parts):
        for s in range(patches):
            there = (t ^ (mask % parts)) * patches + (s ^ (mask // parts))
            route.append((t * patches + s, there))
    return lax.ppermute(x, ("tm", "space"), route)


def shift_rows(x, by):
    edge = jnp.zeros((1, x.shape[1]), x.dtype)
    if by > 0:
        return jnp.concatenate([edge, x[:-1]], axis=0)
    return jnp.concatenate([x[1:], edge], axis=0)


def mask_columns(mask, mask_t):
    mask_t[...] = mask.astype(F32).T
    half = mask.shape[1] // 2
    return mask_t[pl.ds(0, half, stride=2), :], mask_t[pl.ds(1, half, stride=2), :]


def narrowed_row(snaps, x, mask, taps):
    half = snaps.shape[1] // 2
    even = snaps[x, pl.ds(0, half, stride=2), :] * mask[0]
    odd = snaps[x, pl.ds(1, half, stride=2), :] * mask[1]
    before = taps[0] * even + taps[1] * odd
    here = taps[2] * even + taps[3] * odd
    after = taps[4] * even + taps[5] * odd
    return shift_rows(before, 1) + here + shift_rows(after, -1)


def edge_kernel(rtaps_ref, ctaps_ref, first_ref, last_ref, mask_first_ref, mask_last_ref, near_ref, far_ref, mask_t):
    ctaps = [ctaps_ref[k] for k in range(TAPS)]
    even = lax.axis_index("space") % 2 == 0
    shares = []
    for snaps, mask_ref, taps, at in (
        (first_ref, mask_first_ref, (rtaps_ref[4], rtaps_ref[5]), 0),
        (last_ref, mask_last_ref, (rtaps_ref[0], rtaps_ref[1]), CHUNK - 2),
    ):
        masks = mask_columns(mask_ref[...], mask_t)
        rows = [narrowed_row(snaps, x, [m[:, at + x:at + x + 1] for m in masks], ctaps) for x in range(2)]
        shares.append(taps[0] * rows[0] + taps[1] * rows[1])
    up, down = shares
    near_ref[...] = jnp.where(even, down, up)
    far_ref[...] = jnp.where(even, up, down)


def filter_kernel(parts, rtaps_ref, ctaps_ref, snap_hbm, mask_ref, *rest):
    pieces, (snaps, sems, mask_t, spread, narrowed, filtered) = rest[:parts], rest[parts:]
    rows, cells = narrowed.shape[0] - 4, narrowed.shape[1]
    me = lax.axis_index("tm")
    chunks = rows // CHUNK

    def fetch(c):
        at = pl.ds(c * CHUNK, CHUNK)
        return pltpu.make_async_copy(snap_hbm.at[at], snaps.at[at], sems.at[c])

    for c in range(chunks):
        fetch(c).start()

    rtaps = [rtaps_ref[k] for k in range(TAPS)]
    ctaps = [ctaps_ref[k] for k in range(TAPS)]
    edge = jnp.zeros((2,) + narrowed.shape[1:], F32)
    narrowed[0:2] = edge
    narrowed[rows + 2:rows + 4] = edge

    masks = mask_columns(mask_ref[...], mask_t)
    for x in range(rows):
        for j, mask in enumerate(masks):
            spread[x, j] = jnp.broadcast_to(mask[:, x:x + 1], (cells, narrowed.shape[2]))

    def narrow(c, carry):
        fetch(c).wait()
        base = pl.multiple_of(c * CHUNK, CHUNK)
        for x in range(CHUNK):
            row = narrowed_row(snaps, base + x, spread[base + x], ctaps)
            narrowed[base + 2 + x] = row
        return carry

    lax.fori_loop(0, chunks, narrow, 0)
    for i in range(rows // 2):
        total = rtaps[0] * narrowed[2 * i]
        for k in range(1, TAPS):
            total = total + rtaps[k] * narrowed[2 * i + k]
        filtered[i * cells:(i + 1) * cells, :] = total
    size = filtered.shape[0] // parts
    for k in range(parts):
        pieces[k][...] = filtered[pl.ds(pl.multiple_of((me ^ k) * size, 8), size), :]


def halo_kernel(parts, near_ref, far_ref, *refs):
    outs = refs[len(refs) // 2:]
    me = lax.axis_index("tm")
    cells = near_ref.shape[0]
    even = lax.axis_index("space") % 2 == 0
    above = jnp.where(even, far_ref[...], near_ref[...])
    below = jnp.where(even, near_ref[...], far_ref[...])
    for k, out in enumerate(outs):
        out[...] = refs[k][...]

        @pl.when((me ^ k) == 0)
        def _():
            out[:cells, :] = out[:cells, :] + above

        @pl.when((me ^ k) == parts - 1)
        def _():
            out[-cells:, :] = out[-cells:, :] + below


def cross_order(parts):
    return [(a, b) for p in range(0, parts, 2) for q in range(p + 2, parts, 2) for a in (p, p + 1) for b in (q, q + 1)]


def triangle(size):
    return tuple(lax.broadcasted_iota(jnp.int32, (size, size), axis) for axis in range(2))


def pair_rows(cols, owners):
    return 2 * cols + 8 * owners


def pair_kernel(parts, span, probes_ref, *refs):
    half = parts // 2
    owners = 2 * span
    mine, theirs, refs = refs[:half], refs[half:2 * half], refs[2 * half:]
    outs, (wide, there, flat, products) = refs[:owners], refs[owners:]
    me, owner = positions(2, span)
    size, cols = mine[0].shape
    low = pl.ds(pl.multiple_of((me % 2) * cols, cols), cols)
    high = pl.ds(pl.multiple_of((1 - me % 2) * cols, cols), cols)
    for h in range(half):
        at = pl.ds(h * size, size)
        wide[at, low] = mine[h][...]
        wide[at, high] = theirs[h][...]
        there[at, :] = probes_ref[pl.ds(pl.multiple_of((me ^ 2 * h) * size, 8), size), :]
    left = split(wide[...])
    gram = dot_parts(left, left, ((0,), (0,)))
    first, second = gram[:cols, :cols], gram[cols:, cols:]
    row, col = triangle(cols)
    flat[:cols, :] = gram[:cols, cols:]
    flat[cols:2 * cols, :] = jnp.where(row <= col, first, second)
    products[...] = dot_parts(left, split(there[...]), ((0,), (0,)))
    diagonal = jnp.sum(jnp.where(row == col, second, 0.0), axis=0, keepdims=True)
    flat[2 * cols:, :] = jnp.broadcast_to(diagonal, (flat.shape[0] - 2 * cols, cols))
    share, rest = flat.shape[0] // owners, 2 * cols // owners
    for k, out in enumerate(outs):
        out[:share, :] = flat[pl.ds(pl.multiple_of((owner ^ k) * share, 8), share), :]
        out[share:, :] = products[pl.ds(pl.multiple_of((owner ^ k) * rest, 8), rest), :]


def positions(count, span):
    me = lax.axis_index("tm")
    return me, me % count + count * (lax.axis_index("space") % span)


def give(owner, flat, send_ref, keep_ref):
    count = 2 * send_ref.shape[0]
    share = flat.shape[0] // count
    for k in range(count):
        out = send_ref if k % 2 else keep_ref
        out[k // 2] = flat[pl.ds(pl.multiple_of((owner ^ k) * share, 8), share), :]


def cross_kernel(parts, span, *refs):
    pieces, (send_ref, keep_ref, high_ref, low_ref, wide, flat) = refs[:parts], refs[parts:]
    me, owner = positions(parts, span)
    cols = pieces[0].shape[1]
    for k in range(parts):
        wide[:, pl.ds(pl.multiple_of((me ^ k) * cols, cols), cols)] = pieces[k][...]
    sides = [split(wide[:, a * cols:(a + 2) * cols]) for a in range(0, parts, 2)]
    for at, (high, low) in enumerate(sides):
        high_ref[:, 2 * at * cols:2 * (at + 1) * cols] = high
        low_ref[:, 2 * at * cols:2 * (at + 1) * cols] = low
    where = {ab: j for j, ab in enumerate(cross_order(parts))}
    for a in range(0, parts, 2):
        for b in range(a + 2, parts, 2):
            prod = dot_parts(sides[a // 2], sides[b // 2], ((0,), (0,)))
            for i in range(2):
                for j in range(2):
                    at = where[a + i, b + j] * cols
                    flat[at:at + cols, :] = prod[i * cols:(i + 1) * cols, j * cols:(j + 1) * cols]
    give(owner, flat, send_ref, keep_ref)


def split(x):
    high = x.astype(jnp.bfloat16)
    return high, (x - high.astype(F32)).astype(jnp.bfloat16)


def dot(a, b, dims):
    return lax.dot_general(a, b, (dims, ((), ())), preferred_element_type=F32)


def dot_parts(a, b, dims=((1,), (0,))):
    (ah, al), (bh, bl) = a, b
    left = jnp.concatenate([ah, ah, al], axis=dims[0][0])
    return dot(left, jnp.concatenate([bh, bl, bh], axis=dims[1][0]), dims)


def split_dot(a, b, dims=((1,), (0,))):
    return dot_parts(split(a), split(b), dims)


def next_sign(y):
    whole_y = split(y)
    size = y.shape[0] // ROW_BLOCKS
    blocks = []
    for at in range(0, y.shape[0], size):
        square = dot_parts([part[at:at + size] for part in whole_y], whole_y)
        blocks.append(1.5 * y[at:at + size] - 0.5 * dot_parts(split(square), whole_y))
    return jnp.concatenate(blocks, axis=0)


def combine_of(grams):
    order = grams[0].shape[0]
    diagonal = lax.broadcasted_iota(jnp.int32, (order, order), 0) == lax.broadcasted_iota(jnp.int32, (order, order), 1)
    signs = []
    for gram in grams:
        mean = jnp.sum(jnp.where(diagonal, gram, 0.0)) / order
        shifted = jnp.where(diagonal, gram - mean, gram)
        signs.append(shifted / jnp.sqrt(jnp.sum(shifted * shifted, keepdims=True) + 1e-6))
    for _ in range(SIGN_STEPS):
        signs = [next_sign(y) for y in signs]
    half = order // 2
    combines = []
    for y in signs:
        projector = 0.5 * (jnp.where(diagonal, 1.0, 0.0) + y)
        combines.append(projector[:, :half] + projector[:, half:])
    return combines


def place_shares(parts, span, even_ref, odd_ref, put):
    _, owner = positions(parts, span)
    for k in range(parts * span):
        put(owner ^ k, (odd_ref if k % 2 else even_ref)[k // 2])


def pair_at(parts, step, j, core):
    return j if step == parts // 2 else 2 * j + core


def level_kernel(parts, span, even_ref, odd_ref, out_ref, pairs):
    cols = even_ref.shape[2]
    share = pairs.shape[1] // (2 * span)

    def put(there, rows):
        place = there % 2 + 2 * (there // parts)
        pairs[(there % parts) // 2, pl.ds(pl.multiple_of(place * share, 8), share), :] = rows

    place_shares(parts, span, even_ref, odd_ref, put)
    row, col = triangle(cols)
    grams = []
    step = out_ref.shape[0]
    for j in range(step):
        p = pair_at(parts, step, j, lax.axis_index("tm") % 2)
        packed = pairs[p, cols:2 * cols, :]
        turned_back = packed.T
        first = jnp.where(row <= col, packed, turned_back)
        between = pairs[p, :cols, :]
        second = jnp.where(row > col, packed, turned_back)
        second = jnp.where(row == col, pairs[p, 2 * cols:2 * cols + 1, :], second)
        grams.append(jnp.concatenate([
            jnp.concatenate([first, between], axis=1), jnp.concatenate([between.T, second], axis=1)
        ], axis=0))
    for j, (gram, combine) in enumerate(zip(grams, combine_of(grams))):
        out_ref[j, :2 * cols, :] = combine
        out_ref[j, 2 * cols:, :] = split_dot(combine, split_dot(gram, combine), ((0,), (0,)))


def merge_kernel(parts, span, even_ref, odd_ref, mine_ref, theirs_ref, high_ref, low_ref, *refs):
    outs, (weight_ref, product_ref, level, cross, turned) = refs[:parts], refs[parts:]
    me = lax.axis_index("tm")
    cols = even_ref.shape[2]
    share = cross.shape[0] // (parts * span)

    rest = 2 * cols // (2 * span)

    def put(there, rows):
        cross[pl.ds(pl.multiple_of(there * share, 8), share), :] = rows[:share]
        at = ((there % parts) // 2) * 2 * cols + (there % 2 + 2 * (there // parts)) * rest
        product_ref[pl.ds(pl.multiple_of(at, 8), rest), :] = rows[share:]

    place_shares(parts, span, even_ref, odd_ref, put)
    where = {ab: j * cols for j, ab in enumerate(cross_order(parts))}
    step = mine_ref.shape[0]
    for j in range(step):
        level[pair_at(parts, step, j, 1 - me % 2)] = theirs_ref[j]
        level[pair_at(parts, step, j, me % 2)] = mine_ref[j]
    weights = [level[p, :2 * cols, :] for p in range(parts // 2)]
    blocks = {(p, p): level[p, 2 * cols:, :] for p in range(parts // 2)}
    for p in range(parts // 2):
        for q in range(p + 1, parts // 2):
            between = jnp.concatenate([
                jnp.concatenate([cross[where[a, b]:where[a, b] + cols, :] for b in (2 * q, 2 * q + 1)], axis=1)
                for a in (2 * p, 2 * p + 1)
            ], axis=0)
            blocks[p, q] = split_dot(weights[p], split_dot(between, weights[q]), ((0,), (0,)))
    count = parts // 2
    while count > 1:
        grams = []
        for p in range(0, count, 2):
            low = jnp.concatenate([blocks[p, p], blocks[p, p + 1]], axis=1)
            high = jnp.concatenate([blocks[p, p + 1].T, blocks[p + 1, p + 1]], axis=1)
            grams.append(jnp.concatenate([low, high], axis=0))
        combines = combine_of(grams)
        per = len(weights) // len(combines)
        weights = [
            split_dot(w, combines[i // per][(i % per) * cols:(i % per + 1) * cols, :])
            for i, w in enumerate(weights)
        ]
        weights = [jnp.concatenate(weights[i:i + per], axis=0) for i in range(0, len(weights), per)]
        merged = {}
        if count > 2:
            for p in range(count // 2):
                for q in range(p, count // 2):
                    if p == q:
                        between = grams[p]
                    else:
                        between = jnp.concatenate([
                            jnp.concatenate([blocks[2 * p + i, 2 * q], blocks[2 * p + i, 2 * q + 1]], axis=1)
                            for i in range(2)
                        ], axis=0)
                    right = split_dot(between, combines[q])
                    merged[p, q] = split_dot(combines[p], right, ((0,), (0,)))
        blocks, count = merged, count // 2
    weight_ref[...] = weights[0]
    width = cols // parts
    turned[...] = dot_parts((high_ref[...], low_ref[...]), split(weights[0])).T
    for k in range(parts):
        outs[k][...] = turned[pl.ds(pl.multiple_of((me ^ k) * width, 8), width), :]


def coefficient_kernel(parts, weight_ref, product_ref, coef_ref, held):
    held[...] = split_dot(weight_ref[...], product_ref[...], ((0,), (0,)))
    width = coef_ref.shape[0]
    coef_ref[...] = held[pl.ds(pl.multiple_of(lax.axis_index("tm") * width, 8), width), :]


def final_kernel(parts, *refs):
    pieces, basis_ref = refs[:parts], refs[parts]
    me = lax.axis_index("tm")
    per, cells = basis_ref.shape[0] // parts, basis_ref.shape[2]
    for k in range(parts):
        base = (me ^ k) * per
        for i in range(per):
            basis_ref[base + i] = pieces[k][:, i * cells:(i + 1) * cells]


def shape(*dims):
    return jax.ShapeDtypeStruct(dims, F32)


def local(snapshots, land_mask, taps_rows, taps_cols, probes):
    rows, grid_cols, cols = snapshots.shape
    half_rows, half_cols = rows // 2, grid_cols // 2
    parts, patches = lax.axis_size("tm"), lax.axis_size("space")
    cells = half_rows * half_cols
    piece = cells // parts
    span = 2 if patches > 1 else 1

    snapshots, land_mask, taps_rows, taps_cols = (
        pltpu.with_memory_space_constraint(x, pltpu.HBM) for x in (snapshots, land_mask, taps_rows, taps_cols)
    )

    row_block, mask_block = (2, grid_cols, cols), (CHUNK, grid_cols)
    to_near, to_far = pl.pallas_call(
        edge_kernel,
        out_shape=[shape(half_cols, cols)] * 2,
        grid=(1,),
        in_specs=[
            scalars(), scalars(),
            pl.BlockSpec(row_block, lambda i: (0, 0, 0)),
            pl.BlockSpec(row_block, lambda i: (rows // 2 - 1, 0, 0)),
            pl.BlockSpec(mask_block, lambda i: (0, 0)),
            pl.BlockSpec(mask_block, lambda i: (rows // CHUNK - 1, 0)),
        ],
        out_specs=[pl.BlockSpec((half_cols, cols), lambda i: (0, 0))] * 2,
        scratch_shapes=[pltpu.VMEM((grid_cols, CHUNK), F32)],
        compiler_params=params(),
        name="edge",
    )(taps_rows, taps_cols, snapshots, snapshots, land_mask, land_mask)
    near = lax.ppermute(to_near, "space", [(i, i ^ 1) for i in range(patches) if i ^ 1 < patches])
    pairs = [(i, i + 1) for i in range(1, patches - 1, 2)]
    other = lax.ppermute(to_far, "space", pairs + [(j, i) for i, j in pairs])

    pieces = pl.pallas_call(
        functools.partial(filter_kernel, parts),
        out_shape=[shape(piece, cols)] * parts,
        in_specs=[scalars(), scalars(), pl.BlockSpec(memory_space=pltpu.HBM), whole()],
        out_specs=[whole()] * parts,
        scratch_shapes=[
            pltpu.VMEM((rows, grid_cols, cols), F32),
            pltpu.SemaphoreType.DMA((rows // CHUNK,)),
            pltpu.VMEM((grid_cols, rows), F32),
            pltpu.VMEM((rows, 2, half_cols, cols), F32),
            pltpu.VMEM((rows + 4, half_cols, cols), F32),
            pltpu.VMEM((cells, cols), F32),
        ],
        compiler_params=params(),
        cost_estimate=pl.CostEstimate(flops=0, bytes_accessed=4 * snapshots.size, transcendentals=0),
        name="filter",
    )(taps_rows, taps_cols, snapshots, land_mask)
    kept = pl.pallas_call(
        functools.partial(halo_kernel, parts),
        out_shape=[shape(piece, cols)] * parts,
        in_specs=[whole()] * (parts + 2),
        out_specs=[whole()] * parts,
        input_output_aliases={2 + k: k for k in range(parts)},
        compiler_params=params(),
        name="halo",
    )(near, other, *pieces)
    theirs = {k: swap(kept[k + 1], "tm", 1) for k in range(0, parts, 2)}
    far = {0: kept[0], 1: theirs[0]}
    for k in range(2, parts, 2):
        far[k] = swap(kept[k], "tm", k)
        far[k + 1] = swap(theirs[k], "tm", k)

    owners = 2 * span
    pair_size = pair_rows(cols, owners) // owners
    sums = pl.pallas_call(
        functools.partial(pair_kernel, parts, span),
        out_shape=[shape(pair_size + 2 * cols // owners, cols)] * owners,
        in_specs=[whole()] * (parts + 1),
        out_specs=[whole()] * owners,
        scratch_shapes=[
            pltpu.VMEM((cells // 2, 2 * cols), F32),
            pltpu.VMEM((cells // 2, cols), F32),
            pltpu.VMEM((pair_rows(cols, owners), cols), F32),
            pltpu.VMEM((2 * cols, cols), F32),
        ],
        compiler_params=params(),
        cost_estimate=pl.CostEstimate(flops=0, bytes_accessed=0, transcendentals=0),
        name="pair",
    )(probes.reshape(cells, cols), *[kept[k] for k in range(0, parts, 2)], *[theirs[k] for k in range(0, parts, 2)])
    got = [swap_both(sums[j], j % 2 + parts * (j // 2)) for j in range(1, owners)]
    tied = lax.optimization_barrier(got + [far[k] for k in range(2, parts)])
    got = tied[:owners - 1]
    far.update(zip(range(2, parts), tied[owners - 1:]))
    pair_share = sums[0]
    for x in got:
        pair_share = pair_share + x
    bits = [1 << b for b in range(1, patches.bit_length() - 1)]

    blocks = len(cross_order(parts))
    owners = parts * span
    size = blocks * cols // owners
    factors = jax.ShapeDtypeStruct((piece, parts * cols), jnp.bfloat16)
    send, keep, high, low = pl.pallas_call(
        functools.partial(cross_kernel, parts, span),
        out_shape=[shape(owners // 2, size, cols)] * 2 + [factors] * 2,
        in_specs=[whole()] * parts,
        out_specs=[whole()] * 4,
        scratch_shapes=[pltpu.VMEM((piece, parts * cols), F32), pltpu.VMEM((blocks * cols, cols), F32)],
        compiler_params=params(),
        cost_estimate=pl.CostEstimate(flops=0, bytes_accessed=0, transcendentals=0),
        name="cross",
    )(*[far[k] for k in range(parts)])
    got = swap(send, "tm", 1)
    mine = keep[0] + got[0]
    for h in range(1, owners // 2):
        mine = mine + swap_both(keep[h] + got[h], 2 * h)
    for bit in bits[:1]:
        pair_share = pair_share + swap(pair_share, "space", bit)
    mine, pair_share = lax.optimization_barrier((mine, pair_share))
    pair_share, product_share = pair_share[:pair_size], pair_share[pair_size:]
    for bit in bits[1:]:
        pair_share = pair_share + swap(pair_share, "space", bit)
    for bit in bits[:1]:
        mine = mine + swap(mine, "space", bit)
    mine, pair_share = lax.optimization_barrier((mine, pair_share))
    mine = jnp.concatenate([mine, product_share], axis=0)
    for bit in bits[1:]:
        mine = mine + swap(mine, "space", bit)

    def spread(x):
        return [x] + [swap_both(x, 2 * h) for h in range(1, owners // 2)]

    def gathered(shares):
        even = jnp.stack(shares)
        return even, swap(even, "tm", 1)

    mine, *pair_shares = lax.optimization_barrier([mine] + spread(pair_share))

    half = parts // 2
    level = pl.pallas_call(
        functools.partial(level_kernel, parts, span),
        out_shape=shape(half // 2 if half % 2 == 0 else half, 3 * cols, cols),
        in_specs=[whole()] * 2,
        out_specs=whole(),
        scratch_shapes=[pltpu.VMEM((half, pair_rows(cols, 2 * span), cols), F32)],
        compiler_params=params(),
        cost_estimate=pl.CostEstimate(flops=parts * SIGN_STEPS * 6 * (2 * cols) ** 3, bytes_accessed=0, transcendentals=0),
        name="level",
    )(*gathered(pair_shares))
    level, *shares = lax.optimization_barrier([level] + spread(mine))
    other_level = swap(level, "tm", 1)
    width = cols // parts
    *sent, weight, products = pl.pallas_call(
        functools.partial(merge_kernel, parts, span),
        out_shape=[shape(width, piece)] * parts + [shape(parts * cols, cols)] * 2,
        in_specs=[whole()] * 6,
        out_specs=[whole()] * (parts + 2),
        scratch_shapes=[
            pltpu.VMEM((half, 3 * cols, cols), F32),
            pltpu.VMEM((blocks * cols, cols), F32),
            pltpu.VMEM((cols, piece), F32),
        ],
        compiler_params=params(),
        name="merge",
    )(*gathered(shares), level, other_level, high, low)
    coefficients = pl.pallas_call(
        functools.partial(coefficient_kernel, parts),
        out_shape=shape(width, cols),
        in_specs=[whole()] * 2,
        out_specs=whole(),
        scratch_shapes=[pltpu.VMEM((cols, cols), F32)],
        compiler_params=params(),
        name="coefficients",
    )(weight, products)
    last = [sent[0]] + [swap(sent[k], "tm", k) for k in range(1, parts)]

    basis = pl.pallas_call(
        functools.partial(final_kernel, parts),
        out_shape=shape(half_rows, width, half_cols),
        in_specs=[whole()] * parts,
        out_specs=whole(),
        compiler_params=params(),
        name="final",
    )(*last)
    return basis.transpose(0, 2, 1), coefficients


def solution(mesh):
    placed = (P("space", None, "tm"), P("space", None), P(), P(), P("space", None, None))
    return jax.shard_map(
        local,
        mesh=mesh,
        in_specs=placed,
        out_specs=(P("space", None, "tm"), P("tm", None)),
        check_vma=False,
    )
```

```python
import functools

import jax
import jax.numpy as jnp
from jax import lax
from jax.experimental import pallas as pl
from jax.experimental.pallas import tpu as pltpu
from jax.sharding import PartitionSpec as P

SIGN_STEPS = 8
TAPS = 6
CHUNK = 8
ROW_BLOCKS = 2
F32 = jnp.float32
VMEM_LIMIT = 48 * 1024 * 1024


def params():
    return pltpu.CompilerParams(vmem_limit_bytes=VMEM_LIMIT)


def whole():
    return pl.BlockSpec(memory_space=pltpu.VMEM)


def scalars():
    return pl.BlockSpec(memory_space=pltpu.SMEM)


def swap(x, axis, mask):
    count = lax.axis_size(axis)
    return lax.ppermute(x, axis, [(i, i ^ mask) for i in range(count)])


def swap_both(x, mask):
    parts, patches = lax.axis_size("tm"), lax.axis_size("space")
    route = []
    for t in range(parts):
        for s in range(patches):
            there = (t ^ (mask % parts)) * patches + (s ^ (mask // parts))
            route.append((t * patches + s, there))
    return lax.ppermute(x, ("tm", "space"), route)


def shift_rows(x, by):
    edge = jnp.zeros((1, x.shape[1]), x.dtype)
    if by > 0:
        return jnp.concatenate([edge, x[:-1]], axis=0)
    return jnp.concatenate([x[1:], edge], axis=0)


def mask_columns(mask, mask_t):
    mask_t[...] = mask.astype(F32).T
    half = mask.shape[1] // 2
    return mask_t[pl.ds(0, half, stride=2), :], mask_t[pl.ds(1, half, stride=2), :]


def narrowed_row(snaps, x, mask, taps):
    half = snaps.shape[1] // 2
    even = snaps[x, pl.ds(0, half, stride=2), :] * mask[0]
    odd = snaps[x, pl.ds(1, half, stride=2), :] * mask[1]
    before = taps[0] * even + taps[1] * odd
    here = taps[2] * even + taps[3] * odd
    after = taps[4] * even + taps[5] * odd
    return shift_rows(before, 1) + here + shift_rows(after, -1)


def edge_kernel(rtaps_ref, ctaps_ref, first_ref, last_ref, mask_first_ref, mask_last_ref, near_ref, far_ref, mask_t):
    ctaps = [ctaps_ref[k] for k in range(TAPS)]
    even = lax.axis_index("space") % 2 == 0
    shares = []
    for snaps, mask_ref, taps, at in (
        (first_ref, mask_first_ref, (rtaps_ref[4], rtaps_ref[5]), 0),
        (last_ref, mask_last_ref, (rtaps_ref[0], rtaps_ref[1]), CHUNK - 2),
    ):
        masks = mask_columns(mask_ref[...], mask_t)
        rows = [narrowed_row(snaps, x, [m[:, at + x:at + x + 1] for m in masks], ctaps) for x in range(2)]
        shares.append(taps[0] * rows[0] + taps[1] * rows[1])
    up, down = shares
    near_ref[...] = jnp.where(even, down, up)
    far_ref[...] = jnp.where(even, up, down)


def filter_kernel(parts, rtaps_ref, ctaps_ref, snap_hbm, mask_ref, *rest):
    pieces, (snaps, sems, mask_t, spread, narrowed, filtered) = rest[:parts], rest[parts:]
    rows, cells = narrowed.shape[0] - 4, narrowed.shape[1]
    me = lax.axis_index("tm")
    chunks = rows // CHUNK

    def fetch(c):
        at = pl.ds(c * CHUNK, CHUNK)
        return pltpu.make_async_copy(snap_hbm.at[at], snaps.at[at], sems.at[c])

    for c in range(chunks):
        fetch(c).start()

    rtaps = [rtaps_ref[k] for k in range(TAPS)]
    ctaps = [ctaps_ref[k] for k in range(TAPS)]
    edge = jnp.zeros((2,) + narrowed.shape[1:], F32)
    narrowed[0:2] = edge
    narrowed[rows + 2:rows + 4] = edge

    masks = mask_columns(mask_ref[...], mask_t)
    for x in range(rows):
        for j, mask in enumerate(masks):
            spread[x, j] = jnp.broadcast_to(mask[:, x:x + 1], (cells, narrowed.shape[2]))

    def narrow(c, carry):
        fetch(c).wait()
        base = pl.multiple_of(c * CHUNK, CHUNK)
        for x in range(CHUNK):
            row = narrowed_row(snaps, base + x, spread[base + x], ctaps)
            narrowed[base + 2 + x] = row
        return carry

    lax.fori_loop(0, chunks, narrow, 0)
    for i in range(rows // 2):
        total = rtaps[0] * narrowed[2 * i]
        for k in range(1, TAPS):
            total = total + rtaps[k] * narrowed[2 * i + k]
        filtered[i * cells:(i + 1) * cells, :] = total
    size = filtered.shape[0] // parts
    for k in range(parts):
        pieces[k][...] = filtered[pl.ds(pl.multiple_of((me ^ k) * size, 8), size), :]


def halo_kernel(parts, near_ref, far_ref, *refs):
    outs = refs[len(refs) // 2:]
    me = lax.axis_index("tm")
    cells = near_ref.shape[0]
    even = lax.axis_index("space") % 2 == 0
    above = jnp.where(even, far_ref[...], near_ref[...])
    below = jnp.where(even, near_ref[...], far_ref[...])
    for k, out in enumerate(outs):
        out[...] = refs[k][...]

        @pl.when((me ^ k) == 0)
        def _():
            out[:cells, :] = out[:cells, :] + above

        @pl.when((me ^ k) == parts - 1)
        def _():
            out[-cells:, :] = out[-cells:, :] + below


def cross_order(parts):
    return [(a, b) for p in range(0, parts, 2) for q in range(p + 2, parts, 2) for a in (p, p + 1) for b in (q, q + 1)]


def triangle(size):
    return tuple(lax.broadcasted_iota(jnp.int32, (size, size), axis) for axis in range(2))


def pair_rows(cols):
    return 2 * cols + 16


def pair_kernel(parts, span, probes_ref, *refs):
    half = parts // 2
    owners = 2 * span
    mine, theirs, refs = refs[:half], refs[half:2 * half], refs[2 * half:]
    outs, (wide, there, flat, products) = refs[:owners], refs[owners:]
    me, owner = positions(2, span)
    size, cols = mine[0].shape
    low = pl.ds(pl.multiple_of((me % 2) * cols, cols), cols)
    high = pl.ds(pl.multiple_of((1 - me % 2) * cols, cols), cols)
    for h in range(half):
        at = pl.ds(h * size, size)
        wide[at, low] = mine[h][...]
        wide[at, high] = theirs[h][...]
        there[at, :] = probes_ref[pl.ds(pl.multiple_of((me ^ 2 * h) * size, 8), size), :]
    left = split(wide[...])
    gram = dot_parts(left, left, ((0,), (0,)))
    first, second = gram[:cols, :cols], gram[cols:, cols:]
    row, col = triangle(cols)
    flat[:cols, :] = gram[:cols, cols:]
    flat[cols:2 * cols, :] = jnp.where(row <= col, first, second)
    products[...] = dot_parts(left, split(there[...]), ((0,), (0,)))
    diagonal = jnp.sum(jnp.where(row == col, second, 0.0), axis=0, keepdims=True)
    flat[2 * cols:, :] = jnp.broadcast_to(diagonal, (flat.shape[0] - 2 * cols, cols))
    share, rest = flat.shape[0] // 2, 2 * cols // owners
    for k, out in enumerate(outs):
        out[:share, :] = flat[pl.ds(pl.multiple_of(((owner ^ k) % 2) * share, 8), share), :]
        out[share:, :] = products[pl.ds(pl.multiple_of((owner ^ k) * rest, 8), rest), :]


def positions(count, span):
    me = lax.axis_index("tm")
    return me, me % count + count * (lax.axis_index("space") % span)


def give(owner, flat, send_ref, keep_ref):
    count = 2 * send_ref.shape[0]
    share = flat.shape[0] // count
    for k in range(count):
        out = send_ref if k % 2 else keep_ref
        out[k // 2] = flat[pl.ds(pl.multiple_of((owner ^ k) * share, 8), share), :]


def cross_kernel(parts, span, *refs):
    pieces, (send_ref, keep_ref, high_ref, low_ref, wide, flat) = refs[:parts], refs[parts:]
    me, owner = positions(parts, span)
    cols = pieces[0].shape[1]
    for k in range(parts):
        wide[:, pl.ds(pl.multiple_of((me ^ k) * cols, cols), cols)] = pieces[k][...]
    sides = [split(wide[:, a * cols:(a + 2) * cols]) for a in range(0, parts, 2)]
    for at, (high, low) in enumerate(sides):
        high_ref[:, 2 * at * cols:2 * (at + 1) * cols] = high
        low_ref[:, 2 * at * cols:2 * (at + 1) * cols] = low
    where = {ab: j for j, ab in enumerate(cross_order(parts))}
    for a in range(0, parts, 2):
        for b in range(a + 2, parts, 2):
            prod = dot_parts(sides[a // 2], sides[b // 2], ((0,), (0,)))
            for i in range(2):
                for j in range(2):
                    at = where[a + i, b + j] * cols
                    flat[at:at + cols, :] = prod[i * cols:(i + 1) * cols, j * cols:(j + 1) * cols]
    give(owner, flat, send_ref, keep_ref)


def split(x):
    high = x.astype(jnp.bfloat16)
    return high, (x - high.astype(F32)).astype(jnp.bfloat16)


def dot(a, b, dims):
    return lax.dot_general(a, b, (dims, ((), ())), preferred_element_type=F32)


def dot_parts(a, b, dims=((1,), (0,))):
    (ah, al), (bh, bl) = a, b
    left = jnp.concatenate([ah, ah, al], axis=dims[0][0])
    return dot(left, jnp.concatenate([bh, bl, bh], axis=dims[1][0]), dims)


def split_dot(a, b, dims=((1,), (0,))):
    return dot_parts(split(a), split(b), dims)


def next_sign(y):
    whole_y = split(y)
    size = y.shape[0] // ROW_BLOCKS
    blocks = []
    for at in range(0, y.shape[0], size):
        square = dot_parts([part[at:at + size] for part in whole_y], whole_y)
        blocks.append(1.5 * y[at:at + size] - 0.5 * dot_parts(split(square), whole_y))
    return jnp.concatenate(blocks, axis=0)


def combine_of(grams):
    order = grams[0].shape[0]
    diagonal = lax.broadcasted_iota(jnp.int32, (order, order), 0) == lax.broadcasted_iota(jnp.int32, (order, order), 1)
    signs = []
    for gram in grams:
        mean = jnp.sum(jnp.where(diagonal, gram, 0.0)) / order
        shifted = jnp.where(diagonal, gram - mean, gram)
        signs.append(shifted / jnp.sqrt(jnp.sum(shifted * shifted, keepdims=True) + 1e-6))
    for _ in range(SIGN_STEPS):
        signs = [next_sign(y) for y in signs]
    half = order // 2
    combines = []
    for y in signs:
        projector = 0.5 * (jnp.where(diagonal, 1.0, 0.0) + y)
        combines.append(projector[:, :half] + projector[:, half:])
    return combines


def place_shares(parts, span, even_ref, odd_ref, put):
    _, owner = positions(parts, span)
    for k in range(parts * span):
        put(owner ^ k, (odd_ref if k % 2 else even_ref)[k // 2])


def pair_at(parts, step, j, core):
    return j if step == parts // 2 else 2 * j + core


def level_kernel(parts, even_ref, odd_ref, out_ref, pairs):
    cols = even_ref.shape[2]
    share = pairs.shape[1] // 2

    def put(there, rows):
        pairs[there // 2, pl.ds(pl.multiple_of((there % 2) * share, 8), share), :] = rows

    place_shares(parts, 1, even_ref, odd_ref, put)
    row, col = triangle(cols)
    grams = []
    step = out_ref.shape[0]
    for j in range(step):
        p = pair_at(parts, step, j, lax.axis_index("tm") % 2)
        packed = pairs[p, cols:2 * cols, :]
        turned_back = packed.T
        first = jnp.where(row <= col, packed, turned_back)
        between = pairs[p, :cols, :]
        second = jnp.where(row > col, packed, turned_back)
        second = jnp.where(row == col, pairs[p, 2 * cols:2 * cols + 1, :], second)
        grams.append(jnp.concatenate([
            jnp.concatenate([first, between], axis=1), jnp.concatenate([between.T, second], axis=1)
        ], axis=0))
    for j, (gram, combine) in enumerate(zip(grams, combine_of(grams))):
        out_ref[j, :2 * cols, :] = combine
        out_ref[j, 2 * cols:, :] = split_dot(combine, split_dot(gram, combine), ((0,), (0,)))


def merge_kernel(parts, span, even_ref, odd_ref, mine_ref, theirs_ref, high_ref, low_ref, *refs):
    outs, (weight_ref, product_ref, level, cross, turned) = refs[:parts], refs[parts:]
    me = lax.axis_index("tm")
    cols = even_ref.shape[2]
    share = cross.shape[0] // (parts * span)

    rest = 2 * cols // (2 * span)

    def put(there, rows):
        cross[pl.ds(pl.multiple_of(there * share, 8), share), :] = rows[:share]
        at = ((there % parts) // 2) * 2 * cols + (there % 2 + 2 * (there // parts)) * rest
        product_ref[pl.ds(pl.multiple_of(at, 8), rest), :] = rows[share:]

    place_shares(parts, span, even_ref, odd_ref, put)
    where = {ab: j * cols for j, ab in enumerate(cross_order(parts))}
    step = mine_ref.shape[0]
    for j in range(step):
        level[pair_at(parts, step, j, 1 - me % 2)] = theirs_ref[j]
        level[pair_at(parts, step, j, me % 2)] = mine_ref[j]
    weights = [level[p, :2 * cols, :] for p in range(parts // 2)]
    blocks = {(p, p): level[p, 2 * cols:, :] for p in range(parts // 2)}
    for p in range(parts // 2):
        for q in range(p + 1, parts // 2):
            between = jnp.concatenate([
                jnp.concatenate([cross[where[a, b]:where[a, b] + cols, :] for b in (2 * q, 2 * q + 1)], axis=1)
                for a in (2 * p, 2 * p + 1)
            ], axis=0)
            blocks[p, q] = split_dot(weights[p], split_dot(between, weights[q]), ((0,), (0,)))
    count = parts // 2
    while count > 1:
        grams = []
        for p in range(0, count, 2):
            low = jnp.concatenate([blocks[p, p], blocks[p, p + 1]], axis=1)
            high = jnp.concatenate([blocks[p, p + 1].T, blocks[p + 1, p + 1]], axis=1)
            grams.append(jnp.concatenate([low, high], axis=0))
        combines = combine_of(grams)
        per = len(weights) // len(combines)
        weights = [
            split_dot(w, combines[i // per][(i % per) * cols:(i % per + 1) * cols, :])
            for i, w in enumerate(weights)
        ]
        weights = [jnp.concatenate(weights[i:i + per], axis=0) for i in range(0, len(weights), per)]
        merged = {}
        if count > 2:
            for p in range(count // 2):
                for q in range(p, count // 2):
                    if p == q:
                        between = grams[p]
                    else:
                        between = jnp.concatenate([
                            jnp.concatenate([blocks[2 * p + i, 2 * q], blocks[2 * p + i, 2 * q + 1]], axis=1)
                            for i in range(2)
                        ], axis=0)
                    right = split_dot(between, combines[q])
                    merged[p, q] = split_dot(combines[p], right, ((0,), (0,)))
        blocks, count = merged, count // 2
    weight_ref[...] = weights[0]
    width = cols // parts
    turned[...] = dot_parts((high_ref[...], low_ref[...]), split(weights[0])).T
    for k in range(parts):
        outs[k][...] = turned[pl.ds(pl.multiple_of((me ^ k) * width, 8), width), :]


def coefficient_kernel(parts, weight_ref, product_ref, coef_ref, held):
    held[...] = split_dot(weight_ref[...], product_ref[...], ((0,), (0,)))
    width = coef_ref.shape[0]
    coef_ref[...] = held[pl.ds(pl.multiple_of(lax.axis_index("tm") * width, 8), width), :]


def final_kernel(parts, *refs):
    pieces, basis_ref = refs[:parts], refs[parts]
    me = lax.axis_index("tm")
    per, cells = basis_ref.shape[0] // parts, basis_ref.shape[2]
    for k in range(parts):
        base = (me ^ k) * per
        for i in range(per):
            basis_ref[base + i] = pieces[k][:, i * cells:(i + 1) * cells]


def shape(*dims):
    return jax.ShapeDtypeStruct(dims, F32)


def local(snapshots, land_mask, taps_rows, taps_cols, probes):
    rows, grid_cols, cols = snapshots.shape
    half_rows, half_cols = rows // 2, grid_cols // 2
    parts, patches = lax.axis_size("tm"), lax.axis_size("space")
    cells = half_rows * half_cols
    piece = cells // parts
    span = 2 if patches > 1 else 1

    snapshots, land_mask, taps_rows, taps_cols = (
        pltpu.with_memory_space_constraint(x, pltpu.HBM) for x in (snapshots, land_mask, taps_rows, taps_cols)
    )

    row_block, mask_block = (2, grid_cols, cols), (CHUNK, grid_cols)
    to_near, to_far = pl.pallas_call(
        edge_kernel,
        out_shape=[shape(half_cols, cols)] * 2,
        grid=(1,),
        in_specs=[
            scalars(), scalars(),
            pl.BlockSpec(row_block, lambda i: (0, 0, 0)),
            pl.BlockSpec(row_block, lambda i: (rows // 2 - 1, 0, 0)),
            pl.BlockSpec(mask_block, lambda i: (0, 0)),
            pl.BlockSpec(mask_block, lambda i: (rows // CHUNK - 1, 0)),
        ],
        out_specs=[pl.BlockSpec((half_cols, cols), lambda i: (0, 0))] * 2,
        scratch_shapes=[pltpu.VMEM((grid_cols, CHUNK), F32)],
        compiler_params=params(),
        name="edge",
    )(taps_rows, taps_cols, snapshots, snapshots, land_mask, land_mask)
    near = lax.ppermute(to_near, "space", [(i, i ^ 1) for i in range(patches) if i ^ 1 < patches])
    pairs = [(i, i + 1) for i in range(1, patches - 1, 2)]
    other = lax.ppermute(to_far, "space", pairs + [(j, i) for i, j in pairs])

    pieces = pl.pallas_call(
        functools.partial(filter_kernel, parts),
        out_shape=[shape(piece, cols)] * parts,
        in_specs=[scalars(), scalars(), pl.BlockSpec(memory_space=pltpu.HBM), whole()],
        out_specs=[whole()] * parts,
        scratch_shapes=[
            pltpu.VMEM((rows, grid_cols, cols), F32),
            pltpu.SemaphoreType.DMA((rows // CHUNK,)),
            pltpu.VMEM((grid_cols, rows), F32),
            pltpu.VMEM((rows, 2, half_cols, cols), F32),
            pltpu.VMEM((rows + 4, half_cols, cols), F32),
            pltpu.VMEM((cells, cols), F32),
        ],
        compiler_params=params(),
        cost_estimate=pl.CostEstimate(flops=0, bytes_accessed=4 * snapshots.size, transcendentals=0),
        name="filter",
    )(taps_rows, taps_cols, snapshots, land_mask)
    kept = pl.pallas_call(
        functools.partial(halo_kernel, parts),
        out_shape=[shape(piece, cols)] * parts,
        in_specs=[whole()] * (parts + 2),
        out_specs=[whole()] * parts,
        input_output_aliases={2 + k: k for k in range(parts)},
        compiler_params=params(),
        name="halo",
    )(near, other, *pieces)
    theirs = {k: swap(kept[k + 1], "tm", 1) for k in range(0, parts, 2)}
    far = {0: kept[0], 1: theirs[0]}
    for k in range(2, parts, 2):
        far[k] = swap(kept[k], "tm", k)
        far[k + 1] = swap(theirs[k], "tm", k)

    owners = 2 * span
    pair_size = pair_rows(cols) // 2
    sums = pl.pallas_call(
        functools.partial(pair_kernel, parts, span),
        out_shape=[shape(pair_size + 2 * cols // owners, cols)] * owners,
        in_specs=[whole()] * (parts + 1),
        out_specs=[whole()] * owners,
        scratch_shapes=[
            pltpu.VMEM((cells // 2, 2 * cols), F32),
            pltpu.VMEM((cells // 2, cols), F32),
            pltpu.VMEM((pair_rows(cols), cols), F32),
            pltpu.VMEM((2 * cols, cols), F32),
        ],
        compiler_params=params(),
        cost_estimate=pl.CostEstimate(flops=0, bytes_accessed=0, transcendentals=0),
        name="pair",
    )(probes.reshape(cells, cols), *[kept[k] for k in range(0, parts, 2)], *[theirs[k] for k in range(0, parts, 2)])
    got = [swap_both(sums[j], j % 2 + parts * (j // 2)) for j in range(1, owners)]
    tied = lax.optimization_barrier(got + [far[k] for k in range(2, parts)])
    got = tied[:owners - 1]
    far.update(zip(range(2, parts), tied[owners - 1:]))
    pair_share = sums[0] + got[0]
    if span > 1:
        pair_share = pair_share + (got[1] + got[2])
    bits = [1 << b for b in range(1, patches.bit_length() - 1)]

    blocks = len(cross_order(parts))
    owners = parts * span
    size = blocks * cols // owners
    factors = jax.ShapeDtypeStruct((piece, parts * cols), jnp.bfloat16)
    send, keep, high, low = pl.pallas_call(
        functools.partial(cross_kernel, parts, span),
        out_shape=[shape(owners // 2, size, cols)] * 2 + [factors] * 2,
        in_specs=[whole()] * parts,
        out_specs=[whole()] * 4,
        scratch_shapes=[pltpu.VMEM((piece, parts * cols), F32), pltpu.VMEM((blocks * cols, cols), F32)],
        compiler_params=params(),
        cost_estimate=pl.CostEstimate(flops=0, bytes_accessed=0, transcendentals=0),
        name="cross",
    )(*[far[k] for k in range(parts)])
    got = swap(send, "tm", 1)
    mine = keep[0] + got[0]
    for h in range(1, owners // 2):
        mine = mine + swap_both(keep[h] + got[h], 2 * h)
    for bit in bits[:1]:
        pair_share = pair_share + swap(pair_share, "space", bit)
    mine, pair_share = lax.optimization_barrier((mine, pair_share))
    pair_share, product_share = pair_share[:pair_size], pair_share[pair_size:]
    for bit in bits[1:]:
        pair_share = pair_share + swap(pair_share, "space", bit)
    for bit in bits[:1]:
        mine = mine + swap(mine, "space", bit)
    mine, pair_share = lax.optimization_barrier((mine, pair_share))
    mine = jnp.concatenate([mine, product_share], axis=0)
    for bit in bits[1:]:
        mine = mine + swap(mine, "space", bit)

    def spread(x, count):
        return [x] + [swap_both(x, 2 * h) for h in range(1, count // 2)]

    def gathered(shares):
        even = jnp.stack(shares)
        return even, swap(even, "tm", 1)

    mine, *pair_shares = lax.optimization_barrier([mine] + spread(pair_share, parts))

    half = parts // 2
    level = pl.pallas_call(
        functools.partial(level_kernel, parts),
        out_shape=shape(half // 2 if half % 2 == 0 else half, 3 * cols, cols),
        in_specs=[whole()] * 2,
        out_specs=whole(),
        scratch_shapes=[pltpu.VMEM((half, pair_rows(cols), cols), F32)],
        compiler_params=params(),
        cost_estimate=pl.CostEstimate(flops=parts * SIGN_STEPS * 6 * (2 * cols) ** 3, bytes_accessed=0, transcendentals=0),
        name="level",
    )(*gathered(pair_shares))
    level, *shares = lax.optimization_barrier([level] + spread(mine, owners))
    other_level = swap(level, "tm", 1)
    width = cols // parts
    *sent, weight, products = pl.pallas_call(
        functools.partial(merge_kernel, parts, span),
        out_shape=[shape(width, piece)] * parts + [shape(parts * cols, cols)] * 2,
        in_specs=[whole()] * 6,
        out_specs=[whole()] * (parts + 2),
        scratch_shapes=[
            pltpu.VMEM((half, 3 * cols, cols), F32),
            pltpu.VMEM((blocks * cols, cols), F32),
            pltpu.VMEM((cols, piece), F32),
        ],
        compiler_params=params(),
        name="merge",
    )(*gathered(shares), level, other_level, high, low)
    coefficients = pl.pallas_call(
        functools.partial(coefficient_kernel, parts),
        out_shape=shape(width, cols),
        in_specs=[whole()] * 2,
        out_specs=whole(),
        scratch_shapes=[pltpu.VMEM((cols, cols), F32)],
        compiler_params=params(),
        name="coefficients",
    )(weight, products)
    last = [sent[0]] + [swap(sent[k], "tm", k) for k in range(1, parts)]

    basis = pl.pallas_call(
        functools.partial(final_kernel, parts),
        out_shape=shape(half_rows, width, half_cols),
        in_specs=[whole()] * parts,
        out_specs=whole(),
        compiler_params=params(),
        name="final",
    )(*last)
    return basis.transpose(0, 2, 1), coefficients


def solution(mesh):
    placed = (P("space", None, "tm"), P("space", None), P(), P(), P("space", None, None))
    return jax.shard_map(
        local,
        mesh=mesh,
        in_specs=placed,
        out_specs=(P("space", None, "tm"), P("tm", None)),
        check_vma=False,
    )
```

```python
import functools

import jax
import jax.numpy as jnp
from jax import lax
from jax.experimental import pallas as pl
from jax.experimental.pallas import tpu as pltpu
from jax.sharding import PartitionSpec as P

SIGN_STEPS = 8
TAPS = 6
CHUNK = 8
ROW_BLOCKS = 2
F32 = jnp.float32
VMEM_LIMIT = 48 * 1024 * 1024


def params():
    return pltpu.CompilerParams(vmem_limit_bytes=VMEM_LIMIT)


def whole():
    return pl.BlockSpec(memory_space=pltpu.VMEM)


def scalars():
    return pl.BlockSpec(memory_space=pltpu.SMEM)


def swap(x, axis, mask):
    count = lax.axis_size(axis)
    return lax.ppermute(x, axis, [(i, i ^ mask) for i in range(count)])


def swap_both(x, mask):
    parts, patches = lax.axis_size("tm"), lax.axis_size("space")
    route = []
    for t in range(parts):
        for s in range(patches):
            there = (t ^ (mask % parts)) * patches + (s ^ (mask // parts))
            route.append((t * patches + s, there))
    return lax.ppermute(x, ("tm", "space"), route)


def shift_rows(x, by):
    edge = jnp.zeros((1, x.shape[1]), x.dtype)
    if by > 0:
        return jnp.concatenate([edge, x[:-1]], axis=0)
    return jnp.concatenate([x[1:], edge], axis=0)


def mask_columns(mask, mask_t):
    mask_t[...] = mask.astype(F32).T
    half = mask.shape[1] // 2
    return mask_t[pl.ds(0, half, stride=2), :], mask_t[pl.ds(1, half, stride=2), :]


def narrowed_row(snaps, x, mask, taps):
    half = snaps.shape[1] // 2
    even = snaps[x, pl.ds(0, half, stride=2), :] * mask[0]
    odd = snaps[x, pl.ds(1, half, stride=2), :] * mask[1]
    before = taps[0] * even + taps[1] * odd
    here = taps[2] * even + taps[3] * odd
    after = taps[4] * even + taps[5] * odd
    return shift_rows(before, 1) + here + shift_rows(after, -1)


def edge_kernel(rtaps_ref, ctaps_ref, first_ref, last_ref, mask_first_ref, mask_last_ref, near_ref, far_ref, mask_t):
    ctaps = [ctaps_ref[k] for k in range(TAPS)]
    even = lax.axis_index("space") % 2 == 0
    shares = []
    for snaps, mask_ref, taps, at in (
        (first_ref, mask_first_ref, (rtaps_ref[4], rtaps_ref[5]), 0),
        (last_ref, mask_last_ref, (rtaps_ref[0], rtaps_ref[1]), CHUNK - 2),
    ):
        masks = mask_columns(mask_ref[...], mask_t)
        rows = [narrowed_row(snaps, x, [m[:, at + x:at + x + 1] for m in masks], ctaps) for x in range(2)]
        shares.append(taps[0] * rows[0] + taps[1] * rows[1])
    up, down = shares
    near_ref[...] = jnp.where(even, down, up)
    far_ref[...] = jnp.where(even, up, down)


def filter_kernel(parts, rtaps_ref, ctaps_ref, snap_hbm, mask_ref, *rest):
    pieces, (snaps, sems, mask_t, spread, narrowed, filtered) = rest[:parts], rest[parts:]
    rows, cells = narrowed.shape[0] - 4, narrowed.shape[1]
    me = lax.axis_index("tm")
    chunks = rows // CHUNK

    def fetch(c):
        at = pl.ds(c * CHUNK, CHUNK)
        return pltpu.make_async_copy(snap_hbm.at[at], snaps.at[at], sems.at[c])

    for c in range(chunks):
        fetch(c).start()

    rtaps = [rtaps_ref[k] for k in range(TAPS)]
    ctaps = [ctaps_ref[k] for k in range(TAPS)]
    edge = jnp.zeros((2,) + narrowed.shape[1:], F32)
    narrowed[0:2] = edge
    narrowed[rows + 2:rows + 4] = edge

    masks = mask_columns(mask_ref[...], mask_t)
    for x in range(rows):
        for j, mask in enumerate(masks):
            spread[x, j] = jnp.broadcast_to(mask[:, x:x + 1], (cells, narrowed.shape[2]))

    def narrow(c, carry):
        fetch(c).wait()
        base = pl.multiple_of(c * CHUNK, CHUNK)
        for x in range(CHUNK):
            row = narrowed_row(snaps, base + x, spread[base + x], ctaps)
            narrowed[base + 2 + x] = row
        return carry

    lax.fori_loop(0, chunks, narrow, 0)
    for i in range(rows // 2):
        total = rtaps[0] * narrowed[2 * i]
        for k in range(1, TAPS):
            total = total + rtaps[k] * narrowed[2 * i + k]
        filtered[i * cells:(i + 1) * cells, :] = total
    size = filtered.shape[0] // parts
    for k in range(parts):
        pieces[k][...] = filtered[pl.ds(pl.multiple_of((me ^ k) * size, 8), size), :]


def halo_kernel(parts, near_ref, far_ref, *refs):
    outs = refs[len(refs) // 2:]
    me = lax.axis_index("tm")
    cells = near_ref.shape[0]
    even = lax.axis_index("space") % 2 == 0
    above = jnp.where(even, far_ref[...], near_ref[...])
    below = jnp.where(even, near_ref[...], far_ref[...])
    for k, out in enumerate(outs):
        out[...] = refs[k][...]

        @pl.when((me ^ k) == 0)
        def _():
            out[:cells, :] = out[:cells, :] + above

        @pl.when((me ^ k) == parts - 1)
        def _():
            out[-cells:, :] = out[-cells:, :] + below


def cross_order(parts):
    return [(a, b) for p in range(0, parts, 2) for q in range(p + 2, parts, 2) for a in (p, p + 1) for b in (q, q + 1)]


def triangle(size):
    return tuple(lax.broadcasted_iota(jnp.int32, (size, size), axis) for axis in range(2))


def pair_rows(cols):
    return 2 * cols + 16


def pair_kernel(parts, span, probes_ref, *refs):
    half = parts // 2
    owners = 2 * span
    mine, theirs, refs = refs[:half], refs[half:2 * half], refs[2 * half:]
    outs, (wide, there, flat, products) = refs[:owners], refs[owners:]
    me, owner = positions(2, span)
    size, cols = mine[0].shape
    low = pl.ds(pl.multiple_of((me % 2) * cols, cols), cols)
    high = pl.ds(pl.multiple_of((1 - me % 2) * cols, cols), cols)
    for h in range(half):
        at = pl.ds(h * size, size)
        wide[at, low] = mine[h][...]
        wide[at, high] = theirs[h][...]
        there[at, :] = probes_ref[pl.ds(pl.multiple_of((me ^ 2 * h) * size, 8), size), :]
    left = split(wide[...])
    gram = dot_parts(left, left, ((0,), (0,)))
    first, second = gram[:cols, :cols], gram[cols:, cols:]
    row, col = triangle(cols)
    flat[:cols, :] = gram[:cols, cols:]
    flat[cols:2 * cols, :] = jnp.where(row <= col, first, second)
    products[...] = dot_parts(left, split(there[...]), ((0,), (0,)))
    diagonal = jnp.sum(jnp.where(row == col, second, 0.0), axis=0, keepdims=True)
    flat[2 * cols:, :] = jnp.broadcast_to(diagonal, (flat.shape[0] - 2 * cols, cols))
    share, rest = flat.shape[0] // 2, 2 * cols // owners
    for k, out in enumerate(outs):
        out[:share, :] = flat[pl.ds(pl.multiple_of(((owner ^ k) % 2) * share, 8), share), :]
        out[share:, :] = products[pl.ds(pl.multiple_of((owner ^ k) * rest, 8), rest), :]


def positions(count, span):
    me = lax.axis_index("tm")
    return me, me % count + count * (lax.axis_index("space") % span)


def give(owner, flat, send_ref, keep_ref):
    count = 2 * send_ref.shape[0]
    share = flat.shape[0] // count
    for k in range(count):
        out = send_ref if k % 2 else keep_ref
        out[k // 2] = flat[pl.ds(pl.multiple_of((owner ^ k) * share, 8), share), :]


def cross_kernel(parts, span, *refs):
    pieces, (send_ref, keep_ref, high_ref, low_ref, wide, flat) = refs[:parts], refs[parts:]
    me, owner = positions(parts, span)
    cols = pieces[0].shape[1]
    for k in range(parts):
        wide[:, pl.ds(pl.multiple_of((me ^ k) * cols, cols), cols)] = pieces[k][...]
    sides = [split(wide[:, a * cols:(a + 2) * cols]) for a in range(0, parts, 2)]
    for at, (high, low) in enumerate(sides):
        high_ref[:, 2 * at * cols:2 * (at + 1) * cols] = high
        low_ref[:, 2 * at * cols:2 * (at + 1) * cols] = low
    where = {ab: j for j, ab in enumerate(cross_order(parts))}
    for a in range(0, parts, 2):
        for b in range(a + 2, parts, 2):
            prod = dot_parts(sides[a // 2], sides[b // 2], ((0,), (0,)))
            for i in range(2):
                for j in range(2):
                    at = where[a + i, b + j] * cols
                    flat[at:at + cols, :] = prod[i * cols:(i + 1) * cols, j * cols:(j + 1) * cols]
    give(owner, flat, send_ref, keep_ref)


def split(x):
    high = x.astype(jnp.bfloat16)
    return high, (x - high.astype(F32)).astype(jnp.bfloat16)


def dot(a, b, dims):
    return lax.dot_general(a, b, (dims, ((), ())), preferred_element_type=F32)


def dot_parts(a, b, dims=((1,), (0,))):
    (ah, al), (bh, bl) = a, b
    left = jnp.concatenate([ah, ah, al], axis=dims[0][0])
    return dot(left, jnp.concatenate([bh, bl, bh], axis=dims[1][0]), dims)


def split_dot(a, b, dims=((1,), (0,))):
    return dot_parts(split(a), split(b), dims)


def next_sign(y):
    whole_y = split(y)
    size = y.shape[0] // ROW_BLOCKS
    blocks = []
    for at in range(0, y.shape[0], size):
        square = dot_parts([part[at:at + size] for part in whole_y], whole_y)
        blocks.append(1.5 * y[at:at + size] - 0.5 * dot_parts(split(square), whole_y))
    return jnp.concatenate(blocks, axis=0)


def combine_of(grams):
    order = grams[0].shape[0]
    diagonal = lax.broadcasted_iota(jnp.int32, (order, order), 0) == lax.broadcasted_iota(jnp.int32, (order, order), 1)
    signs = []
    for gram in grams:
        mean = jnp.sum(jnp.where(diagonal, gram, 0.0)) / order
        shifted = jnp.where(diagonal, gram - mean, gram)
        signs.append(shifted / jnp.sqrt(jnp.sum(shifted * shifted, keepdims=True) + 1e-6))
    for _ in range(SIGN_STEPS - 1):
        signs = [next_sign(y) for y in signs]
    half = order // 2
    combines = []
    for y in signs:
        whole_y = split(y)
        folded = y[:, :half] + y[:, half:]
        cubed = dot_parts(whole_y, split(dot_parts(whole_y, split(folded))))
        ones = jnp.where(diagonal[:, :half] | diagonal[:, half:], 1.0, 0.0)
        combines.append(0.5 * (ones + (1.5 * folded - 0.5 * cubed)))
    return combines


def place_shares(parts, span, even_ref, odd_ref, put):
    _, owner = positions(parts, span)
    for k in range(parts * span):
        put(owner ^ k, (odd_ref if k % 2 else even_ref)[k // 2])


def pair_at(parts, step, j, core):
    return j if step == parts // 2 else 2 * j + core


def level_kernel(parts, even_ref, odd_ref, out_ref, pairs):
    cols = even_ref.shape[2]
    share = pairs.shape[1] // 2

    def put(there, rows):
        pairs[there // 2, pl.ds(pl.multiple_of((there % 2) * share, 8), share), :] = rows

    place_shares(parts, 1, even_ref, odd_ref, put)
    row, col = triangle(cols)
    grams = []
    step = out_ref.shape[0]
    for j in range(step):
        p = pair_at(parts, step, j, lax.axis_index("tm") % 2)
        packed = pairs[p, cols:2 * cols, :]
        turned_back = packed.T
        first = jnp.where(row <= col, packed, turned_back)
        between = pairs[p, :cols, :]
        second = jnp.where(row > col, packed, turned_back)
        second = jnp.where(row == col, pairs[p, 2 * cols:2 * cols + 1, :], second)
        grams.append(jnp.concatenate([
            jnp.concatenate([first, between], axis=1), jnp.concatenate([between.T, second], axis=1)
        ], axis=0))
    for j, (gram, combine) in enumerate(zip(grams, combine_of(grams))):
        out_ref[j, :2 * cols, :] = combine
        out_ref[j, 2 * cols:, :] = split_dot(combine, split_dot(gram, combine), ((0,), (0,)))


def merge_kernel(parts, span, even_ref, odd_ref, mine_ref, theirs_ref, high_ref, low_ref, *refs):
    outs, (weight_ref, product_ref, level, cross, turned) = refs[:parts], refs[parts:]
    me = lax.axis_index("tm")
    cols = even_ref.shape[2]
    share = cross.shape[0] // (parts * span)

    rest = 2 * cols // (2 * span)

    def put(there, rows):
        cross[pl.ds(pl.multiple_of(there * share, 8), share), :] = rows[:share]
        at = ((there % parts) // 2) * 2 * cols + (there % 2 + 2 * (there // parts)) * rest
        product_ref[pl.ds(pl.multiple_of(at, 8), rest), :] = rows[share:]

    place_shares(parts, span, even_ref, odd_ref, put)
    where = {ab: j * cols for j, ab in enumerate(cross_order(parts))}
    step = mine_ref.shape[0]
    for j in range(step):
        level[pair_at(parts, step, j, 1 - me % 2)] = theirs_ref[j]
        level[pair_at(parts, step, j, me % 2)] = mine_ref[j]
    weights = [level[p, :2 * cols, :] for p in range(parts // 2)]
    blocks = {(p, p): level[p, 2 * cols:, :] for p in range(parts // 2)}
    for p in range(parts // 2):
        for q in range(p + 1, parts // 2):
            between = jnp.concatenate([
                jnp.concatenate([cross[where[a, b]:where[a, b] + cols, :] for b in (2 * q, 2 * q + 1)], axis=1)
                for a in (2 * p, 2 * p + 1)
            ], axis=0)
            blocks[p, q] = split_dot(weights[p], split_dot(between, weights[q]), ((0,), (0,)))
    count = parts // 2
    while count > 1:
        grams = []
        for p in range(0, count, 2):
            low = jnp.concatenate([blocks[p, p], blocks[p, p + 1]], axis=1)
            high = jnp.concatenate([blocks[p, p + 1].T, blocks[p + 1, p + 1]], axis=1)
            grams.append(jnp.concatenate([low, high], axis=0))
        combines = combine_of(grams)
        per = len(weights) // len(combines)
        weights = [
            split_dot(w, combines[i // per][(i % per) * cols:(i % per + 1) * cols, :])
            for i, w in enumerate(weights)
        ]
        weights = [jnp.concatenate(weights[i:i + per], axis=0) for i in range(0, len(weights), per)]
        merged = {}
        if count > 2:
            for p in range(count // 2):
                for q in range(p, count // 2):
                    if p == q:
                        between = grams[p]
                    else:
                        between = jnp.concatenate([
                            jnp.concatenate([blocks[2 * p + i, 2 * q], blocks[2 * p + i, 2 * q + 1]], axis=1)
                            for i in range(2)
                        ], axis=0)
                    right = split_dot(between, combines[q])
                    merged[p, q] = split_dot(combines[p], right, ((0,), (0,)))
        blocks, count = merged, count // 2
    weight_ref[...] = weights[0]
    width = cols // parts
    turned[...] = dot_parts((high_ref[...], low_ref[...]), split(weights[0])).T
    for k in range(parts):
        outs[k][...] = turned[pl.ds(pl.multiple_of((me ^ k) * width, 8), width), :]


def coefficient_kernel(parts, weight_ref, product_ref, coef_ref, held):
    held[...] = split_dot(weight_ref[...], product_ref[...], ((0,), (0,)))
    width = coef_ref.shape[0]
    coef_ref[...] = held[pl.ds(pl.multiple_of(lax.axis_index("tm") * width, 8), width), :]


def final_kernel(parts, *refs):
    pieces, basis_ref = refs[:parts], refs[parts]
    me = lax.axis_index("tm")
    per, cells = basis_ref.shape[0] // parts, basis_ref.shape[2]
    for k in range(parts):
        base = (me ^ k) * per
        for i in range(per):
            basis_ref[base + i] = pieces[k][:, i * cells:(i + 1) * cells]


def shape(*dims):
    return jax.ShapeDtypeStruct(dims, F32)


def local(snapshots, land_mask, taps_rows, taps_cols, probes):
    rows, grid_cols, cols = snapshots.shape
    half_rows, half_cols = rows // 2, grid_cols // 2
    parts, patches = lax.axis_size("tm"), lax.axis_size("space")
    cells = half_rows * half_cols
    piece = cells // parts
    span = 2 if patches > 1 else 1

    snapshots, land_mask, taps_rows, taps_cols = (
        pltpu.with_memory_space_constraint(x, pltpu.HBM) for x in (snapshots, land_mask, taps_rows, taps_cols)
    )

    row_block, mask_block = (2, grid_cols, cols), (CHUNK, grid_cols)
    to_near, to_far = pl.pallas_call(
        edge_kernel,
        out_shape=[shape(half_cols, cols)] * 2,
        grid=(1,),
        in_specs=[
            scalars(), scalars(),
            pl.BlockSpec(row_block, lambda i: (0, 0, 0)),
            pl.BlockSpec(row_block, lambda i: (rows // 2 - 1, 0, 0)),
            pl.BlockSpec(mask_block, lambda i: (0, 0)),
            pl.BlockSpec(mask_block, lambda i: (rows // CHUNK - 1, 0)),
        ],
        out_specs=[pl.BlockSpec((half_cols, cols), lambda i: (0, 0))] * 2,
        scratch_shapes=[pltpu.VMEM((grid_cols, CHUNK), F32)],
        compiler_params=params(),
        name="edge",
    )(taps_rows, taps_cols, snapshots, snapshots, land_mask, land_mask)
    near = lax.ppermute(to_near, "space", [(i, i ^ 1) for i in range(patches) if i ^ 1 < patches])
    pairs = [(i, i + 1) for i in range(1, patches - 1, 2)]
    other = lax.ppermute(to_far, "space", pairs + [(j, i) for i, j in pairs])

    pieces = pl.pallas_call(
        functools.partial(filter_kernel, parts),
        out_shape=[shape(piece, cols)] * parts,
        in_specs=[scalars(), scalars(), pl.BlockSpec(memory_space=pltpu.HBM), whole()],
        out_specs=[whole()] * parts,
        scratch_shapes=[
            pltpu.VMEM((rows, grid_cols, cols), F32),
            pltpu.SemaphoreType.DMA((rows // CHUNK,)),
            pltpu.VMEM((grid_cols, rows), F32),
            pltpu.VMEM((rows, 2, half_cols, cols), F32),
            pltpu.VMEM((rows + 4, half_cols, cols), F32),
            pltpu.VMEM((cells, cols), F32),
        ],
        compiler_params=params(),
        cost_estimate=pl.CostEstimate(flops=0, bytes_accessed=4 * snapshots.size, transcendentals=0),
        name="filter",
    )(taps_rows, taps_cols, snapshots, land_mask)
    kept = pl.pallas_call(
        functools.partial(halo_kernel, parts),
        out_shape=[shape(piece, cols)] * parts,
        in_specs=[whole()] * (parts + 2),
        out_specs=[whole()] * parts,
        input_output_aliases={2 + k: k for k in range(parts)},
        compiler_params=params(),
        name="halo",
    )(near, other, *pieces)
    theirs = {k: swap(kept[k + 1], "tm", 1) for k in range(0, parts, 2)}
    far = {0: kept[0], 1: theirs[0]}
    for k in range(2, parts, 2):
        far[k] = swap(kept[k], "tm", k)
        far[k + 1] = swap(theirs[k], "tm", k)

    owners = 2 * span
    pair_size = pair_rows(cols) // 2
    sums = pl.pallas_call(
        functools.partial(pair_kernel, parts, span),
        out_shape=[shape(pair_size + 2 * cols // owners, cols)] * owners,
        in_specs=[whole()] * (parts + 1),
        out_specs=[whole()] * owners,
        scratch_shapes=[
            pltpu.VMEM((cells // 2, 2 * cols), F32),
            pltpu.VMEM((cells // 2, cols), F32),
            pltpu.VMEM((pair_rows(cols), cols), F32),
            pltpu.VMEM((2 * cols, cols), F32),
        ],
        compiler_params=params(),
        cost_estimate=pl.CostEstimate(flops=0, bytes_accessed=0, transcendentals=0),
        name="pair",
    )(probes.reshape(cells, cols), *[kept[k] for k in range(0, parts, 2)], *[theirs[k] for k in range(0, parts, 2)])
    got = [swap_both(sums[j], j % 2 + parts * (j // 2)) for j in range(1, owners)]
    tied = lax.optimization_barrier(got + [far[k] for k in range(2, parts)])
    got = tied[:owners - 1]
    far.update(zip(range(2, parts), tied[owners - 1:]))
    pair_share = sums[0] + got[0]
    if span > 1:
        pair_share = pair_share + (got[1] + got[2])
    bits = [1 << b for b in range(1, patches.bit_length() - 1)]

    blocks = len(cross_order(parts))
    owners = parts * span
    size = blocks * cols // owners
    factors = jax.ShapeDtypeStruct((piece, parts * cols), jnp.bfloat16)
    send, keep, high, low = pl.pallas_call(
        functools.partial(cross_kernel, parts, span),
        out_shape=[shape(owners // 2, size, cols)] * 2 + [factors] * 2,
        in_specs=[whole()] * parts,
        out_specs=[whole()] * 4,
        scratch_shapes=[pltpu.VMEM((piece, parts * cols), F32), pltpu.VMEM((blocks * cols, cols), F32)],
        compiler_params=params(),
        cost_estimate=pl.CostEstimate(flops=0, bytes_accessed=0, transcendentals=0),
        name="cross",
    )(*[far[k] for k in range(parts)])
    got = swap(send, "tm", 1)
    mine = keep[0] + got[0]
    for h in range(1, owners // 2):
        mine = mine + swap_both(keep[h] + got[h], 2 * h)
    for bit in bits[:1]:
        pair_share = pair_share + swap(pair_share, "space", bit)
    mine, pair_share = lax.optimization_barrier((mine, pair_share))
    pair_share, product_share = pair_share[:pair_size], pair_share[pair_size:]
    for bit in bits[1:]:
        pair_share = pair_share + swap(pair_share, "space", bit)
    for bit in bits[:1]:
        mine = mine + swap(mine, "space", bit)
    mine, pair_share = lax.optimization_barrier((mine, pair_share))
    mine = jnp.concatenate([mine, product_share], axis=0)
    for bit in bits[1:]:
        mine = mine + swap(mine, "space", bit)

    def spread(x, count):
        return [x] + [swap_both(x, 2 * h) for h in range(1, count // 2)]

    def gathered(shares):
        even = jnp.stack(shares)
        return even, swap(even, "tm", 1)

    mine, *pair_shares = lax.optimization_barrier([mine] + spread(pair_share, parts))

    half = parts // 2
    level = pl.pallas_call(
        functools.partial(level_kernel, parts),
        out_shape=shape(half // 2 if half % 2 == 0 else half, 3 * cols, cols),
        in_specs=[whole()] * 2,
        out_specs=whole(),
        scratch_shapes=[pltpu.VMEM((half, pair_rows(cols), cols), F32)],
        compiler_params=params(),
        cost_estimate=pl.CostEstimate(flops=parts * SIGN_STEPS * 6 * (2 * cols) ** 3, bytes_accessed=0, transcendentals=0),
        name="level",
    )(*gathered(pair_shares))
    level, *shares = lax.optimization_barrier([level] + spread(mine, owners))
    other_level = swap(level, "tm", 1)
    width = cols // parts
    *sent, weight, products = pl.pallas_call(
        functools.partial(merge_kernel, parts, span),
        out_shape=[shape(width, piece)] * parts + [shape(parts * cols, cols)] * 2,
        in_specs=[whole()] * 6,
        out_specs=[whole()] * (parts + 2),
        scratch_shapes=[
            pltpu.VMEM((half, 3 * cols, cols), F32),
            pltpu.VMEM((blocks * cols, cols), F32),
            pltpu.VMEM((cols, piece), F32),
        ],
        compiler_params=params(),
        name="merge",
    )(*gathered(shares), level, other_level, high, low)
    coefficients = pl.pallas_call(
        functools.partial(coefficient_kernel, parts),
        out_shape=shape(width, cols),
        in_specs=[whole()] * 2,
        out_specs=whole(),
        scratch_shapes=[pltpu.VMEM((cols, cols), F32)],
        compiler_params=params(),
        name="coefficients",
    )(weight, products)
    last = [sent[0]] + [swap(sent[k], "tm", k) for k in range(1, parts)]

    basis = pl.pallas_call(
        functools.partial(final_kernel, parts),
        out_shape=shape(half_rows, width, half_cols),
        in_specs=[whole()] * parts,
        out_specs=whole(),
        compiler_params=params(),
        name="final",
    )(*last)
    return basis.transpose(0, 2, 1), coefficients


def solution(mesh):
    placed = (P("space", None, "tm"), P("space", None), P(), P(), P("space", None, None))
    return jax.shard_map(
        local,
        mesh=mesh,
        in_specs=placed,
        out_specs=(P("space", None, "tm"), P("tm", None)),
        check_vma=False,
    )
```

```python
import functools

import jax
import jax.numpy as jnp
from jax import lax
from jax.experimental import pallas as pl
from jax.experimental.pallas import tpu as pltpu
from jax.sharding import PartitionSpec as P

SIGN_STEPS = 8
TAPS = 6
CHUNK = 8
ROW_BLOCKS = 1
F32 = jnp.float32
VMEM_LIMIT = 48 * 1024 * 1024


def params():
    return pltpu.CompilerParams(vmem_limit_bytes=VMEM_LIMIT)


def whole():
    return pl.BlockSpec(memory_space=pltpu.VMEM)


def scalars():
    return pl.BlockSpec(memory_space=pltpu.SMEM)


def swap(x, axis, mask):
    count = lax.axis_size(axis)
    return lax.ppermute(x, axis, [(i, i ^ mask) for i in range(count)])


def swap_both(x, mask):
    parts, patches = lax.axis_size("tm"), lax.axis_size("space")
    route = []
    for t in range(parts):
        for s in range(patches):
            there = (t ^ (mask % parts)) * patches + (s ^ (mask // parts))
            route.append((t * patches + s, there))
    return lax.ppermute(x, ("tm", "space"), route)


def shift_rows(x, by):
    edge = jnp.zeros((1, x.shape[1]), x.dtype)
    if by > 0:
        return jnp.concatenate([edge, x[:-1]], axis=0)
    return jnp.concatenate([x[1:], edge], axis=0)


def mask_columns(mask, mask_t):
    mask_t[...] = mask.astype(F32).T
    half = mask.shape[1] // 2
    return mask_t[pl.ds(0, half, stride=2), :], mask_t[pl.ds(1, half, stride=2), :]


def narrowed_row(snaps, x, mask, taps):
    half = snaps.shape[1] // 2
    even = snaps[x, pl.ds(0, half, stride=2), :] * mask[0]
    odd = snaps[x, pl.ds(1, half, stride=2), :] * mask[1]
    before = taps[0] * even + taps[1] * odd
    here = taps[2] * even + taps[3] * odd
    after = taps[4] * even + taps[5] * odd
    return shift_rows(before, 1) + here + shift_rows(after, -1)


def edge_kernel(rtaps_ref, ctaps_ref, first_ref, last_ref, mask_first_ref, mask_last_ref, near_ref, far_ref, mask_t):
    ctaps = [ctaps_ref[k] for k in range(TAPS)]
    even = lax.axis_index("space") % 2 == 0
    shares = []
    for snaps, mask_ref, taps, at in (
        (first_ref, mask_first_ref, (rtaps_ref[4], rtaps_ref[5]), 0),
        (last_ref, mask_last_ref, (rtaps_ref[0], rtaps_ref[1]), CHUNK - 2),
    ):
        masks = mask_columns(mask_ref[...], mask_t)
        rows = [narrowed_row(snaps, x, [m[:, at + x:at + x + 1] for m in masks], ctaps) for x in range(2)]
        shares.append(taps[0] * rows[0] + taps[1] * rows[1])
    up, down = shares
    near_ref[...] = jnp.where(even, down, up)
    far_ref[...] = jnp.where(even, up, down)


def filter_kernel(parts, rtaps_ref, ctaps_ref, snap_hbm, mask_ref, *rest):
    pieces, (snaps, sems, mask_t, spread, narrowed, filtered) = rest[:parts], rest[parts:]
    rows, cells = narrowed.shape[0] - 4, narrowed.shape[1]
    me = lax.axis_index("tm")
    chunks = rows // CHUNK

    def fetch(c):
        at = pl.ds(c * CHUNK, CHUNK)
        return pltpu.make_async_copy(snap_hbm.at[at], snaps.at[at], sems.at[c])

    for c in range(chunks):
        fetch(c).start()

    rtaps = [rtaps_ref[k] for k in range(TAPS)]
    ctaps = [ctaps_ref[k] for k in range(TAPS)]
    edge = jnp.zeros((2,) + narrowed.shape[1:], F32)
    narrowed[0:2] = edge
    narrowed[rows + 2:rows + 4] = edge

    masks = mask_columns(mask_ref[...], mask_t)
    for x in range(rows):
        for j, mask in enumerate(masks):
            spread[x, j] = jnp.broadcast_to(mask[:, x:x + 1], (cells, narrowed.shape[2]))

    def narrow(c, carry):
        fetch(c).wait()
        base = pl.multiple_of(c * CHUNK, CHUNK)
        for x in range(CHUNK):
            row = narrowed_row(snaps, base + x, spread[base + x], ctaps)
            narrowed[base + 2 + x] = row
        return carry

    lax.fori_loop(0, chunks, narrow, 0)
    for i in range(rows // 2):
        total = rtaps[0] * narrowed[2 * i]
        for k in range(1, TAPS):
            total = total + rtaps[k] * narrowed[2 * i + k]
        filtered[i * cells:(i + 1) * cells, :] = total
    size = filtered.shape[0] // parts
    for k in range(parts):
        pieces[k][...] = filtered[pl.ds(pl.multiple_of((me ^ k) * size, 8), size), :]


def halo_kernel(parts, near_ref, far_ref, *refs):
    outs = refs[len(refs) // 2:]
    me = lax.axis_index("tm")
    cells = near_ref.shape[0]
    even = lax.axis_index("space") % 2 == 0
    above = jnp.where(even, far_ref[...], near_ref[...])
    below = jnp.where(even, near_ref[...], far_ref[...])
    for k, out in enumerate(outs):
        out[...] = refs[k][...]

        @pl.when((me ^ k) == 0)
        def _():
            out[:cells, :] = out[:cells, :] + above

        @pl.when((me ^ k) == parts - 1)
        def _():
            out[-cells:, :] = out[-cells:, :] + below


def cross_order(parts):
    return [(a, b) for p in range(0, parts, 2) for q in range(p + 2, parts, 2) for a in (p, p + 1) for b in (q, q + 1)]


def triangle(size):
    return tuple(lax.broadcasted_iota(jnp.int32, (size, size), axis) for axis in range(2))


def pair_rows(cols):
    return 2 * cols + 16


def pair_kernel(parts, span, probes_ref, *refs):
    half = parts // 2
    owners = 2 * span
    mine, theirs, refs = refs[:half], refs[half:2 * half], refs[2 * half:]
    outs, (wide, there, flat, products) = refs[:owners], refs[owners:]
    me, owner = positions(2, span)
    size, cols = mine[0].shape
    low = pl.ds(pl.multiple_of((me % 2) * cols, cols), cols)
    high = pl.ds(pl.multiple_of((1 - me % 2) * cols, cols), cols)
    for h in range(half):
        at = pl.ds(h * size, size)
        wide[at, low] = mine[h][...]
        wide[at, high] = theirs[h][...]
        there[at, :] = probes_ref[pl.ds(pl.multiple_of((me ^ 2 * h) * size, 8), size), :]
    left = split(wide[...])
    gram = dot_parts(left, left, ((0,), (0,)))
    first, second = gram[:cols, :cols], gram[cols:, cols:]
    row, col = triangle(cols)
    flat[:cols, :] = gram[:cols, cols:]
    flat[cols:2 * cols, :] = jnp.where(row <= col, first, second)
    products[...] = dot_parts(left, split(there[...]), ((0,), (0,)))
    diagonal = jnp.sum(jnp.where(row == col, second, 0.0), axis=0, keepdims=True)
    flat[2 * cols:, :] = jnp.broadcast_to(diagonal, (flat.shape[0] - 2 * cols, cols))
    share, rest = flat.shape[0] // 2, 2 * cols // owners
    for k, out in enumerate(outs):
        out[:share, :] = flat[pl.ds(pl.multiple_of(((owner ^ k) % 2) * share, 8), share), :]
        out[share:, :] = products[pl.ds(pl.multiple_of((owner ^ k) * rest, 8), rest), :]


def positions(count, span):
    me = lax.axis_index("tm")
    return me, me % count + count * (lax.axis_index("space") % span)


def give(owner, flat, send_ref, keep_ref):
    count = 2 * send_ref.shape[0]
    share = flat.shape[0] // count
    for k in range(count):
        out = send_ref if k % 2 else keep_ref
        out[k // 2] = flat[pl.ds(pl.multiple_of((owner ^ k) * share, 8), share), :]


def cross_kernel(parts, span, *refs):
    pieces, (send_ref, keep_ref, high_ref, low_ref, wide, flat) = refs[:parts], refs[parts:]
    me, owner = positions(parts, span)
    cols = pieces[0].shape[1]
    for k in range(parts):
        wide[:, pl.ds(pl.multiple_of((me ^ k) * cols, cols), cols)] = pieces[k][...]
    sides = [split(wide[:, a * cols:(a + 2) * cols]) for a in range(0, parts, 2)]
    for at, (high, low) in enumerate(sides):
        high_ref[:, 2 * at * cols:2 * (at + 1) * cols] = high
        low_ref[:, 2 * at * cols:2 * (at + 1) * cols] = low
    where = {ab: j for j, ab in enumerate(cross_order(parts))}
    for a in range(0, parts, 2):
        for b in range(a + 2, parts, 2):
            prod = dot_parts(sides[a // 2], sides[b // 2], ((0,), (0,)))
            for i in range(2):
                for j in range(2):
                    at = where[a + i, b + j] * cols
                    flat[at:at + cols, :] = prod[i * cols:(i + 1) * cols, j * cols:(j + 1) * cols]
    give(owner, flat, send_ref, keep_ref)


def split(x):
    high = x.astype(jnp.bfloat16)
    return high, (x - high.astype(F32)).astype(jnp.bfloat16)


def dot(a, b, dims):
    return lax.dot_general(a, b, (dims, ((), ())), preferred_element_type=F32)


def dot_parts(a, b, dims=((1,), (0,))):
    (ah, al), (bh, bl) = a, b
    left = jnp.concatenate([ah, ah, al], axis=dims[0][0])
    return dot(left, jnp.concatenate([bh, bl, bh], axis=dims[1][0]), dims)


def split_dot(a, b, dims=((1,), (0,))):
    return dot_parts(split(a), split(b), dims)


def next_sign(y):
    whole_y = split(y)
    size = y.shape[0] // ROW_BLOCKS
    blocks = []
    for at in range(0, y.shape[0], size):
        square = dot_parts([part[at:at + size] for part in whole_y], whole_y)
        blocks.append(1.5 * y[at:at + size] - 0.5 * dot_parts(split(square), whole_y))
    return jnp.concatenate(blocks, axis=0)


def combine_of(grams):
    order = grams[0].shape[0]
    diagonal = lax.broadcasted_iota(jnp.int32, (order, order), 0) == lax.broadcasted_iota(jnp.int32, (order, order), 1)
    signs = []
    for gram in grams:
        mean = jnp.sum(jnp.where(diagonal, gram, 0.0)) / order
        shifted = jnp.where(diagonal, gram - mean, gram)
        signs.append(shifted / jnp.sqrt(jnp.sum(shifted * shifted, keepdims=True) + 1e-6))
    for _ in range(SIGN_STEPS):
        signs = [next_sign(y) for y in signs]
    half = order // 2
    combines = []
    for y in signs:
        projector = 0.5 * (jnp.where(diagonal, 1.0, 0.0) + y)
        combines.append(projector[:, :half] + projector[:, half:])
    return combines


def place_shares(parts, span, even_ref, odd_ref, put):
    _, owner = positions(parts, span)
    for k in range(parts * span):
        put(owner ^ k, (odd_ref if k % 2 else even_ref)[k // 2])


def pair_at(parts, step, j, core):
    return j if step == parts // 2 else 2 * j + core


def level_kernel(parts, even_ref, odd_ref, out_ref, pairs):
    cols = even_ref.shape[2]
    share = pairs.shape[1] // 2

    def put(there, rows):
        pairs[there // 2, pl.ds(pl.multiple_of((there % 2) * share, 8), share), :] = rows

    place_shares(parts, 1, even_ref, odd_ref, put)
    row, col = triangle(cols)
    grams = []
    step = out_ref.shape[0]
    for j in range(step):
        p = pair_at(parts, step, j, lax.axis_index("tm") % 2)
        packed = pairs[p, cols:2 * cols, :]
        turned_back = packed.T
        first = jnp.where(row <= col, packed, turned_back)
        between = pairs[p, :cols, :]
        second = jnp.where(row > col, packed, turned_back)
        second = jnp.where(row == col, pairs[p, 2 * cols:2 * cols + 1, :], second)
        grams.append(jnp.concatenate([
            jnp.concatenate([first, between], axis=1), jnp.concatenate([between.T, second], axis=1)
        ], axis=0))
    for j, (gram, combine) in enumerate(zip(grams, combine_of(grams))):
        out_ref[j, :2 * cols, :] = combine
        out_ref[j, 2 * cols:, :] = split_dot(combine, split_dot(gram, combine), ((0,), (0,)))


def merge_kernel(parts, span, even_ref, odd_ref, mine_ref, theirs_ref, high_ref, low_ref, *refs):
    outs, (weight_ref, product_ref, level, cross, turned) = refs[:parts], refs[parts:]
    me = lax.axis_index("tm")
    cols = even_ref.shape[2]
    share = cross.shape[0] // (parts * span)

    rest = 2 * cols // (2 * span)

    def put(there, rows):
        cross[pl.ds(pl.multiple_of(there * share, 8), share), :] = rows[:share]
        at = ((there % parts) // 2) * 2 * cols + (there % 2 + 2 * (there // parts)) * rest
        product_ref[pl.ds(pl.multiple_of(at, 8), rest), :] = rows[share:]

    place_shares(parts, span, even_ref, odd_ref, put)
    where = {ab: j * cols for j, ab in enumerate(cross_order(parts))}
    step = mine_ref.shape[0]
    for j in range(step):
        level[pair_at(parts, step, j, 1 - me % 2)] = theirs_ref[j]
        level[pair_at(parts, step, j, me % 2)] = mine_ref[j]
    weights = [level[p, :2 * cols, :] for p in range(parts // 2)]
    blocks = {(p, p): level[p, 2 * cols:, :] for p in range(parts // 2)}
    for p in range(parts // 2):
        for q in range(p + 1, parts // 2):
            between = jnp.concatenate([
                jnp.concatenate([cross[where[a, b]:where[a, b] + cols, :] for b in (2 * q, 2 * q + 1)], axis=1)
                for a in (2 * p, 2 * p + 1)
            ], axis=0)
            blocks[p, q] = split_dot(weights[p], split_dot(between, weights[q]), ((0,), (0,)))
    count = parts // 2
    while count > 1:
        grams = []
        for p in range(0, count, 2):
            low = jnp.concatenate([blocks[p, p], blocks[p, p + 1]], axis=1)
            high = jnp.concatenate([blocks[p, p + 1].T, blocks[p + 1, p + 1]], axis=1)
            grams.append(jnp.concatenate([low, high], axis=0))
        combines = combine_of(grams)
        per = len(weights) // len(combines)
        weights = [
            split_dot(w, combines[i // per][(i % per) * cols:(i % per + 1) * cols, :])
            for i, w in enumerate(weights)
        ]
        weights = [jnp.concatenate(weights[i:i + per], axis=0) for i in range(0, len(weights), per)]
        merged = {}
        if count > 2:
            for p in range(count // 2):
                for q in range(p, count // 2):
                    if p == q:
                        between = grams[p]
                    else:
                        between = jnp.concatenate([
                            jnp.concatenate([blocks[2 * p + i, 2 * q], blocks[2 * p + i, 2 * q + 1]], axis=1)
                            for i in range(2)
                        ], axis=0)
                    right = split_dot(between, combines[q])
                    merged[p, q] = split_dot(combines[p], right, ((0,), (0,)))
        blocks, count = merged, count // 2
    weight_ref[...] = weights[0]
    width = cols // parts
    turned[...] = dot_parts((high_ref[...], low_ref[...]), split(weights[0])).T
    for k in range(parts):
        outs[k][...] = turned[pl.ds(pl.multiple_of((me ^ k) * width, 8), width), :]


def coefficient_kernel(parts, weight_ref, product_ref, coef_ref, held):
    held[...] = split_dot(weight_ref[...], product_ref[...], ((0,), (0,)))
    width = coef_ref.shape[0]
    coef_ref[...] = held[pl.ds(pl.multiple_of(lax.axis_index("tm") * width, 8), width), :]


def final_kernel(parts, *refs):
    pieces, basis_ref = refs[:parts], refs[parts]
    me = lax.axis_index("tm")
    per, cells = basis_ref.shape[0] // parts, basis_ref.shape[2]
    for k in range(parts):
        base = (me ^ k) * per
        for i in range(per):
            basis_ref[base + i] = pieces[k][:, i * cells:(i + 1) * cells]


def shape(*dims):
    return jax.ShapeDtypeStruct(dims, F32)


def local(snapshots, land_mask, taps_rows, taps_cols, probes):
    rows, grid_cols, cols = snapshots.shape
    half_rows, half_cols = rows // 2, grid_cols // 2
    parts, patches = lax.axis_size("tm"), lax.axis_size("space")
    cells = half_rows * half_cols
    piece = cells // parts
    span = 2 if patches > 1 else 1

    snapshots, land_mask, taps_rows, taps_cols = (
        pltpu.with_memory_space_constraint(x, pltpu.HBM) for x in (snapshots, land_mask, taps_rows, taps_cols)
    )

    row_block, mask_block = (2, grid_cols, cols), (CHUNK, grid_cols)
    to_near, to_far = pl.pallas_call(
        edge_kernel,
        out_shape=[shape(half_cols, cols)] * 2,
        grid=(1,),
        in_specs=[
            scalars(), scalars(),
            pl.BlockSpec(row_block, lambda i: (0, 0, 0)),
            pl.BlockSpec(row_block, lambda i: (rows // 2 - 1, 0, 0)),
            pl.BlockSpec(mask_block, lambda i: (0, 0)),
            pl.BlockSpec(mask_block, lambda i: (rows // CHUNK - 1, 0)),
        ],
        out_specs=[pl.BlockSpec((half_cols, cols), lambda i: (0, 0))] * 2,
        scratch_shapes=[pltpu.VMEM((grid_cols, CHUNK), F32)],
        compiler_params=params(),
        name="edge",
    )(taps_rows, taps_cols, snapshots, snapshots, land_mask, land_mask)
    near = lax.ppermute(to_near, "space", [(i, i ^ 1) for i in range(patches) if i ^ 1 < patches])
    pairs = [(i, i + 1) for i in range(1, patches - 1, 2)]
    other = lax.ppermute(to_far, "space", pairs + [(j, i) for i, j in pairs])

    pieces = pl.pallas_call(
        functools.partial(filter_kernel, parts),
        out_shape=[shape(piece, cols)] * parts,
        in_specs=[scalars(), scalars(), pl.BlockSpec(memory_space=pltpu.HBM), whole()],
        out_specs=[whole()] * parts,
        scratch_shapes=[
            pltpu.VMEM((rows, grid_cols, cols), F32),
            pltpu.SemaphoreType.DMA((rows // CHUNK,)),
            pltpu.VMEM((grid_cols, rows), F32),
            pltpu.VMEM((rows, 2, half_cols, cols), F32),
            pltpu.VMEM((rows + 4, half_cols, cols), F32),
            pltpu.VMEM((cells, cols), F32),
        ],
        compiler_params=params(),
        cost_estimate=pl.CostEstimate(flops=0, bytes_accessed=4 * snapshots.size, transcendentals=0),
        name="filter",
    )(taps_rows, taps_cols, snapshots, land_mask)
    kept = pl.pallas_call(
        functools.partial(halo_kernel, parts),
        out_shape=[shape(piece, cols)] * parts,
        in_specs=[whole()] * (parts + 2),
        out_specs=[whole()] * parts,
        input_output_aliases={2 + k: k for k in range(parts)},
        compiler_params=params(),
        name="halo",
    )(near, other, *pieces)
    theirs = {k: swap(kept[k + 1], "tm", 1) for k in range(0, parts, 2)}
    far = {0: kept[0], 1: theirs[0]}
    for k in range(2, parts, 2):
        far[k] = swap(kept[k], "tm", k)
        far[k + 1] = swap(theirs[k], "tm", k)

    owners = 2 * span
    pair_size = pair_rows(cols) // 2
    sums = pl.pallas_call(
        functools.partial(pair_kernel, parts, span),
        out_shape=[shape(pair_size + 2 * cols // owners, cols)] * owners,
        in_specs=[whole()] * (parts + 1),
        out_specs=[whole()] * owners,
        scratch_shapes=[
            pltpu.VMEM((cells // 2, 2 * cols), F32),
            pltpu.VMEM((cells // 2, cols), F32),
            pltpu.VMEM((pair_rows(cols), cols), F32),
            pltpu.VMEM((2 * cols, cols), F32),
        ],
        compiler_params=params(),
        cost_estimate=pl.CostEstimate(flops=0, bytes_accessed=0, transcendentals=0),
        name="pair",
    )(probes.reshape(cells, cols), *[kept[k] for k in range(0, parts, 2)], *[theirs[k] for k in range(0, parts, 2)])
    got = [swap_both(sums[j], j % 2 + parts * (j // 2)) for j in range(1, owners)]
    tied = lax.optimization_barrier(got + [far[k] for k in range(2, parts)])
    got = tied[:owners - 1]
    far.update(zip(range(2, parts), tied[owners - 1:]))
    pair_share = sums[0] + got[0]
    if span > 1:
        pair_share = pair_share + (got[1] + got[2])
    bits = [1 << b for b in range(1, patches.bit_length() - 1)]

    blocks = len(cross_order(parts))
    owners = parts * span
    size = blocks * cols // owners
    factors = jax.ShapeDtypeStruct((piece, parts * cols), jnp.bfloat16)
    send, keep, high, low = pl.pallas_call(
        functools.partial(cross_kernel, parts, span),
        out_shape=[shape(owners // 2, size, cols)] * 2 + [factors] * 2,
        in_specs=[whole()] * parts,
        out_specs=[whole()] * 4,
        scratch_shapes=[pltpu.VMEM((piece, parts * cols), F32), pltpu.VMEM((blocks * cols, cols), F32)],
        compiler_params=params(),
        cost_estimate=pl.CostEstimate(flops=0, bytes_accessed=0, transcendentals=0),
        name="cross",
    )(*[far[k] for k in range(parts)])
    got = swap(send, "tm", 1)
    mine = keep[0] + got[0]
    for h in range(1, owners // 2):
        mine = mine + swap_both(keep[h] + got[h], 2 * h)
    for bit in bits[:1]:
        pair_share = pair_share + swap(pair_share, "space", bit)
    mine, pair_share = lax.optimization_barrier((mine, pair_share))
    pair_share, product_share = pair_share[:pair_size], pair_share[pair_size:]
    for bit in bits[1:]:
        pair_share = pair_share + swap(pair_share, "space", bit)
    for bit in bits[:1]:
        mine = mine + swap(mine, "space", bit)
    mine, pair_share = lax.optimization_barrier((mine, pair_share))
    mine = jnp.concatenate([mine, product_share], axis=0)
    for bit in bits[1:]:
        mine = mine + swap(mine, "space", bit)

    def spread(x, count):
        return [x] + [swap_both(x, 2 * h) for h in range(1, count // 2)]

    def gathered(shares):
        even = jnp.stack(shares)
        return even, swap(even, "tm", 1)

    mine, *pair_shares = lax.optimization_barrier([mine] + spread(pair_share, parts))

    half = parts // 2
    level = pl.pallas_call(
        functools.partial(level_kernel, parts),
        out_shape=shape(half // 2 if half % 2 == 0 else half, 3 * cols, cols),
        in_specs=[whole()] * 2,
        out_specs=whole(),
        scratch_shapes=[pltpu.VMEM((half, pair_rows(cols), cols), F32)],
        compiler_params=params(),
        cost_estimate=pl.CostEstimate(flops=parts * SIGN_STEPS * 6 * (2 * cols) ** 3, bytes_accessed=0, transcendentals=0),
        name="level",
    )(*gathered(pair_shares))
    level, *shares = lax.optimization_barrier([level] + spread(mine, owners))
    other_level = swap(level, "tm", 1)
    width = cols // parts
    *sent, weight, products = pl.pallas_call(
        functools.partial(merge_kernel, parts, span),
        out_shape=[shape(width, piece)] * parts + [shape(parts * cols, cols)] * 2,
        in_specs=[whole()] * 6,
        out_specs=[whole()] * (parts + 2),
        scratch_shapes=[
            pltpu.VMEM((half, 3 * cols, cols), F32),
            pltpu.VMEM((blocks * cols, cols), F32),
            pltpu.VMEM((cols, piece), F32),
        ],
        compiler_params=params(),
        name="merge",
    )(*gathered(shares), level, other_level, high, low)
    coefficients = pl.pallas_call(
        functools.partial(coefficient_kernel, parts),
        out_shape=shape(width, cols),
        in_specs=[whole()] * 2,
        out_specs=whole(),
        scratch_shapes=[pltpu.VMEM((cols, cols), F32)],
        compiler_params=params(),
        name="coefficients",
    )(weight, products)
    last = [sent[0]] + [swap(sent[k], "tm", k) for k in range(1, parts)]

    basis = pl.pallas_call(
        functools.partial(final_kernel, parts),
        out_shape=shape(half_rows, width, half_cols),
        in_specs=[whole()] * parts,
        out_specs=whole(),
        compiler_params=params(),
        name="final",
    )(*last)
    return basis.transpose(0, 2, 1), coefficients


def solution(mesh):
    placed = (P("space", None, "tm"), P("space", None), P(), P(), P("space", None, None))
    return jax.shard_map(
        local,
        mesh=mesh,
        in_specs=placed,
        out_specs=(P("space", None, "tm"), P("tm", None)),
        check_vma=False,
    )
```

```python
import functools

import jax
import jax.numpy as jnp
from jax import lax
from jax.experimental import pallas as pl
from jax.experimental.pallas import tpu as pltpu
from jax.sharding import PartitionSpec as P

SIGN_STEPS = 8
TAPS = 6
CHUNK = 8
ROW_BLOCKS = 2
F32 = jnp.float32
VMEM_LIMIT = 48 * 1024 * 1024


def params():
    return pltpu.CompilerParams(vmem_limit_bytes=VMEM_LIMIT)


def whole():
    return pl.BlockSpec(memory_space=pltpu.VMEM)


def scalars():
    return pl.BlockSpec(memory_space=pltpu.SMEM)


def swap(x, axis, mask):
    count = lax.axis_size(axis)
    return lax.ppermute(x, axis, [(i, i ^ mask) for i in range(count)])


def swap_both(x, mask):
    parts, patches = lax.axis_size("tm"), lax.axis_size("space")
    route = []
    for t in range(parts):
        for s in range(patches):
            there = (t ^ (mask % parts)) * patches + (s ^ (mask // parts))
            route.append((t * patches + s, there))
    return lax.ppermute(x, ("tm", "space"), route)


def shift_rows(x, by):
    edge = jnp.zeros((1, x.shape[1]), x.dtype)
    if by > 0:
        return jnp.concatenate([edge, x[:-1]], axis=0)
    return jnp.concatenate([x[1:], edge], axis=0)


def mask_columns(mask, mask_t):
    mask_t[...] = mask.astype(F32).T
    half = mask.shape[1] // 2
    return mask_t[pl.ds(0, half, stride=2), :], mask_t[pl.ds(1, half, stride=2), :]


def narrowed_row(snaps, x, mask, taps):
    half = snaps.shape[1] // 2
    even = snaps[x, pl.ds(0, half, stride=2), :] * mask[0]
    odd = snaps[x, pl.ds(1, half, stride=2), :] * mask[1]
    before = taps[0] * even + taps[1] * odd
    here = taps[2] * even + taps[3] * odd
    after = taps[4] * even + taps[5] * odd
    return shift_rows(before, 1) + here + shift_rows(after, -1)


def edge_kernel(rtaps_ref, ctaps_ref, first_ref, last_ref, mask_first_ref, mask_last_ref, near_ref, far_ref, mask_t):
    ctaps = [ctaps_ref[k] for k in range(TAPS)]
    even = lax.axis_index("space") % 2 == 0
    shares = []
    for snaps, mask_ref, taps, at in (
        (first_ref, mask_first_ref, (rtaps_ref[4], rtaps_ref[5]), 0),
        (last_ref, mask_last_ref, (rtaps_ref[0], rtaps_ref[1]), CHUNK - 2),
    ):
        masks = mask_columns(mask_ref[...], mask_t)
        rows = [narrowed_row(snaps, x, [m[:, at + x:at + x + 1] for m in masks], ctaps) for x in range(2)]
        shares.append(taps[0] * rows[0] + taps[1] * rows[1])
    up, down = shares
    near_ref[...] = jnp.where(even, down, up)
    far_ref[...] = jnp.where(even, up, down)


def filter_kernel(parts, rtaps_ref, ctaps_ref, snap_hbm, mask_ref, *rest):
    pieces, (snaps, sems, mask_t, spread, narrowed, filtered) = rest[:parts], rest[parts:]
    rows, cells = narrowed.shape[0] - 4, narrowed.shape[1]
    me = lax.axis_index("tm")
    chunks = rows // CHUNK

    def fetch(c):
        at = pl.ds(c * CHUNK, CHUNK)
        return pltpu.make_async_copy(snap_hbm.at[at], snaps.at[at], sems.at[c])

    for c in range(chunks):
        fetch(c).start()

    rtaps = [rtaps_ref[k] for k in range(TAPS)]
    ctaps = [ctaps_ref[k] for k in range(TAPS)]
    edge = jnp.zeros((2,) + narrowed.shape[1:], F32)
    narrowed[0:2] = edge
    narrowed[rows + 2:rows + 4] = edge

    masks = mask_columns(mask_ref[...], mask_t)
    for x in range(rows):
        for j, mask in enumerate(masks):
            spread[x, j] = jnp.broadcast_to(mask[:, x:x + 1], (cells, narrowed.shape[2]))

    def narrow(c, carry):
        fetch(c).wait()
        base = pl.multiple_of(c * CHUNK, CHUNK)
        for x in range(CHUNK):
            row = narrowed_row(snaps, base + x, spread[base + x], ctaps)
            narrowed[base + 2 + x] = row
        return carry

    lax.fori_loop(0, chunks, narrow, 0)
    for i in range(rows // 2):
        total = rtaps[0] * narrowed[2 * i]
        for k in range(1, TAPS):
            total = total + rtaps[k] * narrowed[2 * i + k]
        filtered[i * cells:(i + 1) * cells, :] = total
    size = filtered.shape[0] // parts
    for k in range(parts):
        pieces[k][...] = filtered[pl.ds(pl.multiple_of((me ^ k) * size, 8), size), :]


def halo_kernel(parts, near_ref, far_ref, *refs):
    outs = refs[len(refs) // 2:]
    me = lax.axis_index("tm")
    cells = near_ref.shape[0]
    even = lax.axis_index("space") % 2 == 0
    above = jnp.where(even, far_ref[...], near_ref[...])
    below = jnp.where(even, near_ref[...], far_ref[...])
    for k, out in enumerate(outs):
        out[...] = refs[k][...]

        @pl.when((me ^ k) == 0)
        def _():
            out[:cells, :] = out[:cells, :] + above

        @pl.when((me ^ k) == parts - 1)
        def _():
            out[-cells:, :] = out[-cells:, :] + below


def cross_order(parts):
    return [(a, b) for p in range(0, parts, 2) for q in range(p + 2, parts, 2) for a in (p, p + 1) for b in (q, q + 1)]


def triangle(size):
    return tuple(lax.broadcasted_iota(jnp.int32, (size, size), axis) for axis in range(2))


def pair_rows(cols):
    return 2 * cols + 16


def pair_kernel(parts, span, probes_ref, *refs):
    half = parts // 2
    owners = 2 * span
    mine, theirs, refs = refs[:half], refs[half:2 * half], refs[2 * half:]
    outs, (wide, there, flat, products) = refs[:owners], refs[owners:]
    me, owner = positions(2, span)
    size, cols = mine[0].shape
    low = pl.ds(pl.multiple_of((me % 2) * cols, cols), cols)
    high = pl.ds(pl.multiple_of((1 - me % 2) * cols, cols), cols)
    for h in range(half):
        at = pl.ds(h * size, size)
        wide[at, low] = mine[h][...]
        wide[at, high] = theirs[h][...]
        there[at, :] = probes_ref[pl.ds(pl.multiple_of((me ^ 2 * h) * size, 8), size), :]
    left = split(wide[...])
    gram = dot_parts(left, left, ((0,), (0,)))
    first, second = gram[:cols, :cols], gram[cols:, cols:]
    row, col = triangle(cols)
    flat[:cols, :] = gram[:cols, cols:]
    flat[cols:2 * cols, :] = jnp.where(row <= col, first, second)
    products[...] = dot_parts(left, split(there[...]), ((0,), (0,)))
    diagonal = jnp.sum(jnp.where(row == col, second, 0.0), axis=0, keepdims=True)
    flat[2 * cols:, :] = jnp.broadcast_to(diagonal, (flat.shape[0] - 2 * cols, cols))
    share, rest = flat.shape[0] // 2, 2 * cols // owners
    for k, out in enumerate(outs):
        out[:share, :] = flat[pl.ds(pl.multiple_of(((owner ^ k) % 2) * share, 8), share), :]
        out[share:, :] = products[pl.ds(pl.multiple_of((owner ^ k) * rest, 8), rest), :]


def positions(count, span):
    me = lax.axis_index("tm")
    return me, me % count + count * (lax.axis_index("space") % span)


def give(owner, flat, send_ref, keep_ref):
    count = 2 * send_ref.shape[0]
    share = flat.shape[0] // count
    for k in range(count):
        out = send_ref if k % 2 else keep_ref
        out[k // 2] = flat[pl.ds(pl.multiple_of((owner ^ k) * share, 8), share), :]


def cross_kernel(parts, span, *refs):
    pieces, (send_ref, keep_ref, high_ref, low_ref, wide, flat) = refs[:parts], refs[parts:]
    me, owner = positions(parts, span)
    cols = pieces[0].shape[1]
    for k in range(parts):
        wide[:, pl.ds(pl.multiple_of((me ^ k) * cols, cols), cols)] = pieces[k][...]
    sides = [split(wide[:, a * cols:(a + 2) * cols]) for a in range(0, parts, 2)]
    for at, (high, low) in enumerate(sides):
        high_ref[:, 2 * at * cols:2 * (at + 1) * cols] = high
        low_ref[:, 2 * at * cols:2 * (at + 1) * cols] = low
    where = {ab: j for j, ab in enumerate(cross_order(parts))}
    for a in range(0, parts, 2):
        for b in range(a + 2, parts, 2):
            prod = dot_parts(sides[a // 2], sides[b // 2], ((0,), (0,)))
            for i in range(2):
                for j in range(2):
                    at = where[a + i, b + j] * cols
                    flat[at:at + cols, :] = prod[i * cols:(i + 1) * cols, j * cols:(j + 1) * cols]
    give(owner, flat, send_ref, keep_ref)


def split(x):
    high = x.astype(jnp.bfloat16)
    return high, (x - high.astype(F32)).astype(jnp.bfloat16)


def dot(a, b, dims):
    return lax.dot_general(a, b, (dims, ((), ())), preferred_element_type=F32)


def dot_parts(a, b, dims=((1,), (0,))):
    (ah, al), (bh, bl) = a, b
    left = jnp.concatenate([ah, ah, al], axis=dims[0][0])
    return dot(left, jnp.concatenate([bh, bl, bh], axis=dims[1][0]), dims)


def split_dot(a, b, dims=((1,), (0,))):
    return dot_parts(split(a), split(b), dims)


def next_sign(y):
    whole_y = split(y)
    size = y.shape[0] // ROW_BLOCKS
    blocks = []
    for at in range(0, y.shape[0], size):
        square = dot_parts([part[at:at + size] for part in whole_y], whole_y)
        blocks.append(1.5 * y[at:at + size] - 0.5 * dot_parts(split(square), whole_y))
    return jnp.concatenate(blocks, axis=0)


def combine_of(grams):
    order = grams[0].shape[0]
    diagonal = lax.broadcasted_iota(jnp.int32, (order, order), 0) == lax.broadcasted_iota(jnp.int32, (order, order), 1)
    signs = []
    for gram in grams:
        mean = jnp.sum(jnp.where(diagonal, gram, 0.0)) / order
        shifted = jnp.where(diagonal, gram - mean, gram)
        signs.append(shifted / jnp.sqrt(jnp.sum(shifted * shifted, keepdims=True) + 1e-6))
    for _ in range(SIGN_STEPS):
        signs = [next_sign(y) for y in signs]
    half = order // 2
    combines = []
    for y in signs:
        projector = 0.5 * (jnp.where(diagonal, 1.0, 0.0) + y)
        combines.append(projector[:, :half] + projector[:, half:])
    return combines


def place_shares(parts, span, even_ref, odd_ref, put):
    _, owner = positions(parts, span)
    for k in range(parts * span):
        put(owner ^ k, (odd_ref if k % 2 else even_ref)[k // 2])


def pair_at(parts, step, j, core):
    return j if step == parts // 2 else 2 * j + core


def level_kernel(parts, even_ref, odd_ref, out_ref, pairs):
    cols = even_ref.shape[2]
    share = pairs.shape[1] // 2

    def put(there, rows):
        pairs[there // 2, pl.ds(pl.multiple_of((there % 2) * share, 8), share), :] = rows

    place_shares(parts, 1, even_ref, odd_ref, put)
    row, col = triangle(cols)
    grams = []
    step = out_ref.shape[0]
    for j in range(step):
        p = pair_at(parts, step, j, lax.axis_index("tm") % 2)
        packed = pairs[p, cols:2 * cols, :]
        turned_back = packed.T
        first = jnp.where(row <= col, packed, turned_back)
        between = pairs[p, :cols, :]
        second = jnp.where(row > col, packed, turned_back)
        second = jnp.where(row == col, pairs[p, 2 * cols:2 * cols + 1, :], second)
        grams.append(jnp.concatenate([
            jnp.concatenate([first, between], axis=1), jnp.concatenate([between.T, second], axis=1)
        ], axis=0))
    for j, (gram, combine) in enumerate(zip(grams, combine_of(grams))):
        out_ref[j, :2 * cols, :] = combine
        out_ref[j, 2 * cols:, :] = split_dot(combine, split_dot(gram, combine), ((0,), (0,)))


def merge_kernel(parts, span, even_ref, odd_ref, mine_ref, theirs_ref, high_ref, low_ref, *refs):
    outs, (weight_ref, product_ref, level, cross, turned) = refs[:parts], refs[parts:]
    me = lax.axis_index("tm")
    cols = even_ref.shape[2]
    share = cross.shape[0] // (parts * span)

    rest = 2 * cols // (2 * span)

    def put(there, rows):
        cross[pl.ds(pl.multiple_of(there * share, 8), share), :] = rows[:share]
        at = ((there % parts) // 2) * 2 * cols + (there % 2 + 2 * (there // parts)) * rest
        product_ref[pl.ds(pl.multiple_of(at, 8), rest), :] = rows[share:]

    place_shares(parts, span, even_ref, odd_ref, put)
    where = {ab: j * cols for j, ab in enumerate(cross_order(parts))}
    step = mine_ref.shape[0]
    for j in range(step):
        level[pair_at(parts, step, j, 1 - me % 2)] = theirs_ref[j]
        level[pair_at(parts, step, j, me % 2)] = mine_ref[j]
    weights = [level[p, :2 * cols, :] for p in range(parts // 2)]
    blocks = {(p, p): level[p, 2 * cols:, :] for p in range(parts // 2)}
    for p in range(parts // 2):
        for q in range(p + 1, parts // 2):
            between = jnp.concatenate([
                jnp.concatenate([cross[where[a, b]:where[a, b] + cols, :] for b in (2 * q, 2 * q + 1)], axis=1)
                for a in (2 * p, 2 * p + 1)
            ], axis=0)
            blocks[p, q] = split_dot(weights[p], split_dot(between, weights[q]), ((0,), (0,)))
    count = parts // 2
    while count > 1:
        grams = []
        for p in range(0, count, 2):
            low = jnp.concatenate([blocks[p, p], blocks[p, p + 1]], axis=1)
            high = jnp.concatenate([blocks[p, p + 1].T, blocks[p + 1, p + 1]], axis=1)
            grams.append(jnp.concatenate([low, high], axis=0))
        combines = combine_of(grams)
        per = len(weights) // len(combines)
        weights = [
            split_dot(w, combines[i // per][(i % per) * cols:(i % per + 1) * cols, :])
            for i, w in enumerate(weights)
        ]
        weights = [jnp.concatenate(weights[i:i + per], axis=0) for i in range(0, len(weights), per)]
        merged = {}
        if count > 2:
            for p in range(count // 2):
                for q in range(p, count // 2):
                    if p == q:
                        between = grams[p]
                    else:
                        between = jnp.concatenate([
                            jnp.concatenate([blocks[2 * p + i, 2 * q], blocks[2 * p + i, 2 * q + 1]], axis=1)
                            for i in range(2)
                        ], axis=0)
                    right = split_dot(between, combines[q])
                    merged[p, q] = split_dot(combines[p], right, ((0,), (0,)))
        blocks, count = merged, count // 2
    weight_ref[...] = weights[0]
    width = cols // parts
    turned[...] = dot_parts((high_ref[...], low_ref[...]), split(weights[0])).T
    for k in range(parts):
        outs[k][...] = turned[pl.ds(pl.multiple_of((me ^ k) * width, 8), width), :]


def coefficient_kernel(parts, weight_ref, product_ref, coef_ref, held):
    held[...] = split_dot(weight_ref[...], product_ref[...], ((0,), (0,)))
    width = coef_ref.shape[0]
    coef_ref[...] = held[pl.ds(pl.multiple_of(lax.axis_index("tm") * width, 8), width), :]


def final_kernel(parts, *refs):
    pieces, basis_ref = refs[:parts], refs[parts]
    me = lax.axis_index("tm")
    per, cells = basis_ref.shape[0] // parts, basis_ref.shape[2]
    for k in range(parts):
        base = (me ^ k) * per
        for i in range(per):
            basis_ref[base + i] = pieces[k][:, i * cells:(i + 1) * cells]


def shape(*dims):
    return jax.ShapeDtypeStruct(dims, F32)


def local(snapshots, land_mask, taps_rows, taps_cols, probes):
    rows, grid_cols, cols = snapshots.shape
    half_rows, half_cols = rows // 2, grid_cols // 2
    parts, patches = lax.axis_size("tm"), lax.axis_size("space")
    cells = half_rows * half_cols
    piece = cells // parts
    span = 2 if patches > 1 else 1

    snapshots, land_mask, taps_rows, taps_cols = (
        pltpu.with_memory_space_constraint(x, pltpu.HBM) for x in (snapshots, land_mask, taps_rows, taps_cols)
    )

    row_block, mask_block = (2, grid_cols, cols), (CHUNK, grid_cols)
    to_near, to_far = pl.pallas_call(
        edge_kernel,
        out_shape=[shape(half_cols, cols)] * 2,
        grid=(1,),
        in_specs=[
            scalars(), scalars(),
            pl.BlockSpec(row_block, lambda i: (0, 0, 0)),
            pl.BlockSpec(row_block, lambda i: (rows // 2 - 1, 0, 0)),
            pl.BlockSpec(mask_block, lambda i: (0, 0)),
            pl.BlockSpec(mask_block, lambda i: (rows // CHUNK - 1, 0)),
        ],
        out_specs=[pl.BlockSpec((half_cols, cols), lambda i: (0, 0))] * 2,
        scratch_shapes=[pltpu.VMEM((grid_cols, CHUNK), F32)],
        compiler_params=params(),
        name="edge",
    )(taps_rows, taps_cols, snapshots, snapshots, land_mask, land_mask)
    near = lax.ppermute(to_near, "space", [(i, i ^ 1) for i in range(patches) if i ^ 1 < patches])
    pairs = [(i, i + 1) for i in range(1, patches - 1, 2)]
    other = lax.ppermute(to_far, "space", pairs + [(j, i) for i, j in pairs])

    pieces = pl.pallas_call(
        functools.partial(filter_kernel, parts),
        out_shape=[shape(piece, cols)] * parts,
        in_specs=[scalars(), scalars(), pl.BlockSpec(memory_space=pltpu.HBM), whole()],
        out_specs=[whole()] * parts,
        scratch_shapes=[
            pltpu.VMEM((rows, grid_cols, cols), F32),
            pltpu.SemaphoreType.DMA((rows // CHUNK,)),
            pltpu.VMEM((grid_cols, rows), F32),
            pltpu.VMEM((rows, 2, half_cols, cols), F32),
            pltpu.VMEM((rows + 4, half_cols, cols), F32),
            pltpu.VMEM((cells, cols), F32),
        ],
        compiler_params=params(),
        cost_estimate=pl.CostEstimate(flops=0, bytes_accessed=4 * snapshots.size, transcendentals=0),
        name="filter",
    )(taps_rows, taps_cols, snapshots, land_mask)
    kept = pl.pallas_call(
        functools.partial(halo_kernel, parts),
        out_shape=[shape(piece, cols)] * parts,
        in_specs=[whole()] * (parts + 2),
        out_specs=[whole()] * parts,
        input_output_aliases={2 + k: k for k in range(parts)},
        compiler_params=params(),
        name="halo",
    )(near, other, *pieces)
    theirs = {k: swap(kept[k + 1], "tm", 1) for k in range(0, parts, 2)}
    far = {0: kept[0], 1: theirs[0]}
    for k in range(2, parts, 2):
        far[k] = swap(kept[k], "tm", k)
        far[k + 1] = swap(theirs[k], "tm", k)

    owners = 2 * span
    pair_size = pair_rows(cols) // 2
    sums = pl.pallas_call(
        functools.partial(pair_kernel, parts, span),
        out_shape=[shape(pair_size + 2 * cols // owners, cols)] * owners,
        in_specs=[whole()] * (parts + 1),
        out_specs=[whole()] * owners,
        scratch_shapes=[
            pltpu.VMEM((cells // 2, 2 * cols), F32),
            pltpu.VMEM((cells // 2, cols), F32),
            pltpu.VMEM((pair_rows(cols), cols), F32),
            pltpu.VMEM((2 * cols, cols), F32),
        ],
        compiler_params=params(),
        cost_estimate=pl.CostEstimate(flops=0, bytes_accessed=0, transcendentals=0),
        name="pair",
    )(probes.reshape(cells, cols), *[kept[k] for k in range(0, parts, 2)], *[theirs[k] for k in range(0, parts, 2)])
    got = [swap_both(sums[j], j % 2 + parts * (j // 2)) for j in range(1, owners)]
    tied = lax.optimization_barrier(got + [far[k] for k in range(2, parts)])
    got = tied[:owners - 1]
    far.update(zip(range(2, parts), tied[owners - 1:]))
    pair_share = sums[0] + got[0]
    if span > 1:
        pair_share = pair_share + (got[1] + got[2])
    bits = [1 << b for b in range(1, patches.bit_length() - 1)]

    blocks = len(cross_order(parts))
    owners = parts * span
    size = blocks * cols // owners
    factors = jax.ShapeDtypeStruct((piece, parts * cols), jnp.bfloat16)
    send, keep, high, low = pl.pallas_call(
        functools.partial(cross_kernel, parts, span),
        out_shape=[shape(owners // 2, size, cols)] * 2 + [factors] * 2,
        in_specs=[whole()] * parts,
        out_specs=[whole()] * 4,
        scratch_shapes=[pltpu.VMEM((piece, parts * cols), F32), pltpu.VMEM((blocks * cols, cols), F32)],
        compiler_params=params(),
        cost_estimate=pl.CostEstimate(flops=0, bytes_accessed=0, transcendentals=0),
        name="cross",
    )(*[far[k] for k in range(parts)])
    got = swap(send, "tm", 1)
    mine = keep[0] + got[0]
    for h in range(1, owners // 2):
        mine = mine + swap_both(keep[h] + got[h], 2 * h)
    for bit in bits[:1]:
        pair_share = pair_share + swap(pair_share, "space", bit)
    pair_share, product_share = pair_share[:pair_size], pair_share[pair_size:]
    for bit in bits[1:]:
        pair_share = pair_share + swap(pair_share, "space", bit)
    mine, pair_share = lax.optimization_barrier((mine, pair_share))
    for bit in bits[:1]:
        mine = mine + swap(mine, "space", bit)
    mine, pair_share = lax.optimization_barrier((mine, pair_share))
    mine = jnp.concatenate([mine, product_share], axis=0)
    for bit in bits[1:]:
        mine = mine + swap(mine, "space", bit)

    def spread(x, count):
        return [x] + [swap_both(x, 2 * h) for h in range(1, count // 2)]

    def gathered(shares):
        even = jnp.stack(shares)
        return even, swap(even, "tm", 1)

    mine, *pair_shares = lax.optimization_barrier([mine] + spread(pair_share, parts))

    half = parts // 2
    level = pl.pallas_call(
        functools.partial(level_kernel, parts),
        out_shape=shape(half // 2 if half % 2 == 0 else half, 3 * cols, cols),
        in_specs=[whole()] * 2,
        out_specs=whole(),
        scratch_shapes=[pltpu.VMEM((half, pair_rows(cols), cols), F32)],
        compiler_params=params(),
        cost_estimate=pl.CostEstimate(flops=parts * SIGN_STEPS * 6 * (2 * cols) ** 3, bytes_accessed=0, transcendentals=0),
        name="level",
    )(*gathered(pair_shares))
    level, *shares = lax.optimization_barrier([level] + spread(mine, owners))
    other_level = swap(level, "tm", 1)
    width = cols // parts
    *sent, weight, products = pl.pallas_call(
        functools.partial(merge_kernel, parts, span),
        out_shape=[shape(width, piece)] * parts + [shape(parts * cols, cols)] * 2,
        in_specs=[whole()] * 6,
        out_specs=[whole()] * (parts + 2),
        scratch_shapes=[
            pltpu.VMEM((half, 3 * cols, cols), F32),
            pltpu.VMEM((blocks * cols, cols), F32),
            pltpu.VMEM((cols, piece), F32),
        ],
        compiler_params=params(),
        name="merge",
    )(*gathered(shares), level, other_level, high, low)
    coefficients = pl.pallas_call(
        functools.partial(coefficient_kernel, parts),
        out_shape=shape(width, cols),
        in_specs=[whole()] * 2,
        out_specs=whole(),
        scratch_shapes=[pltpu.VMEM((cols, cols), F32)],
        compiler_params=params(),
        name="coefficients",
    )(weight, products)
    last = [sent[0]] + [swap(sent[k], "tm", k) for k in range(1, parts)]

    basis = pl.pallas_call(
        functools.partial(final_kernel, parts),
        out_shape=shape(half_rows, width, half_cols),
        in_specs=[whole()] * parts,
        out_specs=whole(),
        compiler_params=params(),
        name="final",
    )(*last)
    return basis.transpose(0, 2, 1), coefficients


def solution(mesh):
    placed = (P("space", None, "tm"), P("space", None), P(), P(), P("space", None, None))
    return jax.shard_map(
        local,
        mesh=mesh,
        in_specs=placed,
        out_specs=(P("space", None, "tm"), P("tm", None)),
        check_vma=False,
    )
```

```python
import functools

import jax
import jax.numpy as jnp
from jax import lax
from jax.experimental import pallas as pl
from jax.experimental.pallas import tpu as pltpu
from jax.sharding import PartitionSpec as P

SIGN_STEPS = 8
TAPS = 6
CHUNK = 16
ROW_BLOCKS = 2
F32 = jnp.float32
VMEM_LIMIT = 48 * 1024 * 1024


def params():
    return pltpu.CompilerParams(vmem_limit_bytes=VMEM_LIMIT)


def whole():
    return pl.BlockSpec(memory_space=pltpu.VMEM)


def scalars():
    return pl.BlockSpec(memory_space=pltpu.SMEM)


def swap(x, axis, mask):
    count = lax.axis_size(axis)
    return lax.ppermute(x, axis, [(i, i ^ mask) for i in range(count)])


def swap_both(x, mask):
    parts, patches = lax.axis_size("tm"), lax.axis_size("space")
    route = []
    for t in range(parts):
        for s in range(patches):
            there = (t ^ (mask % parts)) * patches + (s ^ (mask // parts))
            route.append((t * patches + s, there))
    return lax.ppermute(x, ("tm", "space"), route)


def shift_rows(x, by):
    edge = jnp.zeros((1, x.shape[1]), x.dtype)
    if by > 0:
        return jnp.concatenate([edge, x[:-1]], axis=0)
    return jnp.concatenate([x[1:], edge], axis=0)


def mask_columns(mask, mask_t):
    mask_t[...] = mask.astype(F32).T
    half = mask.shape[1] // 2
    return mask_t[pl.ds(0, half, stride=2), :], mask_t[pl.ds(1, half, stride=2), :]


def narrowed_row(snaps, x, mask, taps):
    half = snaps.shape[1] // 2
    even = snaps[x, pl.ds(0, half, stride=2), :] * mask[0]
    odd = snaps[x, pl.ds(1, half, stride=2), :] * mask[1]
    before = taps[0] * even + taps[1] * odd
    here = taps[2] * even + taps[3] * odd
    after = taps[4] * even + taps[5] * odd
    return shift_rows(before, 1) + here + shift_rows(after, -1)


def edge_kernel(rtaps_ref, ctaps_ref, first_ref, last_ref, mask_first_ref, mask_last_ref, near_ref, far_ref, mask_t):
    ctaps = [ctaps_ref[k] for k in range(TAPS)]
    even = lax.axis_index("space") % 2 == 0
    shares = []
    for snaps, mask_ref, taps, at in (
        (first_ref, mask_first_ref, (rtaps_ref[4], rtaps_ref[5]), 0),
        (last_ref, mask_last_ref, (rtaps_ref[0], rtaps_ref[1]), CHUNK - 2),
    ):
        masks = mask_columns(mask_ref[...], mask_t)
        rows = [narrowed_row(snaps, x, [m[:, at + x:at + x + 1] for m in masks], ctaps) for x in range(2)]
        shares.append(taps[0] * rows[0] + taps[1] * rows[1])
    up, down = shares
    near_ref[...] = jnp.where(even, down, up)
    far_ref[...] = jnp.where(even, up, down)


def filter_kernel(parts, rtaps_ref, ctaps_ref, snap_hbm, mask_ref, *rest):
    pieces, (snaps, sems, mask_t, spread, narrowed, filtered) = rest[:parts], rest[parts:]
    rows, cells = narrowed.shape[0] - 4, narrowed.shape[1]
    me = lax.axis_index("tm")
    chunks = rows // CHUNK

    def fetch(c):
        at = pl.ds(c * CHUNK, CHUNK)
        return pltpu.make_async_copy(snap_hbm.at[at], snaps.at[at], sems.at[c])

    for c in range(chunks):
        fetch(c).start()

    rtaps = [rtaps_ref[k] for k in range(TAPS)]
    ctaps = [ctaps_ref[k] for k in range(TAPS)]
    edge = jnp.zeros((2,) + narrowed.shape[1:], F32)
    narrowed[0:2] = edge
    narrowed[rows + 2:rows + 4] = edge

    masks = mask_columns(mask_ref[...], mask_t)
    for x in range(rows):
        for j, mask in enumerate(masks):
            spread[x, j] = jnp.broadcast_to(mask[:, x:x + 1], (cells, narrowed.shape[2]))

    def narrow(c, carry):
        fetch(c).wait()
        base = pl.multiple_of(c * CHUNK, CHUNK)
        for x in range(CHUNK):
            row = narrowed_row(snaps, base + x, spread[base + x], ctaps)
            narrowed[base + 2 + x] = row
        return carry

    lax.fori_loop(0, chunks, narrow, 0)
    for i in range(rows // 2):
        total = rtaps[0] * narrowed[2 * i]
        for k in range(1, TAPS):
            total = total + rtaps[k] * narrowed[2 * i + k]
        filtered[i * cells:(i + 1) * cells, :] = total
    size = filtered.shape[0] // parts
    for k in range(parts):
        pieces[k][...] = filtered[pl.ds(pl.multiple_of((me ^ k) * size, 8), size), :]


def halo_kernel(parts, near_ref, far_ref, *refs):
    outs = refs[len(refs) // 2:]
    me = lax.axis_index("tm")
    cells = near_ref.shape[0]
    even = lax.axis_index("space") % 2 == 0
    above = jnp.where(even, far_ref[...], near_ref[...])
    below = jnp.where(even, near_ref[...], far_ref[...])
    for k, out in enumerate(outs):
        out[...] = refs[k][...]

        @pl.when((me ^ k) == 0)
        def _():
            out[:cells, :] = out[:cells, :] + above

        @pl.when((me ^ k) == parts - 1)
        def _():
            out[-cells:, :] = out[-cells:, :] + below


def cross_order(parts):
    return [(a, b) for p in range(0, parts, 2) for q in range(p + 2, parts, 2) for a in (p, p + 1) for b in (q, q + 1)]


def triangle(size):
    return tuple(lax.broadcasted_iota(jnp.int32, (size, size), axis) for axis in range(2))


def pair_rows(cols):
    return 2 * cols + 16


def pair_kernel(parts, span, probes_ref, *refs):
    half = parts // 2
    owners = 2 * span
    mine, theirs, refs = refs[:half], refs[half:2 * half], refs[2 * half:]
    outs, (wide, there, flat, products) = refs[:owners], refs[owners:]
    me, owner = positions(2, span)
    size, cols = mine[0].shape
    low = pl.ds(pl.multiple_of((me % 2) * cols, cols), cols)
    high = pl.ds(pl.multiple_of((1 - me % 2) * cols, cols), cols)
    for h in range(half):
        at = pl.ds(h * size, size)
        wide[at, low] = mine[h][...]
        wide[at, high] = theirs[h][...]
        there[at, :] = probes_ref[pl.ds(pl.multiple_of((me ^ 2 * h) * size, 8), size), :]
    left = split(wide[...])
    gram = dot_parts(left, left, ((0,), (0,)))
    first, second = gram[:cols, :cols], gram[cols:, cols:]
    row, col = triangle(cols)
    flat[:cols, :] = gram[:cols, cols:]
    flat[cols:2 * cols, :] = jnp.where(row <= col, first, second)
    products[...] = dot_parts(left, split(there[...]), ((0,), (0,)))
    diagonal = jnp.sum(jnp.where(row == col, second, 0.0), axis=0, keepdims=True)
    flat[2 * cols:, :] = jnp.broadcast_to(diagonal, (flat.shape[0] - 2 * cols, cols))
    share, rest = flat.shape[0] // 2, 2 * cols // owners
    for k, out in enumerate(outs):
        out[:share, :] = flat[pl.ds(pl.multiple_of(((owner ^ k) % 2) * share, 8), share), :]
        out[share:, :] = products[pl.ds(pl.multiple_of((owner ^ k) * rest, 8), rest), :]


def positions(count, span):
    me = lax.axis_index("tm")
    return me, me % count + count * (lax.axis_index("space") % span)


def give(owner, flat, send_ref, keep_ref):
    count = 2 * send_ref.shape[0]
    share = flat.shape[0] // count
    for k in range(count):
        out = send_ref if k % 2 else keep_ref
        out[k // 2] = flat[pl.ds(pl.multiple_of((owner ^ k) * share, 8), share), :]


def cross_kernel(parts, span, *refs):
    pieces, (send_ref, keep_ref, high_ref, low_ref, wide, flat) = refs[:parts], refs[parts:]
    me, owner = positions(parts, span)
    cols = pieces[0].shape[1]
    for k in range(parts):
        wide[:, pl.ds(pl.multiple_of((me ^ k) * cols, cols), cols)] = pieces[k][...]
    sides = [split(wide[:, a * cols:(a + 2) * cols]) for a in range(0, parts, 2)]
    for at, (high, low) in enumerate(sides):
        high_ref[:, 2 * at * cols:2 * (at + 1) * cols] = high
        low_ref[:, 2 * at * cols:2 * (at + 1) * cols] = low
    where = {ab: j for j, ab in enumerate(cross_order(parts))}
    for a in range(0, parts, 2):
        for b in range(a + 2, parts, 2):
            prod = dot_parts(sides[a // 2], sides[b // 2], ((0,), (0,)))
            for i in range(2):
                for j in range(2):
                    at = where[a + i, b + j] * cols
                    flat[at:at + cols, :] = prod[i * cols:(i + 1) * cols, j * cols:(j + 1) * cols]
    give(owner, flat, send_ref, keep_ref)


def split(x):
    high = x.astype(jnp.bfloat16)
    return high, (x - high.astype(F32)).astype(jnp.bfloat16)


def dot(a, b, dims):
    return lax.dot_general(a, b, (dims, ((), ())), preferred_element_type=F32)


def dot_parts(a, b, dims=((1,), (0,))):
    (ah, al), (bh, bl) = a, b
    left = jnp.concatenate([ah, ah, al], axis=dims[0][0])
    return dot(left, jnp.concatenate([bh, bl, bh], axis=dims[1][0]), dims)


def split_dot(a, b, dims=((1,), (0,))):
    return dot_parts(split(a), split(b), dims)


def next_sign(y):
    whole_y = split(y)
    size = y.shape[0] // ROW_BLOCKS
    blocks = []
    for at in range(0, y.shape[0], size):
        square = dot_parts([part[at:at + size] for part in whole_y], whole_y)
        blocks.append(1.5 * y[at:at + size] - 0.5 * dot_parts(split(square), whole_y))
    return jnp.concatenate(blocks, axis=0)


def combine_of(grams):
    order = grams[0].shape[0]
    diagonal = lax.broadcasted_iota(jnp.int32, (order, order), 0) == lax.broadcasted_iota(jnp.int32, (order, order), 1)
    signs = []
    for gram in grams:
        mean = jnp.sum(jnp.where(diagonal, gram, 0.0)) / order
        shifted = jnp.where(diagonal, gram - mean, gram)
        signs.append(shifted / jnp.sqrt(jnp.sum(shifted * shifted, keepdims=True) + 1e-6))
    for _ in range(SIGN_STEPS):
        signs = [next_sign(y) for y in signs]
    half = order // 2
    combines = []
    for y in signs:
        projector = 0.5 * (jnp.where(diagonal, 1.0, 0.0) + y)
        combines.append(projector[:, :half] + projector[:, half:])
    return combines


def place_shares(parts, span, even_ref, odd_ref, put):
    _, owner = positions(parts, span)
    for k in range(parts * span):
        put(owner ^ k, (odd_ref if k % 2 else even_ref)[k // 2])


def pair_at(parts, step, j, core):
    return j if step == parts // 2 else 2 * j + core


def level_kernel(parts, even_ref, odd_ref, out_ref, pairs):
    cols = even_ref.shape[2]
    share = pairs.shape[1] // 2

    def put(there, rows):
        pairs[there // 2, pl.ds(pl.multiple_of((there % 2) * share, 8), share), :] = rows

    place_shares(parts, 1, even_ref, odd_ref, put)
    row, col = triangle(cols)
    grams = []
    step = out_ref.shape[0]
    for j in range(step):
        p = pair_at(parts, step, j, lax.axis_index("tm") % 2)
        packed = pairs[p, cols:2 * cols, :]
        turned_back = packed.T
        first = jnp.where(row <= col, packed, turned_back)
        between = pairs[p, :cols, :]
        second = jnp.where(row > col, packed, turned_back)
        second = jnp.where(row == col, pairs[p, 2 * cols:2 * cols + 1, :], second)
        grams.append(jnp.concatenate([
            jnp.concatenate([first, between], axis=1), jnp.concatenate([between.T, second], axis=1)
        ], axis=0))
    for j, (gram, combine) in enumerate(zip(grams, combine_of(grams))):
        out_ref[j, :2 * cols, :] = combine
        out_ref[j, 2 * cols:, :] = split_dot(combine, split_dot(gram, combine), ((0,), (0,)))


def merge_kernel(parts, span, even_ref, odd_ref, mine_ref, theirs_ref, high_ref, low_ref, *refs):
    outs, (weight_ref, product_ref, level, cross, turned) = refs[:parts], refs[parts:]
    me = lax.axis_index("tm")
    cols = even_ref.shape[2]
    share = cross.shape[0] // (parts * span)

    rest = 2 * cols // (2 * span)

    def put(there, rows):
        cross[pl.ds(pl.multiple_of(there * share, 8), share), :] = rows[:share]
        at = ((there % parts) // 2) * 2 * cols + (there % 2 + 2 * (there // parts)) * rest
        product_ref[pl.ds(pl.multiple_of(at, 8), rest), :] = rows[share:]

    place_shares(parts, span, even_ref, odd_ref, put)
    where = {ab: j * cols for j, ab in enumerate(cross_order(parts))}
    step = mine_ref.shape[0]
    for j in range(step):
        level[pair_at(parts, step, j, 1 - me % 2)] = theirs_ref[j]
        level[pair_at(parts, step, j, me % 2)] = mine_ref[j]
    weights = [level[p, :2 * cols, :] for p in range(parts // 2)]
    blocks = {(p, p): level[p, 2 * cols:, :] for p in range(parts // 2)}
    for p in range(parts // 2):
        for q in range(p + 1, parts // 2):
            between = jnp.concatenate([
                jnp.concatenate([cross[where[a, b]:where[a, b] + cols, :] for b in (2 * q, 2 * q + 1)], axis=1)
                for a in (2 * p, 2 * p + 1)
            ], axis=0)
            blocks[p, q] = split_dot(weights[p], split_dot(between, weights[q]), ((0,), (0,)))
    count = parts // 2
    while count > 1:
        grams = []
        for p in range(0, count, 2):
            low = jnp.concatenate([blocks[p, p], blocks[p, p + 1]], axis=1)
            high = jnp.concatenate([blocks[p, p + 1].T, blocks[p + 1, p + 1]], axis=1)
            grams.append(jnp.concatenate([low, high], axis=0))
        combines = combine_of(grams)
        per = len(weights) // len(combines)
        weights = [
            split_dot(w, combines[i // per][(i % per) * cols:(i % per + 1) * cols, :])
            for i, w in enumerate(weights)
        ]
        weights = [jnp.concatenate(weights[i:i + per], axis=0) for i in range(0, len(weights), per)]
        merged = {}
        if count > 2:
            for p in range(count // 2):
                for q in range(p, count // 2):
                    if p == q:
                        between = grams[p]
                    else:
                        between = jnp.concatenate([
                            jnp.concatenate([blocks[2 * p + i, 2 * q], blocks[2 * p + i, 2 * q + 1]], axis=1)
                            for i in range(2)
                        ], axis=0)
                    right = split_dot(between, combines[q])
                    merged[p, q] = split_dot(combines[p], right, ((0,), (0,)))
        blocks, count = merged, count // 2
    weight_ref[...] = weights[0]
    width = cols // parts
    turned[...] = dot_parts((high_ref[...], low_ref[...]), split(weights[0])).T
    for k in range(parts):
        outs[k][...] = turned[pl.ds(pl.multiple_of((me ^ k) * width, 8), width), :]


def coefficient_kernel(parts, weight_ref, product_ref, coef_ref, held):
    held[...] = split_dot(weight_ref[...], product_ref[...], ((0,), (0,)))
    width = coef_ref.shape[0]
    coef_ref[...] = held[pl.ds(pl.multiple_of(lax.axis_index("tm") * width, 8), width), :]


def final_kernel(parts, *refs):
    pieces, basis_ref = refs[:parts], refs[parts]
    me = lax.axis_index("tm")
    per, cells = basis_ref.shape[0] // parts, basis_ref.shape[2]
    for k in range(parts):
        base = (me ^ k) * per
        for i in range(per):
            basis_ref[base + i] = pieces[k][:, i * cells:(i + 1) * cells]


def shape(*dims):
    return jax.ShapeDtypeStruct(dims, F32)


def local(snapshots, land_mask, taps_rows, taps_cols, probes):
    rows, grid_cols, cols = snapshots.shape
    half_rows, half_cols = rows // 2, grid_cols // 2
    parts, patches = lax.axis_size("tm"), lax.axis_size("space")
    cells = half_rows * half_cols
    piece = cells // parts
    span = 2 if patches > 1 else 1

    snapshots, land_mask, taps_rows, taps_cols = (
        pltpu.with_memory_space_constraint(x, pltpu.HBM) for x in (snapshots, land_mask, taps_rows, taps_cols)
    )

    row_block, mask_block = (2, grid_cols, cols), (CHUNK, grid_cols)
    to_near, to_far = pl.pallas_call(
        edge_kernel,
        out_shape=[shape(half_cols, cols)] * 2,
        grid=(1,),
        in_specs=[
            scalars(), scalars(),
            pl.BlockSpec(row_block, lambda i: (0, 0, 0)),
            pl.BlockSpec(row_block, lambda i: (rows // 2 - 1, 0, 0)),
            pl.BlockSpec(mask_block, lambda i: (0, 0)),
            pl.BlockSpec(mask_block, lambda i: (rows // CHUNK - 1, 0)),
        ],
        out_specs=[pl.BlockSpec((half_cols, cols), lambda i: (0, 0))] * 2,
        scratch_shapes=[pltpu.VMEM((grid_cols, CHUNK), F32)],
        compiler_params=params(),
        name="edge",
    )(taps_rows, taps_cols, snapshots, snapshots, land_mask, land_mask)
    near = lax.ppermute(to_near, "space", [(i, i ^ 1) for i in range(patches) if i ^ 1 < patches])
    pairs = [(i, i + 1) for i in range(1, patches - 1, 2)]
    other = lax.ppermute(to_far, "space", pairs + [(j, i) for i, j in pairs])

    pieces = pl.pallas_call(
        functools.partial(filter_kernel, parts),
        out_shape=[shape(piece, cols)] * parts,
        in_specs=[scalars(), scalars(), pl.BlockSpec(memory_space=pltpu.HBM), whole()],
        out_specs=[whole()] * parts,
        scratch_shapes=[
            pltpu.VMEM((rows, grid_cols, cols), F32),
            pltpu.SemaphoreType.DMA((rows // CHUNK,)),
            pltpu.VMEM((grid_cols, rows), F32),
            pltpu.VMEM((rows, 2, half_cols, cols), F32),
            pltpu.VMEM((rows + 4, half_cols, cols), F32),
            pltpu.VMEM((cells, cols), F32),
        ],
        compiler_params=params(),
        cost_estimate=pl.CostEstimate(flops=0, bytes_accessed=4 * snapshots.size, transcendentals=0),
        name="filter",
    )(taps_rows, taps_cols, snapshots, land_mask)
    kept = pl.pallas_call(
        functools.partial(halo_kernel, parts),
        out_shape=[shape(piece, cols)] * parts,
        in_specs=[whole()] * (parts + 2),
        out_specs=[whole()] * parts,
        input_output_aliases={2 + k: k for k in range(parts)},
        compiler_params=params(),
        name="halo",
    )(near, other, *pieces)
    theirs = {k: swap(kept[k + 1], "tm", 1) for k in range(0, parts, 2)}
    far = {0: kept[0], 1: theirs[0]}
    for k in range(2, parts, 2):
        far[k] = swap(kept[k], "tm", k)
        far[k + 1] = swap(theirs[k], "tm", k)

    owners = 2 * span
    pair_size = pair_rows(cols) // 2
    sums = pl.pallas_call(
        functools.partial(pair_kernel, parts, span),
        out_shape=[shape(pair_size + 2 * cols // owners, cols)] * owners,
        in_specs=[whole()] * (parts + 1),
        out_specs=[whole()] * owners,
        scratch_shapes=[
            pltpu.VMEM((cells // 2, 2 * cols), F32),
            pltpu.VMEM((cells // 2, cols), F32),
            pltpu.VMEM((pair_rows(cols), cols), F32),
            pltpu.VMEM((2 * cols, cols), F32),
        ],
        compiler_params=params(),
        cost_estimate=pl.CostEstimate(flops=0, bytes_accessed=0, transcendentals=0),
        name="pair",
    )(probes.reshape(cells, cols), *[kept[k] for k in range(0, parts, 2)], *[theirs[k] for k in range(0, parts, 2)])
    got = [swap_both(sums[j], j % 2 + parts * (j // 2)) for j in range(1, owners)]
    tied = lax.optimization_barrier(got + [far[k] for k in range(2, parts)])
    got = tied[:owners - 1]
    far.update(zip(range(2, parts), tied[owners - 1:]))
    pair_share = sums[0] + got[0]
    if span > 1:
        pair_share = pair_share + (got[1] + got[2])
    bits = [1 << b for b in range(1, patches.bit_length() - 1)]

    blocks = len(cross_order(parts))
    owners = parts * span
    size = blocks * cols // owners
    factors = jax.ShapeDtypeStruct((piece, parts * cols), jnp.bfloat16)
    send, keep, high, low = pl.pallas_call(
        functools.partial(cross_kernel, parts, span),
        out_shape=[shape(owners // 2, size, cols)] * 2 + [factors] * 2,
        in_specs=[whole()] * parts,
        out_specs=[whole()] * 4,
        scratch_shapes=[pltpu.VMEM((piece, parts * cols), F32), pltpu.VMEM((blocks * cols, cols), F32)],
        compiler_params=params(),
        cost_estimate=pl.CostEstimate(flops=0, bytes_accessed=0, transcendentals=0),
        name="cross",
    )(*[far[k] for k in range(parts)])
    got = swap(send, "tm", 1)
    mine = keep[0] + got[0]
    for h in range(1, owners // 2):
        mine = mine + swap_both(keep[h] + got[h], 2 * h)
    for bit in bits[:1]:
        pair_share = pair_share + swap(pair_share, "space", bit)
    mine, pair_share = lax.optimization_barrier((mine, pair_share))
    pair_share, product_share = pair_share[:pair_size], pair_share[pair_size:]
    for bit in bits[1:]:
        pair_share = pair_share + swap(pair_share, "space", bit)
    for bit in bits[:1]:
        mine = mine + swap(mine, "space", bit)
    mine, pair_share = lax.optimization_barrier((mine, pair_share))
    mine = jnp.concatenate([mine, product_share], axis=0)
    for bit in bits[1:]:
        mine = mine + swap(mine, "space", bit)

    def spread(x, count):
        return [x] + [swap_both(x, 2 * h) for h in range(1, count // 2)]

    def gathered(shares):
        even = jnp.stack(shares)
        return even, swap(even, "tm", 1)

    mine, *pair_shares = lax.optimization_barrier([mine] + spread(pair_share, parts))

    half = parts // 2
    level = pl.pallas_call(
        functools.partial(level_kernel, parts),
        out_shape=shape(half // 2 if half % 2 == 0 else half, 3 * cols, cols),
        in_specs=[whole()] * 2,
        out_specs=whole(),
        scratch_shapes=[pltpu.VMEM((half, pair_rows(cols), cols), F32)],
        compiler_params=params(),
        cost_estimate=pl.CostEstimate(flops=parts * SIGN_STEPS * 6 * (2 * cols) ** 3, bytes_accessed=0, transcendentals=0),
        name="level",
    )(*gathered(pair_shares))
    level, *shares = lax.optimization_barrier([level] + spread(mine, owners))
    other_level = swap(level, "tm", 1)
    width = cols // parts
    *sent, weight, products = pl.pallas_call(
        functools.partial(merge_kernel, parts, span),
        out_shape=[shape(width, piece)] * parts + [shape(parts * cols, cols)] * 2,
        in_specs=[whole()] * 6,
        out_specs=[whole()] * (parts + 2),
        scratch_shapes=[
            pltpu.VMEM((half, 3 * cols, cols), F32),
            pltpu.VMEM((blocks * cols, cols), F32),
            pltpu.VMEM((cols, piece), F32),
        ],
        compiler_params=params(),
        name="merge",
    )(*gathered(shares), level, other_level, high, low)
    coefficients = pl.pallas_call(
        functools.partial(coefficient_kernel, parts),
        out_shape=shape(width, cols),
        in_specs=[whole()] * 2,
        out_specs=whole(),
        scratch_shapes=[pltpu.VMEM((cols, cols), F32)],
        compiler_params=params(),
        name="coefficients",
    )(weight, products)
    last = [sent[0]] + [swap(sent[k], "tm", k) for k in range(1, parts)]

    basis = pl.pallas_call(
        functools.partial(final_kernel, parts),
        out_shape=shape(half_rows, width, half_cols),
        in_specs=[whole()] * parts,
        out_specs=whole(),
        compiler_params=params(),
        name="final",
    )(*last)
    return basis.transpose(0, 2, 1), coefficients


def solution(mesh):
    placed = (P("space", None, "tm"), P("space", None), P(), P(), P("space", None, None))
    return jax.shard_map(
        local,
        mesh=mesh,
        in_specs=placed,
        out_specs=(P("space", None, "tm"), P("tm", None)),
        check_vma=False,
    )
```
